128 devices in a mesh: section: 2 (over y_hi), dp: 64 (over z, x, y_lo, core).
Axes of the slice: x: 4, y: 4 (y_hi: 2, y_lo: 2; y = y_hi * 2 + y_lo), z: 4, core: 2. Of those that a mesh axis runs over, the one named last changes fastest.
Arguments:
- block_input: bfloat16 [2, 64, 256, 768], P(None, 'dp'), may hold values from -6 to 6
- out_grad: bfloat16 [2, 64, 256, 768], P(None, 'dp'), may hold values from -6 to 6
- live_mask: int32 [2, 64], P(None, 'dp'), may hold values 0 or 1
- norm_gain: bfloat16 [2, 768], P('section', 'dp'), may hold values from 0.5 to 1.5
- in_weight: bfloat16 [2, 768, 3352], P('section', 'dp'), may hold values from -0.21875 to 0.21875
- conv_weight: bfloat16 [2, 4, 1792], P('section', None, 'dp'), may hold values from -3 to 3
- conv_bias: bfloat16 [2, 1792], P('section', 'dp'), may hold values from -3 to 3
- dt_bias: float32 [2, 24], P('section'), may hold values from -6 to -2
- a_log: float32 [2, 24], P('section'), may hold values from 0 to 3
- d_skip: float32 [2, 24], P('section'), may hold values from 0.5 to 1.5
- gated_gain: bfloat16 [2, 1536], P('section', 'dp'), may hold values from 0.5 to 1.5
- out_weight: bfloat16 [2, 1536, 768], P('section', 'dp'), may hold values from -0.15625 to 0.15625
Outputs:
- activations: bfloat16 [2, 2, 64, 256, 768], P('section', None, 'dp')
- input_grads: float32 [2, 2, 64, 256, 768], P('section', None, 'dp')
- norm_gain_grad: float32 [2, 768], P('section', 'dp')
- in_weight_grad: float32 [2, 768, 3352], P('section', 'dp')
- conv_weight_grad: float32 [2, 4, 1792], P('section', None, 'dp')
- conv_bias_grad: float32 [2, 1792], P('section', 'dp')
- dt_bias_grad: float32 [2, 24], P('section')
- a_log_grad: float32 [2, 24], P('section')
- d_skip_grad: float32 [2, 24], P('section')
- gated_gain_grad: float32 [2, 1536], P('section', 'dp')
- out_weight_grad: float32 [2, 1536, 768], P('section', 'dp')
The draws below stay inside these ranges and needn't reach their ends.
All inputs are finite; a program needn't handle non-finite values. No bound on the sum of `live_mask` on one device may be relied on, other than what follows from the above.
Results may differ from the reference program's by a relative error of at most 0.013.
Values may be sent and summed in bfloat16 or wider, within the bound.
A program may use at most 192 MiB of HBM per device.

```python
import jax
import jax.numpy as jnp
from jax import lax

D = 768
H = 24
P_SIZE = 64
N = 128
CONV = 4
GROUP = 128
SEQ_LEN = 256
MICRO = 2
LAYERS = 2
DI = 1536
CHANNELS = 1792
PROJ = 3352
SEQS = 64


def touch_ends(array, key, least, largest):
    spot = [jax.random.randint(jax.random.fold_in(key, axis), (), 0, length) for axis, length in enumerate(array.shape)]
    longest = array.shape.index(max(array.shape))
    neighbour = spot[:longest] + [(spot[longest] + 1) % array.shape[longest]] + spot[longest + 1:]
    return array.at[tuple(spot)].set(least).at[tuple(neighbour)].set(largest)


def levels(rng, extent, cuts, low, largest):
    def one(position, shards_of):
        heights = jax.random.uniform(jax.random.fold_in(jax.random.fold_in(rng, 6), position), (shards_of,), jnp.float32, low / len(cuts), largest / len(cuts))
        return jnp.repeat(jnp.exp(heights), extent[position] // shards_of).reshape((-1,) + (1,) * (len(extent) - position - 1))

    factor_of = one(*cuts[0])
    for cut in cuts[1:]:
        factor_of = factor_of * one(*cut)
    return factor_of


def gaussian(stream_key, dims, spread, limit, cuts=(), held_as=jnp.bfloat16):
    factor_of = levels(stream_key, dims, cuts, -0.22, 0.18) if cuts else 1.0
    array = jax.random.normal(stream_key, dims, jnp.float32) * spread * factor_of
    return jnp.minimum(jnp.maximum(array, -limit), limit).astype(held_as)


def setup_inputs(seed: int = 0) -> dict:
    splits = jax.random.split(jax.random.key(seed), 13)
    return {
        "block_input": gaussian(splits[0], (MICRO, SEQS, SEQ_LEN, D), 1.0, 6.0, ((1, 64),)),
        "out_grad": gaussian(splits[1], (MICRO, SEQS, SEQ_LEN, D), 1.0, 6.0, ((1, 64),)),
        "live_mask": touch_ends((jax.random.randint(splits[2], (MICRO, SEQS), 0, 4) < 3).astype(jnp.int32), jax.random.fold_in(splits[2], 1), 0, 1),
        "norm_gain": jnp.clip(1.0 + 0.1 * jax.random.normal(splits[3], (LAYERS, D), jnp.float32), 0.5, 1.5).astype(jnp.bfloat16),
        "in_weight": gaussian(splits[4], (LAYERS, D, PROJ), D ** -0.5, 0.21875, ((0, 2), (1, 64))),
        "conv_weight": gaussian(splits[5], (LAYERS, CONV, CHANNELS), CONV ** -0.5, 3.0, ((0, 2), (2, 64))),
        "conv_bias": gaussian(splits[6], (LAYERS, CHANNELS), 0.5, 3.0, ((0, 2), (1, 64))),
        "dt_bias": jnp.clip(-6.0 + 4.0 * jax.random.uniform(splits[7], (LAYERS, H), jnp.float32) ** levels(splits[7], (LAYERS, H), ((0, 2),), -0.2, 0.2), -6.0, -2.0),
        "a_log": jnp.clip(3.0 * jax.random.uniform(splits[8], (LAYERS, H), jnp.float32) ** levels(splits[8], (LAYERS, H), ((0, 2),), -0.2, 0.2), 0.0, 3.0),
        "d_skip": jnp.clip(0.5 + 1.0 * jax.random.uniform(splits[9], (LAYERS, H), jnp.float32) ** levels(splits[9], (LAYERS, H), ((0, 2),), -0.2, 0.2), 0.5, 1.5),
        "gated_gain": jnp.clip(1.0 + 0.1 * jax.random.normal(splits[10], (LAYERS, DI), jnp.float32), 0.5, 1.5).astype(jnp.bfloat16),
        "out_weight": gaussian(splits[11], (LAYERS, DI, D), DI ** -0.5, 0.15625, ((0, 2), (1, 64))),
    }


EPS = 1e-05

@jax.custom_vjp
def low(v):
    return lax.optimization_barrier(v.astype(jnp.bfloat16)).astype(jnp.float32)

@jax.custom_vjp
def low_back(v):
    return v

def low_keep(v):
    return (low(v), None)

def low_pass(kept, grad):
    return (grad,)

def back_keep(v):
    return (v, None)

def back_low(kept, grad):
    return (low(grad),)
low.defvjp(low_keep, low_pass)
low_back.defvjp(back_keep, back_low)

def exact_dot(left, right):
    return jnp.dot(left, right, precision=lax.Precision.HIGHEST, preferred_element_type=jnp.float32)

def silu_of(value):
    return value * jax.nn.sigmoid(value)

def block_step(state, pieces):
    values, keys_in, queries, steps, rates = pieces
    span = rates.shape[0]
    cumul = jnp.cumsum(rates, axis=0)
    scores = exact_dot(queries, keys_in.T)
    rows = lax.broadcasted_iota(jnp.int32, (span, span), 0)
    cols = lax.broadcasted_iota(jnp.int32, (span, span), 1)
    lower = rows >= cols
    gap = cumul[:, None, :] - cumul[None, :, :]
    decayed = jnp.exp(jnp.where(lower[:, :, None], gap, 0.0)) * lower[:, :, None].astype(jnp.float32)
    weights = scores[:, :, None] * decayed * steps[None, :, :]
    inner = jnp.einsum('tsh,shp->thp', weights, values, precision=lax.Precision.HIGHEST)
    outer = jnp.exp(cumul)[:, :, None] * jnp.einsum('tn,hpn->thp', queries, state, precision=lax.Precision.HIGHEST)
    tail = jnp.exp(cumul[-1][None, :] - cumul) * steps
    carried = jnp.exp(cumul[-1])[:, None, None] * state
    fresh = jnp.einsum('sh,shp,sn->hpn', tail, values, keys_in, precision=lax.Precision.HIGHEST)
    return (carried + fresh, inner + outer)

def group_scan(values, keys_in, queries, steps, rates):
    length = values.shape[0]
    blocks = length // GROUP
    pieces = (values.reshape(blocks, GROUP, H, P_SIZE), keys_in.reshape(blocks, GROUP, N), queries.reshape(blocks, GROUP, N), steps.reshape(blocks, GROUP, H), rates.reshape(blocks, GROUP, H))
    start = jnp.zeros((H, P_SIZE, N), jnp.float32)
    _, outputs = lax.scan(jax.checkpoint(block_step), start, pieces)
    return outputs.reshape(length, H, P_SIZE)

def layer(stream, params):
    gain_in, weight_in, taps, tap_bias, step_bias, decay_log, skip_factor, gain_out, weight_out = params
    length = stream.shape[0]
    normed_in = low(stream * lax.rsqrt(lax.optimization_barrier(jnp.mean(stream * stream, axis=-1, keepdims=True)) + EPS) * gain_in)
    projected = low_back(exact_dot(normed_in, weight_in))
    gate_part = projected[:, :DI]
    conv_in = projected[:, DI:DI + CHANNELS]
    raw_step = projected[:, DI + CHANNELS:]
    padded = jnp.pad(conv_in, ((CONV - 1, 0), (0, 0)))
    conv_out = tap_bias[None, :] + jnp.zeros_like(conv_in)
    for offset in range(CONV):
        conv_out = conv_out + taps[offset][None, :] * padded[offset:offset + length]
    mixed_in = low(silu_of(conv_out))
    values = mixed_in[:, :DI].reshape(length, H, P_SIZE)
    keys_in = mixed_in[:, DI:DI + N]
    queries = mixed_in[:, DI + N:]
    steps = jax.nn.softplus(raw_step + step_bias[None, :])
    rates = -steps * jnp.exp(decay_log)[None, :]
    scanned = group_scan(values, keys_in, queries, steps, rates) + values * skip_factor[None, :, None]
    gated = scanned.reshape(length, DI) * silu_of(gate_part)
    normed_out = low(gated * lax.rsqrt(lax.optimization_barrier(jnp.mean(gated * gated, axis=-1, keepdims=True)) + EPS) * gain_out)
    branch = low_back(exact_dot(normed_out, weight_out))
    return stream + branch

def reference(block_input, out_grad, live_mask, norm_gain, in_weight, conv_weight, conv_bias, dt_bias, a_log, d_skip, gated_gain, out_weight):
    params = (norm_gain.astype(jnp.float32), in_weight.astype(jnp.float32), conv_weight.astype(jnp.float32), conv_bias.astype(jnp.float32), dt_bias.astype(jnp.float32), a_log.astype(jnp.float32), d_skip.astype(jnp.float32), gated_gain.astype(jnp.float32), out_weight.astype(jnp.float32))
    inputs = block_input.astype(jnp.float32).reshape(MICRO * SEQS, SEQ_LEN, D)
    bumps = jnp.zeros_like(inputs)

    def forward(inputs, params, bumps):
        first_params = tuple((item[0] for item in params))
        second_params = tuple((item[1] for item in params))

        def one_seq(carry, item):
            sequence, bumped = item
            first = layer(sequence, first_params)
            handed = low_back(low(first))
            second = layer(handed + bumped, second_params)
            return (carry, (handed, second))
        _, (handed_all, second_all) = lax.scan(jax.checkpoint(one_seq), jnp.zeros((), jnp.float32), (inputs, bumps))
        return (handed_all, second_all)
    (handed_all, second_all), pull = jax.vjp(forward, inputs, params, bumps)
    live = live_mask.astype(jnp.float32)
    cotangent = (out_grad.astype(jnp.float32) * live[:, :, None, None]).reshape(MICRO * SEQS, SEQ_LEN, D)
    input_grad, param_grads, bump_grad = pull((jnp.zeros_like(handed_all), cotangent))
    activations = jnp.stack([handed_all, second_all]).reshape(LAYERS, MICRO, SEQS, SEQ_LEN, D).astype(jnp.bfloat16)
    input_grads = jnp.stack([input_grad, bump_grad]).reshape(LAYERS, MICRO, SEQS, SEQ_LEN, D)
    return (activations, input_grads, param_grads[0], param_grads[1], param_grads[2], param_grads[3], param_grads[4], param_grads[5], param_grads[6], param_grads[7], param_grads[8])
```

```python
import functools

import jax
import jax.numpy as jnp
import numpy as np
from jax import lax
from jax.experimental import pallas as pl
from jax.experimental.pallas import tpu as pltpu
from jax.sharding import PartitionSpec as P

F32 = jnp.float32
BF16 = jnp.bfloat16
MESH = pl.DeviceIdType.MESH
EPS = 1e-05
T = 256
GROUP = 128
LANE = 128
D = 768
DI = 1536
HEADS = 24
CHANNELS = 1792
WIDE = 3584
ROW_GAIN = 0
ROW_TAPS = 6
ROW_BIAS = 62
ROW_GATED = 76
SMALL = 88


def mm(a, b, dims, precision=None):
    return lax.dot_general(a, b, (dims, ((), ())), precision=precision, preferred_element_type=F32)


NN = ((1,), (0,))
NT = ((1,), (1,))
TN = ((0,), (0,))
EXACT = lax.Precision.HIGHEST


def chunk(j):
    return slice(LANE * j, LANE * (j + 1))


def in_pair(w_ref, j):
    left = w_ref[j, :, 0:48, :].reshape(D, LANE)
    right = w_ref[j, :, 48:96, :].reshape(D, LANE)
    return jnp.concatenate([left, right], axis=1)


def out_pair(w_ref, c):
    left = w_ref[14 + c].reshape(DI, LANE)
    right = w_ref[15 + c].reshape(DI, LANE)
    return jnp.concatenate([left, right], axis=1)


def lane_half():
    return lax.broadcasted_iota(jnp.int32, (1, LANE), 1) < 64


def lower_mask():
    rows = lax.broadcasted_iota(jnp.int32, (GROUP, GROUP), 0)
    cols = lax.broadcasted_iota(jnp.int32, (GROUP, GROUP), 1)
    return rows >= cols


def down(x, k):
    if k == 0:
        return x
    rows = lax.broadcasted_iota(jnp.int32, x.shape, 0)
    return jnp.where(rows >= k, pltpu.roll(x, k, 0), 0.0)


def up(x, k):
    if k == 0:
        return x
    rows = lax.broadcasted_iota(jnp.int32, x.shape, 0)
    return jnp.where(rows < T - k, pltpu.roll(x, T - k, 0), 0.0)


def sigmoid(x):
    return 1.0 / (1.0 + jnp.exp(-x))


def conv_of(proj_ref, conv_ref, j):
    x = proj_ref[:, DI + LANE * j : DI + LANE * (j + 1)]
    out = conv_ref[4:5, chunk(j)] + conv_ref[3:4, chunk(j)] * x
    for k in range(1, 4):
        out = out + conv_ref[3 - k : 4 - k, chunk(j)] * down(x, k)
    return x, out


def spread(cols, p):
    return jnp.where(lane_half(), cols[:, 2 * p : 2 * p + 1], cols[:, 2 * p + 1 : 2 * p + 2])


def steps_of(proj_ref, head_ref):
    raw = proj_ref[:, DI + CHANNELS : DI + CHANNELS + LANE] + head_ref[0:1, :]
    steps = jnp.maximum(raw, 0.0) + jnp.log1p(jnp.exp(-jnp.abs(raw)))
    rates = -steps * jnp.exp(head_ref[1:2, :])
    tri = lower_mask().astype(F32)
    cumul = [mm(tri, rates[GROUP * b : GROUP * (b + 1)], NN, EXACT) for b in range(2)]
    return raw, steps, rates, cumul


def forward(s_ref, w_ref, head_ref, idx_ref, act_ref, proj_ref, scan_ref, gain_ref, conv_ref, wide_ref,
            mixed_ref, nout_ref):
    unpack_all(w_ref, idx_ref, head_ref, gain_ref, conv_ref, wide_ref)
    stream = s_ref[...].astype(F32)
    scale = lax.rsqrt(jnp.mean(stream * stream, axis=-1, keepdims=True) + EPS)
    normed = (stream * scale * gain_ref[0:1, :]).astype(BF16)
    for j in range(14):
        got = mm(normed, in_pair(w_ref, j), NN)
        proj_ref[:, 2 * LANE * j : 2 * LANE * (j + 1)] = got
    for j in range(14):
        _, out = conv_of(proj_ref, conv_ref, j)
        mixed_ref[:, chunk(j)] = (out * sigmoid(out)).astype(BF16)
    _, steps, _, cumul = steps_of(proj_ref, head_ref)
    lower = lower_mask()
    half = lane_half()
    key = [mixed_ref[GROUP * b : GROUP * (b + 1), chunk(12)] for b in range(2)]
    query = [mixed_ref[GROUP * b : GROUP * (b + 1), chunk(13)] for b in range(2)]
    scores = [mm(query[b], key[b], NT) for b in range(2)]
    cross = mm(query[1], key[0], NT).astype(BF16)
    cumul_t = [c.T for c in cumul]
    total = jnp.zeros((T, 1), F32)
    for p in range(12):
        tail_u = None
        squares = []
        for b in range(2):
            rows = slice(GROUP * b, GROUP * (b + 1))
            x = mixed_ref[rows, chunk(p)].astype(F32)
            u = x * spread(steps[rows], p)
            weights = []
            for h in (2 * p, 2 * p + 1):
                gap = cumul[b][:, h : h + 1] - cumul_t[b][h : h + 1, :]
                weights.append((scores[b] * jnp.exp(jnp.where(lower, gap, -1e30))).astype(BF16))
            u_two = jnp.concatenate([jnp.where(half, u, 0.0), jnp.where(half, 0.0, u)], axis=0)
            y = mm(jnp.concatenate(weights, axis=1), u_two.astype(BF16), NN)
            cum = spread(cumul[b], p)
            if b == 0:
                tail_u = (jnp.exp(cum[GROUP - 1 : GROUP, :] - cum) * u).astype(BF16)
            else:
                y = y + jnp.exp(cum) * mm(cross, tail_u, NN)
            y = y + x * wide_ref[1:2, chunk(p)]
            scan_ref[rows, chunk(p)] = y
            z = proj_ref[rows, chunk(p)]
            gated = y * (z * sigmoid(z))
            squares.append(jnp.sum(gated * gated, axis=-1, keepdims=True))
        total = total + jnp.concatenate(squares, axis=0)
    scale_out = lax.rsqrt(total * (1.0 / DI) + EPS)
    for p in range(12):
        z = proj_ref[:, chunk(p)]
        gated = scan_ref[:, chunk(p)] * (z * sigmoid(z))
        nout_ref[:, chunk(p)] = (gated * scale_out * wide_ref[0:1, chunk(p)]).astype(BF16)
    for c in range(0, 6, 2):
        cols = slice(LANE * c, LANE * (c + 2))
        branch = mm(nout_ref[...], out_pair(w_ref, c), NN)
        act_ref[:, cols] = (s_ref[:, cols].astype(F32) + branch).astype(BF16)


def fold(value, expand):
    high = value.astype(BF16)
    low = (value - high.astype(F32)).astype(BF16)
    return mm(high, expand, NN) + mm(low, expand, NN)


def backward(s_ref, gout_ref, w_ref, head_ref, idx_ref, proj_ref, scan_ref, gain_ref, conv_ref, wide_ref,
             gin_ref, low_ref, d_ref, hgrad_ref,
             mixed_ref, nout_ref, gno_ref, gproj_ref, dmix_ref, dcum_ref, dstep_ref, small_ref, pack_ref):
    hgrad_ref[...] = jnp.zeros_like(hgrad_ref)
    skip_sum = jnp.zeros((1, LANE), F32)
    lower = lower_mask()
    half = lane_half()
    grad_branch = gout_ref[...]
    total = jnp.zeros((T, 1), F32)
    for p in range(12):
        z = proj_ref[:, chunk(p)]
        gated = scan_ref[:, chunk(p)] * (z * sigmoid(z))
        total = total + jnp.sum(gated * gated, axis=-1, keepdims=True)
    scale_out = lax.rsqrt(total * (1.0 / DI) + EPS)
    for c in range(0, 6, 2):
        part = mm(grad_branch[:, LANE * c : LANE * (c + 2)], out_pair(w_ref, c), NT)
        if c == 0:
            gno_ref[...] = part
        else:
            gno_ref[...] += part
    inner = jnp.zeros((T, 1), F32)
    for p in range(12):
        z = proj_ref[:, chunk(p)]
        gated = scan_ref[:, chunk(p)] * (z * sigmoid(z))
        unit = gated * scale_out
        gain = wide_ref[0:1, chunk(p)]
        nout_ref[:, chunk(p)] = (unit * gain).astype(BF16)
        gno = gno_ref[:, chunk(p)]
        small_ref[ROW_GATED + p : ROW_GATED + p + 1, :] = jnp.sum(gno * unit, axis=0, keepdims=True)
        inner = inner + jnp.sum(gno * gain * unit, axis=-1, keepdims=True)
    inner = inner * (1.0 / DI)
    for c in range(0, 6, 2):
        grad = mm(nout_ref[...], grad_branch[:, LANE * c : LANE * (c + 2)], TN).astype(BF16)
        for e in range(2):
            d_ref[14 + c + e] = grad[:, LANE * e : LANE * (e + 1)].reshape(16, 96, LANE)
    for p in range(12):
        z = proj_ref[:, chunk(p)]
        scan = scan_ref[:, chunk(p)]
        sig = sigmoid(z)
        silu = z * sig
        unit = scan * silu * scale_out
        ggated = scale_out * (gno_ref[:, chunk(p)] * wide_ref[0:1, chunk(p)] - unit * inner)
        gproj_ref[:, chunk(p)] = (ggated * scan * (sig + silu * (1.0 - sig))).astype(BF16)
        gno_ref[:, chunk(p)] = ggated * silu
    for j in range(14):
        _, out = conv_of(proj_ref, conv_ref, j)
        mixed_ref[:, chunk(j)] = (out * sigmoid(out)).astype(BF16)
    raw, steps, rates, cumul = steps_of(proj_ref, head_ref)
    key = [mixed_ref[GROUP * b : GROUP * (b + 1), chunk(12)] for b in range(2)]
    query = [mixed_ref[GROUP * b : GROUP * (b + 1), chunk(13)] for b in range(2)]
    scores = [mm(query[b], key[b], NT) for b in range(2)]
    cross = mm(query[1], key[0], NT).astype(BF16)
    cumul_t = [c.T for c in cumul]
    dscores = [jnp.zeros((GROUP, GROUP), F32) for _ in range(2)]
    dcross = jnp.zeros((GROUP, GROUP), F32)
    dcum_ref[...] = jnp.zeros_like(dcum_ref)
    dstep_ref[...] = jnp.zeros_like(dstep_ref)
    lanes = lax.broadcasted_iota(jnp.int32, (1, LANE), 1)
    head_row = lax.broadcasted_iota(jnp.int32, (LANE, LANE), 0)
    head_col = lax.broadcasted_iota(jnp.int32, (LANE, LANE), 1)
    row_sum = [jnp.zeros((GROUP, LANE), F32) for _ in range(2)]
    for p in range(12):
        expand = (head_col == 2 * p + jnp.where(head_row < 64, 0, 1)).astype(BF16)
        tail_u = eg = None
        us, xs, dus, step_es, grads = [], [], [], [], []
        tail = None
        for b in range(2):
            rows = slice(GROUP * b, GROUP * (b + 1))
            x = mixed_ref[rows, chunk(p)].astype(F32)
            step_e = spread(steps[rows], p)
            u = x * step_e
            g = gno_ref[rows, chunk(p)]
            g_two = jnp.concatenate([jnp.where(half, g, 0.0), jnp.where(half, 0.0, g)], axis=0)
            g_two = g_two.astype(BF16)
            value = mm(g_two, u.astype(BF16), NT)
            weights = []
            for e in range(2):
                h = 2 * p + e
                gap = cumul[b][:, h : h + 1] - cumul_t[b][h : h + 1, :]
                decay = jnp.exp(jnp.where(lower, gap, -1e30))
                weight = scores[b] * decay
                weights.append(weight.astype(BF16))
                v = value[GROUP * e : GROUP * (e + 1)]
                dscores[b] = dscores[b] + v * decay
                both = v * weight
                row_sum[b] = jnp.where(lanes == h, jnp.sum(both, axis=-1, keepdims=True), row_sum[b])
                dcum_ref[b, h : h + 1, :] = -jnp.sum(both, axis=0, keepdims=True)
            du = mm(jnp.concatenate(weights, axis=0), g_two, TN)
            us.append(u)
            xs.append(x)
            dus.append(du)
            step_es.append(step_e)
            grads.append(g)
            cum = spread(cumul[b], p)
            if b == 0:
                tail = jnp.exp(cum[GROUP - 1 : GROUP, :] - cum)
                tail_u = tail * u
            else:
                eg = jnp.exp(cum) * g
        tail_low = tail_u.astype(BF16)
        eg_low = eg.astype(BF16)
        dtail = mm(cross, eg_low, TN)
        dcross = dcross + mm(eg_low, tail_low, NT)
        dus[0] = dus[0] + tail * dtail
        column = fold(tail_u * dtail, expand)
        row_sum[0] = row_sum[0] - column
        row_sum[0] = row_sum[0] + jnp.where(
            lax.broadcasted_iota(jnp.int32, (GROUP, 1), 0) == GROUP - 1,
            jnp.sum(column, axis=0, keepdims=True), 0.0)
        row_sum[1] = row_sum[1] + fold(eg * mm(cross, tail_low, NN), expand)
        skip = jnp.zeros((1, LANE), F32)
        for b in range(2):
            rows = slice(GROUP * b, GROUP * (b + 1))
            dstep_ref[rows, :] += fold(dus[b] * xs[b], expand)
            dmix_ref[rows, chunk(p)] = step_es[b] * dus[b] + grads[b] * wide_ref[1:2, chunk(p)]
            skip = skip + jnp.sum(grads[b] * xs[b], axis=0, keepdims=True)
        skip_sum = skip_sum + fold(jnp.broadcast_to(skip, (8, LANE)), expand)[0:1]
    dcross_low = dcross.astype(BF16)
    ds_low = [d.astype(BF16) for d in dscores]
    dmix_ref[0:GROUP, chunk(12)] = mm(ds_low[0], query[0], TN) + mm(dcross_low, query[1], TN)
    dmix_ref[GROUP:T, chunk(12)] = mm(ds_low[1], query[1], TN)
    dmix_ref[0:GROUP, chunk(13)] = mm(ds_low[0], key[0], NN)
    dmix_ref[GROUP:T, chunk(13)] = mm(ds_low[1], key[1], NN) + mm(dcross_low, key[0], NN)
    tri = lower.astype(F32)
    decay_rate = jnp.exp(head_ref[1:2, :])
    step_sum = jnp.zeros((1, LANE), F32)
    decay_sum = jnp.zeros((1, LANE), F32)
    for b in range(2):
        rows = slice(GROUP * b, GROUP * (b + 1))
        drate = mm(tri, row_sum[b] + dcum_ref[b].T, TN, EXACT)
        draw = (dstep_ref[rows, :] - decay_rate * drate) * sigmoid(raw[rows])
        draw = jnp.where(lanes < HEADS, draw, 0.0)
        decay_sum = decay_sum + jnp.sum(drate * rates[rows], axis=0, keepdims=True)
        step_sum = step_sum + jnp.sum(draw, axis=0, keepdims=True)
        gproj_ref[rows, DI + CHANNELS : DI + CHANNELS + LANE] = draw.astype(BF16)
    hgrad_ref[0:1, :] = step_sum
    hgrad_ref[1:2, :] = decay_sum
    hgrad_ref[2:3, :] = skip_sum
    gproj_ref[:, WIDE - LANE :] = jnp.zeros((T, LANE), BF16)
    for j in range(14):
        x, out = conv_of(proj_ref, conv_ref, j)
        sig = sigmoid(out)
        dconv = dmix_ref[:, chunk(j)] * (sig + out * sig * (1.0 - sig))
        small_ref[ROW_BIAS + j : ROW_BIAS + j + 1, :] = jnp.sum(dconv, axis=0, keepdims=True)
        dx = conv_ref[3:4, chunk(j)] * dconv
        for k in range(4):
            row = ROW_TAPS + 14 * (3 - k) + j
            small_ref[row : row + 1, :] = jnp.sum(dconv * down(x, k), axis=0, keepdims=True)
            if k:
                dx = dx + conv_ref[3 - k : 4 - k, chunk(j)] * up(dconv, k)
        gproj_ref[:, DI + LANE * j : DI + LANE * (j + 1)] = dx.astype(BF16)
    stream = s_ref[...].astype(F32)
    scale = lax.rsqrt(jnp.mean(stream * stream, axis=-1, keepdims=True) + EPS)
    unit = stream * scale
    normed = (unit * gain_ref[0:1, :]).astype(BF16)
    gnormed = jnp.zeros((T, D), F32)
    for j in range(14):
        gp = gproj_ref[:, 2 * LANE * j : 2 * LANE * (j + 1)]
        grad = mm(normed, gp, TN).astype(BF16)
        for e in range(1 if j == 13 else 2):
            part = grad[:, LANE * e : LANE * (e + 1)].reshape(16, 48, LANE)
            d_ref[j, :, 48 * e : 48 * (e + 1), :] = part
        gnormed = gnormed + mm(gp, in_pair(w_ref, j), NT)
    gain_grad = jnp.sum(gnormed * unit, axis=0, keepdims=True)
    for c in range(6):
        small_ref[ROW_GAIN + c : ROW_GAIN + c + 1, :] = gain_grad[:, chunk(c)]
    gunit = gnormed * gain_ref[0:1, :]
    center = jnp.mean(gunit * unit, axis=-1, keepdims=True)
    gin = gout_ref[...].astype(F32) + scale * (gunit - unit * center)
    gin_ref[...] = gin
    low_ref[...] = gin.astype(BF16)
    pack_all(small_ref, idx_ref, pack_ref)
    d_ref[13, :, 48:64, :] = pack_ref[...].astype(BF16).reshape(16, 16, LANE)
    d_ref[13, :, 64:96, :] = jnp.zeros((16, 32, LANE), BF16)


KINDS = (
    (2, 12, ROW_GAIN, 6, 32, 1),
    (0, 28, ROW_TAPS, 14, 0, 0),
    (0, 28, ROW_TAPS + 14, 14, 32, 0),
    (0, 28, ROW_TAPS + 28, 14, 64, 0),
    (0, 28, ROW_TAPS + 42, 14, 96, 0),
    (0, 28, ROW_BIAS, 14, 0, 1),
    (4, 24, ROW_GATED, 12, 64, 1),
)


def owner_index():
    table = np.zeros((8, CHANNELS), np.int32)
    for row, width, length in ((0, 28, CHANNELS), (2, 12, D), (4, 24, DI)):
        position = np.arange(length)
        owner = position // width
        table[row, :length] = 16 * (owner // 4) + 2 * (owner % 4)
        table[row + 1, :length] = position % width
    return jnp.asarray(table)


def window(width, c):
    first, last = LANE * c // width, (LANE * c + LANE - 1) // width
    return 16 * (first // 4), 16 * (last // 4) + 16


def unpack(pack, idx_ref, kind, c):
    row, width, _, _, lane, line = kind
    low, high = window(width, c)
    lanes = lax.broadcasted_iota(jnp.int32, (LANE, LANE), 0)
    pick = (lanes == idx_ref[row + 1 : row + 2, chunk(c)] + lane).astype(BF16)
    rows = lax.broadcasted_iota(jnp.int32, (high - low, LANE), 0) + low
    got = mm(pack[low:high], pick, NN)
    return jnp.sum(jnp.where(rows == idx_ref[row : row + 1, chunk(c)] + line, got, 0.0), axis=0, keepdims=True)


def unpack_all(w_ref, idx_ref, head_ref, gain_ref, conv_ref, wide_ref):
    pack = w_ref[13, :, 48:64, :].reshape(256, LANE)
    for c in range(6):
        gain_ref[0:1, chunk(c)] = unpack(pack, idx_ref, KINDS[0], c)
    for k in range(5):
        for c in range(14):
            conv_ref[k : k + 1, chunk(c)] = unpack(pack, idx_ref, KINDS[1 + k], c)
    for c in range(12):
        wide_ref[0:1, chunk(c)] = unpack(pack, idx_ref, KINDS[6], c)
        wide_ref[1:2, chunk(c)] = spread(head_ref[2:3, :], c)


def pack_all(small_ref, idx_ref, pack_ref):
    pack_ref[...] = jnp.zeros_like(pack_ref)
    for kind in KINDS:
        row, width, start, count, lane, line = kind
        for c in range(count):
            low, high = window(width, c)
            lanes = lax.broadcasted_iota(jnp.int32, (LANE, LANE), 0)
            pick = (lanes == idx_ref[row + 1 : row + 2, chunk(c)] + lane).astype(BF16)
            rows = lax.broadcasted_iota(jnp.int32, (high - low, LANE), 0) + low
            value = small_ref[start + c : start + c + 1, :]
            held = jnp.where(rows == idx_ref[row : row + 1, chunk(c)] + line, value, 0.0).astype(BF16)
            pack_ref[low:high, :] += mm(held, pick, NT)


def vm(count):
    return [pl.BlockSpec(memory_space=pltpu.VMEM)] * count


def run_forward(s, w, heads, idx):
    return pl.pallas_call(
        forward,
        out_shape=(
            jax.ShapeDtypeStruct((T, D), BF16),
            jax.ShapeDtypeStruct((T, WIDE), F32),
            jax.ShapeDtypeStruct((T, DI), F32),
            jax.ShapeDtypeStruct((8, D), F32),
            jax.ShapeDtypeStruct((8, CHANNELS), F32),
            jax.ShapeDtypeStruct((8, DI), F32),
        ),
        in_specs=vm(4),
        out_specs=tuple(vm(6)),
        scratch_shapes=[pltpu.VMEM((T, CHANNELS), BF16), pltpu.VMEM((T, DI), BF16)],
        compiler_params=pltpu.CompilerParams(vmem_limit_bytes=56 * 1024 * 1024),
        name="layer_forward",
    )(s, w, heads, idx)


def run_backward(s, gout, w, heads, idx, proj, scan, gain, conv, wide):
    return pl.pallas_call(
        backward,
        out_shape=(
            jax.ShapeDtypeStruct((T, D), F32),
            jax.ShapeDtypeStruct((T, D), BF16),
            jax.ShapeDtypeStruct((20, 16, 96, LANE), BF16),
            jax.ShapeDtypeStruct((8, LANE), F32),
        ),
        in_specs=vm(10),
        out_specs=tuple(vm(4)),
        scratch_shapes=[
            pltpu.VMEM((T, CHANNELS), BF16),
            pltpu.VMEM((T, DI), BF16),
            pltpu.VMEM((T, DI), F32),
            pltpu.VMEM((T, WIDE), BF16),
            pltpu.VMEM((T, CHANNELS), F32),
            pltpu.VMEM((2, LANE, GROUP), F32),
            pltpu.VMEM((T, LANE), F32),
            pltpu.VMEM((SMALL, LANE), F32),
            pltpu.VMEM((256, LANE), F32),
        ],
        compiler_params=pltpu.CompilerParams(vmem_limit_bytes=56 * 1024 * 1024),
        name="layer_backward",
    )(s, gout, w, heads, idx, proj, scan, gain, conv, wide)


class Sems:
    def __init__(self, send, recv):
        self.send, self.recv, self.used = send, recv, 0

    def take(self):
        index = self.used
        self.used += 1
        return self.send.at[index], self.recv.at[index]


class Place:
    def __init__(self):
        self.section = lax.axis_index("section")
        self.dp = lax.axis_index("dp")
        self.z = lax.div(self.dp, 16)
        self.x = lax.rem(lax.div(self.dp, 4), 4)
        self.q = lax.rem(self.dp, 4)
        self.core = lax.rem(self.dp, 2)
        self.column = self.dp - self.q

    def at(self, z, x):
        return (self.section, 16 * z + 4 * x + self.q)

    def along(self, axis, distance):
        if axis == "z":
            return self.at(lax.rem(self.z + distance, 4), self.x)
        return self.at(self.z, lax.rem(self.x + distance, 4))

    def sibling(self):
        return (self.section, self.dp + 1 - 2 * self.core)

    def in_column(self, section, q):
        return (section, self.column + q)


def greet(place):
    barrier = pltpu.get_barrier_semaphore()
    peers = [place.in_column(place.section, lax.rem(place.q + r, 4)) for r in range(1, 4)]
    peers += [place.in_column(1 - place.section, lax.rem(place.q + r, 4)) for r in range(4)]
    peers += [place.along(axis, r) for axis in "zx" for r in range(1, 4)]
    for peer in peers:
        pl.semaphore_signal(barrier, inc=1, device_id=peer, device_id_type=MESH)
    pl.semaphore_wait(barrier, len(peers))


def push(src, dst, sems, device):
    send, recv = sems
    return pltpu.make_async_remote_copy(
        src_ref=src, dst_ref=dst, send_sem=send, recv_sem=recv, device_id=device, device_id_type=MESH
    )


def gather_steps(layer, place, sems, local, shard_ref, w_ref, slabs, whole, own):
    sent = []

    def start(src, dst, device):
        copy = push(src, dst, sems.take(), device)
        copy.start()
        sent.append(copy)
        return copy

    copies = {}
    for other in (0, 1):
        for r in range(4):
            if other == 0 and r == 0:
                continue
            target = lax.rem(place.q + r, 4)
            section = layer if other == 0 else 1 - layer
            half = pl.ds(10 * lax.rem(target, 2), 10)
            copies[other, r] = push(
                shard_ref.at[half], slabs.at[place.q], sems.take(), place.in_column(section, target)
            )
    mine = pltpu.make_async_copy(shard_ref.at[pl.ds(10 * place.core, 10)], slabs.at[place.q], local.at[0])

    @pl.when(place.section == layer)
    def _():
        for copy in copies.values():
            copy.start()
        mine.start()

    yield

    @pl.when(place.section == layer)
    def _():
        mine.wait()
        for r in range(1, 4):
            copies[0, r].wait_recv()

    @pl.when(place.section != layer)
    def _():
        for r in range(4):
            copies[1, r].wait_recv()

    whole[...] = jnp.zeros_like(whole)
    for q in range(4):
        part = slabs[q].astype(F32)

        @pl.when(place.core == 0)
        def _():
            whole[:, 12 * q : 12 * q + 12, :] = part[:, 0:12]
            whole[:, 48 + 12 * q : 60 + 12 * q, :] = part[:, 16:28]

        @pl.when(place.core == 1)
        def _():
            whole[0:4, 12 * q : 12 * q + 12, :] = part[0:4, 0:12]
            whole[0:3, 48 + 12 * q : 60 + 12 * q, :] = part[0:3, 16:28]
            whole[3, 48 + 2 * q : 50 + 2 * q, :] = part[3, 16:18]
            whole[4:10, 24 * q : 24 * q + 24, :] = part[4:10, 0:24]

    own[...] = whole[...].astype(BF16)
    base = 10 * place.core
    here = w_ref.at[pl.ds(base, 10), place.z, place.x]
    keep = pltpu.make_async_copy(own, here, local.at[1])
    keep.start()

    def part(group, z, x, rows=None):
        pairs = pl.ds(base + 5 * group, 5)
        if rows is None:
            return w_ref.at[pairs, z, x]
        return w_ref.at[pairs, z, x, pl.ds(rows, 48)]

    every = pl.ds(0, 4)

    def slot(group, stage, axis, distance, rows=None):
        coord = lax.rem((place.z if axis == "z" else place.x) + distance, 4)
        if stage == 0:
            z, x = (coord, place.x) if axis == "z" else (place.z, coord)
        else:
            z, x = (coord, every) if axis == "z" else (every, coord)
        return part(group, z, x, rows)

    order = {0: "xz", 1: "zx"}
    forwards = [start(own, here, place.sibling())]
    first = {}
    for group in range(2):
        axis = order[group][0]
        src = own.at[pl.ds(5 * group, 5)]
        there = slot(group, 0, axis, 0)
        first[group] = (
            start(src, there, place.along(axis, 1)),
            start(src, there, place.along(axis, 3)),
        )
    keep.wait()
    for stage in range(2):
        second = {}
        for group in range(2):
            axis = order[group][stage]
            yield
            from_left, from_right = first[group]
            from_left.wait_recv()
            got = slot(group, stage, axis, 3, 0)
            one = start(got, got, place.along(axis, 1))
            whole_left = slot(group, stage, axis, 3)
            from_right.wait_recv()
            got = slot(group, stage, axis, 1, 48)
            two = start(got, got, place.along(axis, 3))
            whole_right = slot(group, stage, axis, 1)
            second[group] = (one, two)
            forwards.append(start(whole_left, whole_left, place.sibling()))
            forwards.append(start(whole_right, whole_right, place.sibling()))
        for group in range(2):
            axis = order[group][stage]
            yield
            for copy in second[group]:
                copy.wait_recv()
            far = slot(group, stage, axis, 2)
            forwards.append(start(far, far, place.sibling()))
            if stage == 0:
                axis = order[group][1]
                src = slot(group, 1, axis, 0)
                first[group] = (
                    start(src, src, place.along(axis, 1)),
                    start(src, src, place.along(axis, 3)),
                )
    yield
    for copy in forwards:
        copy.wait_recv()
    for copy in sent:
        copy.wait_send()

    @pl.when(place.section == layer)
    def _():
        for copy in copies.values():
            copy.wait_send()


GATHER_COPIES = 1 + 7 + 1 + 4 + 2 * 10 + 4


def gather_scratch():
    return [
        pltpu.VMEM((4, 10, 32, LANE), BF16),
        pltpu.VMEM((10, 96, LANE), F32),
        pltpu.VMEM((10, 96, LANE), BF16),
        pltpu.SemaphoreType.DMA((GATHER_COPIES,)),
        pltpu.SemaphoreType.DMA((GATHER_COPIES,)),
        pltpu.SemaphoreType.DMA((2,)),
    ]


def gather_kernel(layer, shard_ref, head_ref, w_ref, heads_ref, slabs, whole, own, send, recv, local):
    place = Place()
    greet(place)
    sems = Sems(send, recv)
    if layer == 0:
        partner = place.in_column(1 - place.section, place.q)
        swap = push(head_ref, heads_ref.at[place.section], sems.take(), partner)
        swap.start()
        heads_ref[place.section] = head_ref[...]
    for _ in gather_steps(layer, place, sems, local, shard_ref, w_ref, slabs, whole, own):
        pass
    if layer == 0:
        swap.wait()
    else:
        heads_ref[...] = jnp.zeros_like(heads_ref)


def run_gather(layer, shard, head):
    return pl.pallas_call(
        functools.partial(gather_kernel, layer),
        out_shape=(
            jax.ShapeDtypeStruct((20, 4, 4, 96, LANE), BF16),
            jax.ShapeDtypeStruct((2, 8, LANE), F32),
        ),
        in_specs=vm(2),
        out_specs=(pl.BlockSpec(memory_space=pl.ANY), pl.BlockSpec(memory_space=pltpu.VMEM)),
        scratch_shapes=gather_scratch(),
        compiler_params=pltpu.CompilerParams(
            collective_id=layer, has_side_effects=True, vmem_limit_bytes=48 * 1024 * 1024
        ),
        name=f"gather_layer_{layer}",
    )(shard, head)


def reduce_steps(layer, place, sems, local, d_ref, heads_ref, g_ref, head_out_ref, bufs):
    acc, got0, got1, got2, got3, got4, whole, slabs, landed, hbuf = bufs
    sent = []

    def start(src, dst, device):
        copy = push(src, dst, sems.take(), device)
        copy.start()
        sent.append(copy)
        return copy

    base = 10 * place.core
    away = 10 - base
    crossing, kept = [], []
    for i in range(10):
        crossing.append(start(d_ref.at[away + i], got0.at[i], place.sibling()))
        keep = pltpu.make_async_copy(d_ref.at[base + i], acc.at[i], local.at[i])
        keep.start()
        kept.append(keep)
    order = {0: "zx", 1: "xz"}
    every = pl.ds(0, 4)

    def chunk_at(group, stage, distance, rows=None):
        axis = order[group][stage]
        coord = lax.rem((place.z if axis == "z" else place.x) + distance, 4)
        other = every if stage == 0 else (place.x if axis == "z" else place.z)
        z, x = (coord, other) if axis == "z" else (other, coord)
        pairs = pl.ds(5 * group, 5)
        if rows is None:
            return (pairs, z, x)
        return (pairs, z, x, pl.ds(rows, 48))

    for stage in range(2):
        early, late = (got1, got2) if stage == 0 else (got3, got4)
        first = {}
        for group in range(2):
            axis = order[group][stage]
            if stage == 0:
                for i in range(5 * group, 5 * group + 5):
                    yield
                    crossing[i].wait_recv()
                    kept[i].wait()
                    acc[i] = acc[i] + got0[i]
            far = chunk_at(group, stage, 2, 0)
            far_two = chunk_at(group, stage, 2, 48)
            first[group] = (
                start(acc.at[far], early.at[group, 0], place.along(axis, 1)),
                start(acc.at[far_two], early.at[group, 1], place.along(axis, 3)),
            )
        second = {}
        for group in range(2):
            axis = order[group][stage]
            yield
            first[group][0].wait_recv()
            near = chunk_at(group, stage, 1, 0)
            acc[near] = acc[near] + early[group, 0]
            right = chunk_at(group, stage, 1)
            one = start(acc.at[right], late.at[group, 0], place.along(axis, 1))
            first[group][1].wait_recv()
            near = chunk_at(group, stage, 3, 48)
            acc[near] = acc[near] + early[group, 1]
            left = chunk_at(group, stage, 3)
            two = start(acc.at[left], late.at[group, 1], place.along(axis, 3))
            second[group] = (one, two)
        for group in range(2):
            yield
            for copy in second[group]:
                copy.wait_recv()
            mine = chunk_at(group, stage, 0)
            total = acc[mine].astype(F32) + late[group, 0].astype(F32) + late[group, 1].astype(F32)
            if stage == 0:
                acc[mine] = total.astype(BF16)
            else:
                whole[5 * group : 5 * group + 5] = total

    slabs[...] = jnp.zeros_like(slabs)
    for q in range(4):

        @pl.when(place.core == 0)
        def _():
            slabs[q, :, 0:12, :] = whole[:, 12 * q : 12 * q + 12, :]
            slabs[q, :, 16:28, :] = whole[:, 48 + 12 * q : 60 + 12 * q, :]

        @pl.when(place.core == 1)
        def _():
            slabs[q, 0:4, 0:12, :] = whole[0:4, 12 * q : 12 * q + 12, :]
            slabs[q, 0:3, 16:28, :] = whole[0:3, 48 + 12 * q : 60 + 12 * q, :]
            slabs[q, 3, 16:18, :] = whole[3, 48 + 2 * q : 50 + 2 * q, :]
            slabs[q, 4:10, 0:24, :] = whole[4:10, 24 * q : 24 * q + 24, :]

    slot = 4 * place.section + place.q
    copies = {}
    for other in (0, 1):
        for r in range(4):
            if other == 0 and r == 0:
                continue
            target = lax.rem(place.q + r, 4)
            copies[other, r] = push(
                slabs.at[target], landed.at[slot], sems.take(), place.in_column(layer, target)
            )

    @pl.when(place.section == layer)
    def _():
        for r in range(1, 4):
            copies[0, r].start()
        landed[slot] = slabs[place.q]

    @pl.when(place.section != layer)
    def _():
        for r in range(4):
            copies[1, r].start()

    yield

    @pl.when(place.section == layer)
    def _():
        for copy in copies.values():
            copy.wait_recv()
        for core in range(2):
            total = landed[core] + landed[2 + core] + landed[4 + core] + landed[6 + core]
            g_ref[10 * core : 10 * core + 10] = total
        for r in range(1, 4):
            copies[0, r].wait_send()

    @pl.when(place.section != layer)
    def _():
        g_ref[...] = jnp.zeros_like(g_ref)
        for r in range(4):
            copies[1, r].wait_send()

    for copy in sent:
        copy.wait_send()


def head_steps(place, sems, heads_ref, head_out_ref, hbuf, hval):
    hval[...] = heads_ref[...]
    y = 2 * place.section + lax.div(place.q, 2)
    for index, axis in enumerate(("core", "y", "x", "z")):
        copies = []
        if axis == "core":
            mine, peers = place.core, [place.sibling()]
        elif axis == "y":
            mine, peers = y, []
            for r in range(1, 4):
                to = lax.rem(y + r, 4)
                peers.append((lax.div(to, 2), place.column + 2 * lax.rem(to, 2) + place.core))
        else:
            mine = place.z if axis == "z" else place.x
            peers = [place.along(axis, r) for r in range(1, 4)]
        for peer in peers:
            copy = push(hval, hbuf.at[index, mine], sems.take(), peer)
            copy.start()
            copies.append(copy)
        hbuf[index, mine] = hval[...]
        yield
        for copy in copies:
            copy.wait_recv()
        for copy in copies:
            copy.wait_send()
        total = hbuf[index, 0] + hbuf[index, 1]
        if axis != "core":
            total = total + hbuf[index, 2] + hbuf[index, 3]
        hval[...] = total
    head_out_ref[...] = hval[...]


REDUCE_COPIES = 10 + 4 * 4 + 7 + 10


def reduce_scratch():
    return [
        pltpu.VMEM((10, 4, 4, 96, LANE), BF16),
        pltpu.VMEM((10, 4, 4, 96, LANE), BF16),
        pltpu.VMEM((2, 2, 5, 4, 48, LANE), BF16),
        pltpu.VMEM((2, 2, 5, 4, 96, LANE), BF16),
        pltpu.VMEM((2, 2, 5, 48, LANE), BF16),
        pltpu.VMEM((2, 2, 5, 96, LANE), BF16),
        pltpu.VMEM((10, 96, LANE), F32),
        pltpu.VMEM((4, 10, 32, LANE), F32),
        pltpu.VMEM((8, 10, 32, LANE), F32),
        pltpu.VMEM((4, 4, 8, LANE), F32),
        pltpu.VMEM((8, LANE), F32),
        pltpu.SemaphoreType.DMA((REDUCE_COPIES,)),
        pltpu.SemaphoreType.DMA((REDUCE_COPIES,)),
        pltpu.SemaphoreType.DMA((10,)),
    ]


def reduce_kernel(layer, d_ref, heads_ref, g_ref, head_out_ref, *scratch):
    *bufs, hval, send, recv, local = scratch
    place = Place()
    greet(place)
    sems = Sems(send, recv)
    work = reduce_steps(layer, place, sems, local, d_ref, heads_ref, g_ref, head_out_ref, bufs)
    if layer == 0:
        small = head_steps(place, sems, heads_ref, head_out_ref, bufs[9], hval)
    else:
        head_out_ref[...] = heads_ref[...]
        small = iter(())
    for index, _ in enumerate(work):
        if index % 4 == 0:
            next(small, None)
    for _ in small:
        pass


def run_reduce(layer, d, heads):
    return pl.pallas_call(
        functools.partial(reduce_kernel, layer),
        out_shape=(
            jax.ShapeDtypeStruct((20, 32, LANE), F32),
            jax.ShapeDtypeStruct((8, LANE), F32),
        ),
        in_specs=[pl.BlockSpec(memory_space=pl.ANY), pl.BlockSpec(memory_space=pltpu.VMEM)],
        out_specs=tuple(vm(2)),
        scratch_shapes=reduce_scratch(),
        compiler_params=pltpu.CompilerParams(
            collective_id=2 + layer, has_side_effects=True, vmem_limit_bytes=56 * 1024 * 1024
        ),
        name=f"reduce_layer_{layer}",
    )(d, heads)


def pack_shards(in_weight, out_weight, norm_gain, conv_weight, conv_bias, gated_gain):
    wide = jnp.pad(in_weight, ((0, 0), (0, WIDE - in_weight.shape[1])))
    wide = jnp.pad(wide.reshape(12, 14, 2, LANE).transpose(1, 2, 0, 3), ((0, 0), (0, 0), (0, 4), (0, 0)))
    taps = jnp.pad(conv_weight, ((0, 0), (0, 4))).reshape(1, LANE)
    rest = (conv_bias, jnp.zeros((4,), BF16), norm_gain, jnp.zeros((20,), BF16), gated_gain, jnp.zeros((40,), BF16))
    small = jnp.concatenate([taps, jnp.concatenate(rest).reshape(1, LANE)], axis=0)
    wide = wide.at[13, 1, 0:2].set(small)
    tall = jnp.pad(out_weight.reshape(24, 6, LANE).transpose(1, 0, 2), ((0, 0), (0, 8), (0, 0)))
    return jnp.concatenate([wide.reshape(14, 32, LANE), tall], axis=0)


def body(
    block_input,
    out_grad,
    live_mask,
    norm_gain,
    in_weight,
    conv_weight,
    conv_bias,
    dt_bias,
    a_log,
    d_skip,
    gated_gain,
    out_weight,
):
    section = lax.axis_index("section")
    first = section == 0
    idx = owner_index()
    shard = pack_shards(
        in_weight[0], out_weight[0], norm_gain[0], conv_weight[0], conv_bias[0], gated_gain[0]
    )
    own_heads = jnp.pad(jnp.concatenate([dt_bias, a_log, d_skip], axis=0), ((0, 5), (0, LANE - HEADS)))
    weight0, heads = run_gather(0, shard, own_heads)
    weight1, _ = run_gather(1, shard, own_heads)
    weight0 = weight0.reshape(20, 16, 96, LANE)
    weight1 = weight1.reshape(20, 16, 96, LANE)
    stream0 = jnp.where(first, block_input[0, 0], block_input[1, 0])
    live = jnp.where(first, live_mask[0, 0], live_mask[1, 0]).astype(BF16)
    cotangent = jnp.where(first, out_grad[0, 0], out_grad[1, 0]) * live
    act0, *saved0 = run_forward(stream0, weight0, heads[0], idx)
    act0_in = lax.ppermute(act0, "section", [(1, 0)])
    act1, *saved1 = run_forward(act0, weight1, heads[1], idx)
    act1_in = lax.ppermute(act1, "section", [(0, 1)])
    grad1, low1, weight_grad1, head_grad1 = run_backward(
        act0, cotangent, weight1, heads[1], idx, *saved1
    )
    grad1_in = lax.ppermute(low1, "section", [(0, 1)])
    total1, _ = run_reduce(1, weight_grad1.reshape(20, 4, 4, 96, LANE), head_grad1)
    grad0, low0, weight_grad0, head_grad0 = run_backward(
        stream0, low1, weight0, heads[0], idx, *saved0
    )
    grad0_in = lax.ppermute(low0, "section", [(1, 0)])
    head_grads = jnp.concatenate([head_grad0[0:4], head_grad1[0:4]], axis=0)
    total0, head_totals = run_reduce(0, weight_grad0.reshape(20, 4, 4, 96, LANE), head_grads)

    activations = jnp.where(first, jnp.stack([act0, act0_in]), jnp.stack([act1_in, act1]))
    input_grads = jnp.where(
        first,
        jnp.stack([grad0, grad0_in.astype(F32)]),
        jnp.stack([grad1_in.astype(F32), grad1]),
    )
    total = jnp.where(first, total0, total1)
    per_head = jnp.where(first, head_totals[0:3, :HEADS], head_totals[4:7, :HEADS])
    wide = total[:14].reshape(14, 2, 16, LANE)[:, :, :12].transpose(2, 0, 1, 3).reshape(12, WIDE)
    small = total[13, 16:18]
    tall = total[14:, :24].transpose(1, 0, 2).reshape(24, D)
    return (
        activations[None, :, None],
        input_grads[None, :, None],
        small[1:2, 32:44],
        wide[None, :, : in_weight.shape[2]],
        small[0].reshape(1, 4, 32)[:, :, :28],
        small[1:2, 0:28],
        per_head[0:1],
        per_head[1:2],
        per_head[2:3],
        small[1:2, 64:88],
        tall[None],
    )


def solution(mesh):
    placed = (
        P(None, "dp", None, None),
        P(None, "dp", None, None),
        P(None, "dp"),
        P("section", "dp"),
        P("section", "dp", None),
        P("section", None, "dp"),
        P("section", "dp"),
        P("section", None),
        P("section", None),
        P("section", None),
        P("section", "dp"),
        P("section", "dp", None),
    )
    return jax.shard_map(
        body,
        mesh=mesh,
        in_specs=placed,
        out_specs=(
            P("section", None, "dp", None, None),
            P("section", None, "dp", None, None),
            P("section", "dp"),
            P("section", "dp", None),
            P("section", None, "dp"),
            P("section", "dp"),
            P("section", None),
            P("section", None),
            P("section", None),
            P("section", "dp"),
            P("section", "dp", None),
        ),
        check_vma=False,
    )
```

```python
import functools

import jax
import jax.numpy as jnp
import numpy as np
from jax import lax
from jax.experimental import pallas as pl
from jax.experimental.pallas import tpu as pltpu
from jax.sharding import PartitionSpec as P

F32 = jnp.float32
BF16 = jnp.bfloat16
MESH = pl.DeviceIdType.MESH
EPS = 1e-05
T = 256
GROUP = 128
LANE = 128
D = 768
DI = 1536
HEADS = 24
CHANNELS = 1792
WIDE = 3584
ROW_GAIN = 0
ROW_TAPS = 6
ROW_BIAS = 62
ROW_GATED = 76
SMALL = 88


def mm(a, b, dims, precision=None):
    return lax.dot_general(a, b, (dims, ((), ())), precision=precision, preferred_element_type=F32)


NN = ((1,), (0,))
NT = ((1,), (1,))
TN = ((0,), (0,))
EXACT = lax.Precision.HIGHEST


def chunk(j):
    return slice(LANE * j, LANE * (j + 1))


def in_pair(w_ref, j):
    left = w_ref[j // 2, j % 2, :, :, 0:48, :].reshape(D, LANE)
    right = w_ref[j // 2, j % 2, :, :, 48:96, :].reshape(D, LANE)
    return jnp.concatenate([left, right], axis=1)


def out_pair(w_ref, c):
    left = w_ref[7 + c // 2, 0].reshape(DI, LANE)
    right = w_ref[7 + c // 2, 1].reshape(DI, LANE)
    return jnp.concatenate([left, right], axis=1)


def lane_half():
    return lax.broadcasted_iota(jnp.int32, (1, LANE), 1) < 64


def lower_mask():
    rows = lax.broadcasted_iota(jnp.int32, (GROUP, GROUP), 0)
    cols = lax.broadcasted_iota(jnp.int32, (GROUP, GROUP), 1)
    return rows >= cols


def down(x, k):
    if k == 0:
        return x
    rows = lax.broadcasted_iota(jnp.int32, x.shape, 0)
    return jnp.where(rows >= k, pltpu.roll(x, k, 0), 0.0)


def up(x, k):
    if k == 0:
        return x
    rows = lax.broadcasted_iota(jnp.int32, x.shape, 0)
    return jnp.where(rows < T - k, pltpu.roll(x, T - k, 0), 0.0)


def sigmoid(x):
    return 1.0 / (1.0 + jnp.exp(-x))


def conv_of(proj_ref, conv_ref, j):
    x = proj_ref[:, DI + LANE * j : DI + LANE * (j + 1)]
    out = conv_ref[4:5, chunk(j)] + conv_ref[3:4, chunk(j)] * x
    for k in range(1, 4):
        out = out + conv_ref[3 - k : 4 - k, chunk(j)] * down(x, k)
    return x, out


def spread(cols, p):
    return jnp.where(lane_half(), cols[:, 2 * p : 2 * p + 1], cols[:, 2 * p + 1 : 2 * p + 2])


def steps_of(proj_ref, head_ref):
    raw = proj_ref[:, DI + CHANNELS : DI + CHANNELS + LANE] + head_ref[0:1, :]
    steps = jnp.maximum(raw, 0.0) + jnp.log1p(jnp.exp(-jnp.abs(raw)))
    rates = -steps * jnp.exp(head_ref[1:2, :])
    tri = lower_mask().astype(F32)
    cumul = [mm(tri, rates[GROUP * b : GROUP * (b + 1)], NN, EXACT) for b in range(2)]
    return raw, steps, rates, cumul


def forward_steps(s_ref, w_ref, head_ref, idx_ref, act_ref, proj_ref, scan_ref, gain_ref, conv_ref, wide_ref,
            mixed_ref, nout_ref):
    unpack_all(w_ref, idx_ref, head_ref, gain_ref, conv_ref, wide_ref)
    stream = s_ref[...].astype(F32)
    scale = lax.rsqrt(jnp.mean(stream * stream, axis=-1, keepdims=True) + EPS)
    normed = (stream * scale * gain_ref[0:1, :]).astype(BF16)
    for j in range(14):
        got = mm(normed, in_pair(w_ref, j), NN)
        proj_ref[:, 2 * LANE * j : 2 * LANE * (j + 1)] = got
        yield "in"
    for j in range(14):
        _, out = conv_of(proj_ref, conv_ref, j)
        mixed_ref[:, chunk(j)] = (out * sigmoid(out)).astype(BF16)
        yield "conv"
    _, steps, _, cumul = steps_of(proj_ref, head_ref)
    lower = lower_mask()
    half = lane_half()
    key = [mixed_ref[GROUP * b : GROUP * (b + 1), chunk(12)] for b in range(2)]
    query = [mixed_ref[GROUP * b : GROUP * (b + 1), chunk(13)] for b in range(2)]
    scores = [mm(query[b], key[b], NT) for b in range(2)]
    cross = mm(query[1], key[0], NT).astype(BF16)
    cumul_t = [c.T for c in cumul]
    total = jnp.zeros((T, 1), F32)
    for p in range(12):
        tail_u = None
        squares = []
        for b in range(2):
            rows = slice(GROUP * b, GROUP * (b + 1))
            x = mixed_ref[rows, chunk(p)].astype(F32)
            u = x * spread(steps[rows], p)
            weights = []
            for h in (2 * p, 2 * p + 1):
                gap = cumul[b][:, h : h + 1] - cumul_t[b][h : h + 1, :]
                weights.append((scores[b] * jnp.exp(jnp.where(lower, gap, -1e30))).astype(BF16))
            u_two = jnp.concatenate([jnp.where(half, u, 0.0), jnp.where(half, 0.0, u)], axis=0)
            y = mm(jnp.concatenate(weights, axis=1), u_two.astype(BF16), NN)
            cum = spread(cumul[b], p)
            if b == 0:
                tail_u = (jnp.exp(cum[GROUP - 1 : GROUP, :] - cum) * u).astype(BF16)
            else:
                y = y + jnp.exp(cum) * mm(cross, tail_u, NN)
            y = y + x * wide_ref[1:2, chunk(p)]
            scan_ref[rows, chunk(p)] = y
            z = proj_ref[rows, chunk(p)]
            gated = y * (z * sigmoid(z))
            squares.append(jnp.sum(gated * gated, axis=-1, keepdims=True))
        total = total + jnp.concatenate(squares, axis=0)
        yield "scan"
    scale_out = lax.rsqrt(total * (1.0 / DI) + EPS)
    for p in range(12):
        z = proj_ref[:, chunk(p)]
        gated = scan_ref[:, chunk(p)] * (z * sigmoid(z))
        nout_ref[:, chunk(p)] = (gated * scale_out * wide_ref[0:1, chunk(p)]).astype(BF16)
    yield "norm"
    for c in range(0, 6, 2):
        cols = slice(LANE * c, LANE * (c + 2))
        branch = mm(nout_ref[...], out_pair(w_ref, c), NN)
        act_ref[:, cols] = (s_ref[:, cols].astype(F32) + branch).astype(BF16)
        yield "branch"


def forward(*refs):
    for _ in forward_steps(*refs):
        pass


def fold(value, expand):
    high = value.astype(BF16)
    low = (value - high.astype(F32)).astype(BF16)
    return mm(high, expand, NN) + mm(low, expand, NN)


def backward_steps(s_ref, gout_ref, w_ref, head_ref, idx_ref, proj_ref, scan_ref, gain_ref, conv_ref, wide_ref,
             gin_ref, low_ref, d_ref, hgrad_ref,
             mixed_ref, nout_ref, gno_ref, gproj_ref, dmix_ref, dcum_ref, dstep_ref, small_ref, pack_ref, norm_ref, gnorm_ref):
    hgrad_ref[...] = jnp.zeros_like(hgrad_ref)
    skip_sum = jnp.zeros((1, LANE), F32)
    lower = lower_mask()
    half = lane_half()
    grad_branch = gout_ref[...]
    total = jnp.zeros((T, 1), F32)
    for p in range(12):
        z = proj_ref[:, chunk(p)]
        gated = scan_ref[:, chunk(p)] * (z * sigmoid(z))
        total = total + jnp.sum(gated * gated, axis=-1, keepdims=True)
        yield "square"
    scale_out = lax.rsqrt(total * (1.0 / DI) + EPS)
    for c in range(0, 6, 2):
        part = mm(grad_branch[:, LANE * c : LANE * (c + 2)], out_pair(w_ref, c), NT)
        if c == 0:
            gno_ref[...] = part
        else:
            gno_ref[...] += part
    inner = jnp.zeros((T, 1), F32)
    for p in range(12):
        z = proj_ref[:, chunk(p)]
        gated = scan_ref[:, chunk(p)] * (z * sigmoid(z))
        unit = gated * scale_out
        gain = wide_ref[0:1, chunk(p)]
        nout_ref[:, chunk(p)] = (unit * gain).astype(BF16)
        gno = gno_ref[:, chunk(p)]
        small_ref[ROW_GATED + p : ROW_GATED + p + 1, :] = jnp.sum(gno * unit, axis=0, keepdims=True)
        inner = inner + jnp.sum(gno * gain * unit, axis=-1, keepdims=True)
        yield "inner"
    inner = inner * (1.0 / DI)
    for c in range(0, 6, 2):
        grad = mm(nout_ref[...], grad_branch[:, LANE * c : LANE * (c + 2)], TN).astype(BF16)
        for e in range(2):
            d_ref[7 + c // 2, e] = grad[:, LANE * e : LANE * (e + 1)].reshape(4, 4, 96, LANE)
        yield 7 + c // 2
    for p in range(12):
        z = proj_ref[:, chunk(p)]
        scan = scan_ref[:, chunk(p)]
        sig = sigmoid(z)
        silu = z * sig
        unit = scan * silu * scale_out
        ggated = scale_out * (gno_ref[:, chunk(p)] * wide_ref[0:1, chunk(p)] - unit * inner)
        gproj_ref[:, chunk(p)] = (ggated * scan * (sig + silu * (1.0 - sig))).astype(BF16)
        gno_ref[:, chunk(p)] = ggated * silu
        yield "gate"
    stream = s_ref[...].astype(F32)
    scale = lax.rsqrt(jnp.mean(stream * stream, axis=-1, keepdims=True) + EPS)
    norm_ref[...] = (stream * scale * gain_ref[0:1, :]).astype(BF16)

    def in_grad(j):
        gp = gproj_ref[:, 2 * LANE * j : 2 * LANE * (j + 1)]
        grad = mm(norm_ref[...], gp, TN).astype(BF16)
        for e in range(1 if j == 13 else 2):
            part = grad[:, LANE * e : LANE * (e + 1)].reshape(4, 4, 48, LANE)
            d_ref[j // 2, j % 2, :, :, 48 * e : 48 * (e + 1), :] = part
        back = mm(gp, in_pair(w_ref, j), NT)
        if j == 0:
            gnorm_ref[...] = back
        else:
            gnorm_ref[...] += back

    for j in range(6):
        in_grad(j)
        yield j // 2 if j % 2 else "grad"
    for j in range(14):
        _, out = conv_of(proj_ref, conv_ref, j)
        mixed_ref[:, chunk(j)] = (out * sigmoid(out)).astype(BF16)
        yield "conv"
    raw, steps, rates, cumul = steps_of(proj_ref, head_ref)
    key = [mixed_ref[GROUP * b : GROUP * (b + 1), chunk(12)] for b in range(2)]
    query = [mixed_ref[GROUP * b : GROUP * (b + 1), chunk(13)] for b in range(2)]
    scores = [mm(query[b], key[b], NT) for b in range(2)]
    cross = mm(query[1], key[0], NT).astype(BF16)
    cumul_t = [c.T for c in cumul]
    dscores = [jnp.zeros((GROUP, GROUP), F32) for _ in range(2)]
    dcross = jnp.zeros((GROUP, GROUP), F32)
    dcum_ref[...] = jnp.zeros_like(dcum_ref)
    dstep_ref[...] = jnp.zeros_like(dstep_ref)
    lanes = lax.broadcasted_iota(jnp.int32, (1, LANE), 1)
    head_row = lax.broadcasted_iota(jnp.int32, (LANE, LANE), 0)
    head_col = lax.broadcasted_iota(jnp.int32, (LANE, LANE), 1)
    row_sum = [jnp.zeros((GROUP, LANE), F32) for _ in range(2)]
    for p in range(12):
        expand = (head_col == 2 * p + jnp.where(head_row < 64, 0, 1)).astype(BF16)
        tail_u = eg = None
        us, xs, dus, step_es, grads = [], [], [], [], []
        tail = None
        for b in range(2):
            rows = slice(GROUP * b, GROUP * (b + 1))
            x = mixed_ref[rows, chunk(p)].astype(F32)
            step_e = spread(steps[rows], p)
            u = x * step_e
            g = gno_ref[rows, chunk(p)]
            g_two = jnp.concatenate([jnp.where(half, g, 0.0), jnp.where(half, 0.0, g)], axis=0)
            g_two = g_two.astype(BF16)
            value = mm(g_two, u.astype(BF16), NT)
            weights = []
            for e in range(2):
                h = 2 * p + e
                gap = cumul[b][:, h : h + 1] - cumul_t[b][h : h + 1, :]
                decay = jnp.exp(jnp.where(lower, gap, -1e30))
                weight = scores[b] * decay
                weights.append(weight.astype(BF16))
                v = value[GROUP * e : GROUP * (e + 1)]
                dscores[b] = dscores[b] + v * decay
                both = v * weight
                row_sum[b] = jnp.where(lanes == h, jnp.sum(both, axis=-1, keepdims=True), row_sum[b])
                dcum_ref[b, h : h + 1, :] = -jnp.sum(both, axis=0, keepdims=True)
            du = mm(jnp.concatenate(weights, axis=0), g_two, TN)
            us.append(u)
            xs.append(x)
            dus.append(du)
            step_es.append(step_e)
            grads.append(g)
            cum = spread(cumul[b], p)
            if b == 0:
                tail = jnp.exp(cum[GROUP - 1 : GROUP, :] - cum)
                tail_u = tail * u
            else:
                eg = jnp.exp(cum) * g
        tail_low = tail_u.astype(BF16)
        eg_low = eg.astype(BF16)
        dtail = mm(cross, eg_low, TN)
        dcross = dcross + mm(eg_low, tail_low, NT)
        dus[0] = dus[0] + tail * dtail
        column = fold(tail_u * dtail, expand)
        row_sum[0] = row_sum[0] - column
        row_sum[0] = row_sum[0] + jnp.where(
            lax.broadcasted_iota(jnp.int32, (GROUP, 1), 0) == GROUP - 1,
            jnp.sum(column, axis=0, keepdims=True), 0.0)
        row_sum[1] = row_sum[1] + fold(eg * mm(cross, tail_low, NN), expand)
        skip = jnp.zeros((1, LANE), F32)
        for b in range(2):
            rows = slice(GROUP * b, GROUP * (b + 1))
            dstep_ref[rows, :] += fold(dus[b] * xs[b], expand)
            dmix_ref[rows, chunk(p)] = step_es[b] * dus[b] + grads[b] * wide_ref[1:2, chunk(p)]
            skip = skip + jnp.sum(grads[b] * xs[b], axis=0, keepdims=True)
        yield "scan"
        skip_sum = skip_sum + fold(jnp.broadcast_to(skip, (8, LANE)), expand)[0:1]
    dcross_low = dcross.astype(BF16)
    ds_low = [d.astype(BF16) for d in dscores]
    dmix_ref[0:GROUP, chunk(12)] = mm(ds_low[0], query[0], TN) + mm(dcross_low, query[1], TN)
    dmix_ref[GROUP:T, chunk(12)] = mm(ds_low[1], query[1], TN)
    dmix_ref[0:GROUP, chunk(13)] = mm(ds_low[0], key[0], NN)
    dmix_ref[GROUP:T, chunk(13)] = mm(ds_low[1], key[1], NN) + mm(dcross_low, key[0], NN)
    tri = lower.astype(F32)
    decay_rate = jnp.exp(head_ref[1:2, :])
    step_sum = jnp.zeros((1, LANE), F32)
    decay_sum = jnp.zeros((1, LANE), F32)
    for b in range(2):
        rows = slice(GROUP * b, GROUP * (b + 1))
        drate = mm(tri, row_sum[b] + dcum_ref[b].T, TN, EXACT)
        draw = (dstep_ref[rows, :] - decay_rate * drate) * sigmoid(raw[rows])
        draw = jnp.where(lanes < HEADS, draw, 0.0)
        decay_sum = decay_sum + jnp.sum(drate * rates[rows], axis=0, keepdims=True)
        step_sum = step_sum + jnp.sum(draw, axis=0, keepdims=True)
        gproj_ref[rows, DI + CHANNELS : DI + CHANNELS + LANE] = draw.astype(BF16)
    hgrad_ref[0:1, :] = step_sum
    hgrad_ref[1:2, :] = decay_sum
    hgrad_ref[2:3, :] = skip_sum
    gproj_ref[:, WIDE - LANE :] = jnp.zeros((T, LANE), BF16)
    for j in range(14):
        x, out = conv_of(proj_ref, conv_ref, j)
        sig = sigmoid(out)
        dconv = dmix_ref[:, chunk(j)] * (sig + out * sig * (1.0 - sig))
        small_ref[ROW_BIAS + j : ROW_BIAS + j + 1, :] = jnp.sum(dconv, axis=0, keepdims=True)
        dx = conv_ref[3:4, chunk(j)] * dconv
        for k in range(4):
            row = ROW_TAPS + 14 * (3 - k) + j
            small_ref[row : row + 1, :] = jnp.sum(dconv * down(x, k), axis=0, keepdims=True)
            if k:
                dx = dx + conv_ref[3 - k : 4 - k, chunk(j)] * up(dconv, k)
        gproj_ref[:, DI + LANE * j : DI + LANE * (j + 1)] = dx.astype(BF16)
        yield "taps"
    for j in (6, 7, 8, 9, 10, 11, 13, 12):
        in_grad(j)
        yield j // 2 if j % 2 and j < 12 else "grad"
    gnormed = gnorm_ref[...]
    unit = stream * scale
    gain_grad = jnp.sum(gnormed * unit, axis=0, keepdims=True)
    for c in range(6):
        small_ref[ROW_GAIN + c : ROW_GAIN + c + 1, :] = gain_grad[:, chunk(c)]
    pack_all(small_ref, idx_ref, pack_ref)
    d_ref[6, 1, :, :, 48:64, :] = pack_ref[...].astype(BF16).reshape(4, 4, 16, LANE)
    d_ref[6, 1, :, :, 64:96, :] = jnp.zeros((4, 4, 32, LANE), BF16)
    yield 6
    gunit = gnormed * gain_ref[0:1, :]
    center = jnp.mean(gunit * unit, axis=-1, keepdims=True)
    gin = gout_ref[...].astype(F32) + scale * (gunit - unit * center)
    gin_ref[...] = gin
    low_ref[...] = gin.astype(BF16)
    yield "done"


def backward(*refs):
    for _ in backward_steps(*refs):
        pass


KINDS = (
    (2, 12, ROW_GAIN, 6, 32, 1),
    (0, 28, ROW_TAPS, 14, 0, 0),
    (0, 28, ROW_TAPS + 14, 14, 32, 0),
    (0, 28, ROW_TAPS + 28, 14, 64, 0),
    (0, 28, ROW_TAPS + 42, 14, 96, 0),
    (0, 28, ROW_BIAS, 14, 0, 1),
    (4, 24, ROW_GATED, 12, 64, 1),
)


def owner_index():
    table = np.zeros((8, CHANNELS), np.int32)
    for row, width, length in ((0, 28, CHANNELS), (2, 12, D), (4, 24, DI)):
        position = np.arange(length)
        owner = position // width
        table[row, :length] = 16 * (owner // 4) + 2 * (owner % 4)
        table[row + 1, :length] = position % width
    return jnp.asarray(table)


def window(width, c):
    first, last = LANE * c // width, (LANE * c + LANE - 1) // width
    return 16 * (first // 4), 16 * (last // 4) + 16


def unpack(pack, idx_ref, kind, c):
    row, width, _, _, lane, line = kind
    low, high = window(width, c)
    lanes = lax.broadcasted_iota(jnp.int32, (LANE, LANE), 0)
    pick = (lanes == idx_ref[row + 1 : row + 2, chunk(c)] + lane).astype(BF16)
    rows = lax.broadcasted_iota(jnp.int32, (high - low, LANE), 0) + low
    got = mm(pack[low:high], pick, NN)
    return jnp.sum(jnp.where(rows == idx_ref[row : row + 1, chunk(c)] + line, got, 0.0), axis=0, keepdims=True)


def unpack_all(w_ref, idx_ref, head_ref, gain_ref, conv_ref, wide_ref):
    pack = w_ref[6, 1, :, :, 48:64, :].reshape(256, LANE)
    for c in range(6):
        gain_ref[0:1, chunk(c)] = unpack(pack, idx_ref, KINDS[0], c)
    for k in range(5):
        for c in range(14):
            conv_ref[k : k + 1, chunk(c)] = unpack(pack, idx_ref, KINDS[1 + k], c)
    for c in range(12):
        wide_ref[0:1, chunk(c)] = unpack(pack, idx_ref, KINDS[6], c)
        wide_ref[1:2, chunk(c)] = spread(head_ref[2:3, :], c)


def pack_all(small_ref, idx_ref, pack_ref):
    pack_ref[...] = jnp.zeros_like(pack_ref)
    for kind in KINDS:
        row, width, start, count, lane, line = kind
        for c in range(count):
            low, high = window(width, c)
            lanes = lax.broadcasted_iota(jnp.int32, (LANE, LANE), 0)
            pick = (lanes == idx_ref[row + 1 : row + 2, chunk(c)] + lane).astype(BF16)
            rows = lax.broadcasted_iota(jnp.int32, (high - low, LANE), 0) + low
            value = small_ref[start + c : start + c + 1, :]
            held = jnp.where(rows == idx_ref[row : row + 1, chunk(c)] + line, value, 0.0).astype(BF16)
            pack_ref[low:high, :] += mm(held, pick, NT)


def vm(count):
    return [pl.BlockSpec(memory_space=pltpu.VMEM)] * count


class Sems:
    def __init__(self, send, recv):
        self.send, self.recv, self.used = send, recv, 0

    def take(self):
        index = self.used
        self.used += 1
        return self.send.at[index], self.recv.at[index]


class Place:
    def __init__(self):
        self.section = lax.axis_index("section")
        self.dp = lax.axis_index("dp")
        self.z = lax.div(self.dp, 16)
        self.x = lax.rem(lax.div(self.dp, 4), 4)
        self.q = lax.rem(self.dp, 4)
        self.core = lax.rem(self.dp, 2)
        self.column = self.dp - self.q

    def at(self, z, x):
        return (self.section, 16 * z + 4 * x + self.q)

    def along(self, axis, distance):
        if axis == "z":
            return self.at(lax.rem(self.z + distance, 4), self.x)
        return self.at(self.z, lax.rem(self.x + distance, 4))

    def sibling(self):
        return (self.section, self.dp + 1 - 2 * self.core)

    def in_column(self, section, q):
        return (section, self.column + q)


def greet(place):
    barrier = pltpu.get_barrier_semaphore()
    peers = [place.in_column(place.section, lax.rem(place.q + r, 4)) for r in range(1, 4)]
    peers += [place.in_column(1 - place.section, lax.rem(place.q + r, 4)) for r in range(4)]
    peers += [place.along(axis, r) for axis in "zx" for r in range(1, 4)]
    for peer in peers:
        pl.semaphore_signal(barrier, inc=1, device_id=peer, device_id_type=MESH)
    pl.semaphore_wait(barrier, len(peers))


def push(src, dst, sems, device):
    send, recv = sems
    return pltpu.make_async_remote_copy(
        src_ref=src, dst_ref=dst, send_sem=send, recv_sem=recv, device_id=device, device_id_type=MESH
    )


PAIRS = range(10)
AXES = ("xz", "zx", "xz", "zx", "xz", "zx", "xz", "zx", "xz", "zx")
SHARD = (10, 32, LANE)
WHOLE = (10, 2, 4, 4, 96, LANE)


class Copies:
    def __init__(self, place, sems):
        self.place, self.sems, self.sent = place, sems, []

    def start(self, src, dst, device):
        copy = push(src, dst, self.sems.take(), device)
        copy.start()
        self.sent.append(copy)
        return copy

    def end(self):
        for copy in self.sent:
            copy.wait_send()


def coord(place, axis, distance):
    return lax.rem((place.z if axis == "z" else place.x) + distance, 4)


def column_copies(place, layer, sems, source, landing):
    copies = {}
    for other in (0, 1):
        for r in range(4):
            if other == 0 and r == 0:
                continue
            target = lax.rem(place.q + r, 4)
            section = layer if other == 0 else 1 - layer
            copies[other, r] = push(
                source(target), landing, sems.take(), place.in_column(section, target)
            )
    return copies


def gather_steps(layer, place, sems, local, shard_ref, w_ref, slabs, whole, own):
    run = Copies(place, sems)
    core = place.core
    copies = column_copies(place, layer, sems, lambda q: shard_ref.at[lax.rem(q, 2)], slabs.at[place.q])
    mine = pltpu.make_async_copy(shard_ref.at[core], slabs.at[place.q], local.at[0])

    @pl.when(place.section == layer)
    def _():
        for copy in copies.values():
            copy.start()
        mine.start()

    yield "column"

    @pl.when(place.section == layer)
    def _():
        mine.wait()
        for r in range(1, 4):
            copies[0, r].wait_recv()

    @pl.when(place.section != layer)
    def _():
        for r in range(4):
            copies[1, r].wait_recv()

    whole[...] = jnp.zeros_like(whole)
    for q in range(4):
        part = slabs[q].astype(F32)
        whole[0:7, 12 * q : 12 * q + 12, :] = part[0:7, 0:12]
        whole[0:6, 48 + 12 * q : 60 + 12 * q, :] = part[0:6, 16:28]

        @pl.when(core == 0)
        def _():
            whole[6, 48 + 12 * q : 60 + 12 * q, :] = part[6, 16:28]

        @pl.when(core == 1)
        def _():
            whole[6, 48 + 2 * q : 50 + 2 * q, :] = part[6, 16:18]

        whole[7:10, 24 * q : 24 * q + 24, :] = part[7:10, 0:24]
    own[...] = whole[...].astype(BF16)
    keep = pltpu.make_async_copy(own, w_ref.at[:, core, place.z, place.x], local.at[1])
    keep.start()
    first, second, third = {}, {}, {}
    for i in PAIRS:
        there = w_ref.at[i, core, place.z, place.x]
        axis = AXES[i][0]
        first[i] = [run.start(own.at[i], there, place.along(axis, r)) for r in (1, 3, 2)]

    def line(i, distance, rows=None):
        axis = AXES[i][1]
        at = coord(place, axis, distance)
        z, x = (at, pl.ds(0, 4)) if axis == "z" else (pl.ds(0, 4), at)
        if rows is None:
            return w_ref.at[i, core, z, x]
        return w_ref.at[i, core, z, x, pl.ds(rows, 48)]

    for i in PAIRS:
        yield "first"
        if i == 0:
            keep.wait()
        for copy in first[i]:
            copy.wait_recv()
        src = line(i, 0)
        second[i] = [run.start(src, src, place.along(AXES[i][1], r)) for r in (1, 3)]
    for i in PAIRS:
        yield "second"
        second[i][0].wait_recv()
        got = line(i, 3, 0)
        one = run.start(got, got, place.along(AXES[i][1], 1))
        second[i][1].wait_recv()
        got = line(i, 1, 48)
        two = run.start(got, got, place.along(AXES[i][1], 3))
        third[i] = (one, two)
    over = {}
    for i in PAIRS:
        yield "third"
        for copy in third[i]:
            copy.wait_recv()
        half = w_ref.at[i, core]
        over[i] = run.start(half, half, place.sibling())
    for i in PAIRS:
        yield "over"
        over[i].wait_recv()
    yield "whole"
    run.end()

    @pl.when(place.section == layer)
    def _():
        for copy in copies.values():
            copy.wait_send()


GATHER_COPIES = 7 + 8 * 10


def gather_scratch():
    return [
        pltpu.VMEM((4,) + SHARD, BF16),
        pltpu.VMEM((10, 96, LANE), F32),
        pltpu.VMEM((10, 96, LANE), BF16),
        pltpu.SemaphoreType.DMA((2,)),
    ]


def go(steps, count):
    for _ in range(count):
        next(steps, None)


def entry_kernel(s_ref, shard_ref, head_ref, idx_ref, w0_ref, w1_ref, heads_ref, act_ref, proj_ref, scan_ref,
                 gain_ref, conv_ref, wide_ref, w_here, mixed, nout, send, recv, local, *scratch):
    place = Place()
    greet(place)
    sems = Sems(send, recv)
    partner = place.in_column(1 - place.section, place.q)
    swap = push(head_ref, heads_ref.at[place.section], sems.take(), partner)
    swap.start()
    heads_ref[place.section] = head_ref[...]
    zero = gather_steps(0, place, sems, scratch[3], shard_ref, w_here, *scratch[0:3])
    one = gather_steps(1, place, sems, scratch[7], shard_ref, w1_ref, *scratch[4:7])
    go(zero, 1)
    go(one, 1)
    go(zero, 11)
    go(one, 1)
    go(zero, 10)
    go(one, 10)
    go(zero, 21)
    swap.wait()
    saved = pltpu.make_async_copy(w_here, w0_ref, local.at[0])
    saved.start()
    work = forward_steps(s_ref, w_here, heads_ref.at[0], idx_ref, act_ref, proj_ref, scan_ref,
                         gain_ref, conv_ref, wide_ref, mixed, nout)
    for what in work:
        if what in ("conv", "scan", "branch"):
            go(one, 1)
    for _ in one:
        pass
    go(zero, 1)
    saved.wait()


def run_entry(s, shard, head, idx):
    copies = 1 + 2 * GATHER_COPIES
    return pl.pallas_call(
        entry_kernel,
        out_shape=(
            jax.ShapeDtypeStruct(WHOLE, BF16),
            jax.ShapeDtypeStruct(WHOLE, BF16),
            jax.ShapeDtypeStruct((2, 8, LANE), F32),
            jax.ShapeDtypeStruct((T, D), BF16),
            jax.ShapeDtypeStruct((T, WIDE), F32),
            jax.ShapeDtypeStruct((T, DI), F32),
            jax.ShapeDtypeStruct((8, D), F32),
            jax.ShapeDtypeStruct((8, CHANNELS), F32),
            jax.ShapeDtypeStruct((8, DI), F32),
        ),
        in_specs=vm(4),
        out_specs=tuple([pl.BlockSpec(memory_space=pl.ANY)] * 2 + vm(7)),
        scratch_shapes=[
            pltpu.VMEM(WHOLE, BF16),
            pltpu.VMEM((T, CHANNELS), BF16),
            pltpu.VMEM((T, DI), BF16),
            pltpu.SemaphoreType.DMA((copies,)),
            pltpu.SemaphoreType.DMA((copies,)),
            pltpu.SemaphoreType.DMA((1,)),
        ]
        + gather_scratch()
        + gather_scratch(),
        compiler_params=pltpu.CompilerParams(
            collective_id=0, has_side_effects=True, vmem_limit_bytes=56 * 1024 * 1024
        ),
        name="gather_and_first_forward",
    )(s, shard, head, idx)


ORDER = (7, 8, 9, 0, 1, 2, 3, 4, 5, 6)


class Reduce:
    def __init__(self, layer, place, sems, local, d_ref, mine_ref, g_ref, bufs):
        self.layer, self.place, self.local = layer, place, local
        self.d, self.mine, self.g = d_ref, mine_ref, g_ref
        self.acc, self.early, self.late, self.last, self.whole, self.slabs, self.landed = bufs
        self.sems, self.run = sems, Copies(place, sems)
        self.crossing, self.kept, self.first, self.second, self.third = {}, {}, {}, {}, {}

    def line(self, i, distance, rows=None):
        axis = AXES[i][1]
        at = coord(self.place, axis, distance)
        z, x = (at, pl.ds(0, 4)) if axis == "z" else (pl.ds(0, 4), at)
        return (i, z, x) if rows is None else (i, z, x, pl.ds(rows, 48))

    def cross(self, i):
        core = self.place.core
        self.crossing[i] = self.run.start(self.d.at[i, 1 - core], self.acc.at[i], self.place.sibling())
        if self.mine is not None:
            self.kept[i] = pltpu.make_async_copy(self.d.at[i, core], self.mine.at[i], self.local.at[i])
            self.kept[i].start()

    def add(self, i):
        if self.mine is not None:
            self.kept[i].wait()
            own = self.mine[i]
        else:
            own = self.d[i, self.place.core]
        self.crossing[i].wait_recv()
        self.acc[i] = self.acc[i] + own
        axis = AXES[i][1]
        self.first[i] = (
            self.run.start(self.acc.at[self.line(i, 2, 0)], self.early.at[i, 0], self.place.along(axis, 1)),
            self.run.start(self.acc.at[self.line(i, 2, 48)], self.early.at[i, 1], self.place.along(axis, 3)),
        )

    def near(self, i):
        axis = AXES[i][1]
        copies = []
        for side, (distance, rows) in enumerate(((1, 0), (3, 48))):
            self.first[i][side].wait_recv()
            at = self.line(i, distance, rows)
            self.acc[at] = self.acc[at] + self.early[i, side]
            copies.append(
                self.run.start(self.acc.at[self.line(i, distance)], self.late.at[i, side],
                               self.place.along(axis, distance))
            )
        self.second[i] = copies

    def across(self, i):
        for copy in self.second[i]:
            copy.wait_recv()
        at = self.line(i, 0)
        total = self.acc[at].astype(F32) + self.late[i, 0].astype(F32) + self.late[i, 1].astype(F32)
        self.acc[at] = total.astype(BF16)
        axis = AXES[i][0]
        place = self.place
        copies = []
        for r in (1, 3, 2):
            to = coord(place, axis, r)
            z, x = (to, place.x) if axis == "z" else (place.z, to)
            copies.append(self.run.start(self.acc.at[i, z, x], self.last.at[i, r - 1], place.along(axis, r)))
        self.third[i] = copies

    def total(self, i):
        for copy in self.third[i]:
            copy.wait_recv()
        own = self.acc[i, self.place.z, self.place.x].astype(F32)
        for r in range(3):
            own = own + self.last[i, r].astype(F32)
        self.whole[i] = own

    def hand(self):
        place, layer, whole, slabs = self.place, self.layer, self.whole, self.slabs
        slabs[...] = jnp.zeros_like(slabs)
        for q in range(4):
            slabs[q, 0:7, 0:12, :] = whole[0:7, 12 * q : 12 * q + 12, :]
            slabs[q, 0:6, 16:28, :] = whole[0:6, 48 + 12 * q : 60 + 12 * q, :]

            @pl.when(place.core == 0)
            def _():
                slabs[q, 6, 16:28, :] = whole[6, 48 + 12 * q : 60 + 12 * q, :]

            @pl.when(place.core == 1)
            def _():
                slabs[q, 6, 16:18, :] = whole[6, 48 + 2 * q : 50 + 2 * q, :]

            slabs[q, 7:10, 0:24, :] = whole[7:10, 24 * q : 24 * q + 24, :]
        slot = 4 * place.section + place.q
        copies = {}
        for other in (0, 1):
            for r in range(4):
                if other == 0 and r == 0:
                    continue
                target = lax.rem(place.q + r, 4)
                copies[other, r] = push(
                    slabs.at[target], self.landed.at[slot], self.sems.take(), place.in_column(layer, target)
                )

        @pl.when(place.section == layer)
        def _():
            for r in range(1, 4):
                copies[0, r].start()
            self.landed[slot] = slabs[place.q]

        @pl.when(place.section != layer)
        def _():
            for r in range(4):
                copies[1, r].start()

        self.copies = copies

    def finish(self):
        place, copies, landed = self.place, self.copies, self.landed

        @pl.when(place.section == self.layer)
        def _():
            for copy in copies.values():
                copy.wait_recv()
            for core in range(2):
                self.g[core] = landed[core] + landed[2 + core] + landed[4 + core] + landed[6 + core]
            for r in range(1, 4):
                copies[0, r].wait_send()

        @pl.when(place.section != self.layer)
        def _():
            for r in range(4):
                copies[1, r].wait_send()

        self.run.end()


REDUCE_COPIES = 8 * 10 + 7


def reduce_scratch():
    return [
        pltpu.VMEM((10, 4, 4, 96, LANE), BF16),
        pltpu.VMEM((10, 2, 4, 48, LANE), BF16),
        pltpu.VMEM((10, 2, 4, 96, LANE), BF16),
        pltpu.VMEM((10, 3, 96, LANE), BF16),
        pltpu.VMEM((10, 96, LANE), F32),
        pltpu.VMEM((4,) + SHARD, F32),
        pltpu.VMEM((8,) + SHARD, F32),
    ]


def head_steps(place, sems, hval, head_out_ref, hbuf):
    y = 2 * place.section + lax.div(place.q, 2)
    for index, axis in enumerate(("core", "y", "x", "z")):
        copies = []
        if axis == "core":
            mine, peers = place.core, [place.sibling()]
        elif axis == "y":
            mine, peers = y, []
            for r in range(1, 4):
                to = lax.rem(y + r, 4)
                peers.append((lax.div(to, 2), place.column + 2 * lax.rem(to, 2) + place.core))
        else:
            mine = place.z if axis == "z" else place.x
            peers = [place.along(axis, r) for r in range(1, 4)]
        for peer in peers:
            copy = push(hval, hbuf.at[index, mine], sems.take(), peer)
            copy.start()
            copies.append(copy)
        hbuf[index, mine] = hval[...]
        yield
        for copy in copies:
            copy.wait_recv()
        for copy in copies:
            copy.wait_send()
        total = hbuf[index, 0] + hbuf[index, 1]
        if axis != "core":
            total = total + hbuf[index, 2] + hbuf[index, 3]
        hval[...] = total
    head_out_ref[...] = hval[...]


def exit_kernel(s_ref, gout_ref, w_ref, head_ref, idx_ref, proj_ref, scan_ref, gain_ref, conv_ref, wide_ref,
                d1_ref, hgrad1_ref, act0_ref, act1_ref, gin1_ref,
                acts_ref, grads_ref, g_ref, head_out_ref,
                d_ref, gin_ref, low_ref, hgrad_ref, hval, hbuf, back_in, mine, send, recv, local, *scratch):
    work_refs, scratch = scratch[:11], scratch[11:]
    place = Place()
    greet(place)
    sems = Sems(send, recv)
    one = Reduce(1, place, sems, local, d1_ref, mine, g_ref, scratch[0:7])
    zero = Reduce(0, place, sems, local, d_ref, None, g_ref, scratch[7:14])
    first = place.section == 0
    partner = place.in_column(1 - place.section, place.q)
    for i in ORDER:
        one.cross(i)
    act_out = [push(ref, acts_ref.at[place.section], pair, partner)
               for pair in (sems.take(),) for ref in (act1_ref, act0_ref)]
    back_out = [push(ref, back_in, pair, partner) for pair in (sems.take(),) for ref in (gout_ref, low_ref)]

    @pl.when(first)
    def _():
        act_out[0].start()
        back_out[0].start()
        acts_ref[0] = act0_ref[...]

    @pl.when(place.section == 1)
    def _():
        act_out[1].start()
        acts_ref[1] = act1_ref[...]
        grads_ref[1] = gin1_ref[...]

    queue = []
    for i in ORDER:
        queue.append((one.add, i))
    for i in ORDER:
        queue.append((one.near, i))
    for i in ORDER:
        queue.append((one.across, i))
    for i in ORDER:
        queue.append((one.total, i))

    def take(count):
        for _ in range(count):
            if queue:
                step, i = queue.pop(0)
                step(i)

    work = backward_steps(s_ref, gout_ref, w_ref, head_ref, idx_ref, proj_ref, scan_ref, gain_ref, conv_ref,
                          wide_ref, gin_ref, low_ref, d_ref, hgrad_ref, *work_refs)
    waiting, count = [], 0
    for what in work:
        count += 1
        if isinstance(what, int):
            zero.cross(what)
            waiting.append(what)
        if count % SPACING == 0:
            take(1)
        if what == "scan" and len(waiting) > 1:
            zero.add(waiting.pop(0))
    hval[...] = jnp.zeros_like(hval)
    hval[0:4, :] = hgrad_ref[0:4, :]
    hval[4:8, :] = hgrad1_ref[0:4, :]
    small = head_steps(place, sems, hval, head_out_ref, hbuf)
    go(small, 1)

    @pl.when(place.section == 1)
    def _():
        back_out[1].start()

    @pl.when(first)
    def _():
        grads_ref[0] = gin_ref[...]

    rest = [(zero.add, i) for i in waiting]
    while rest or queue:
        if rest:
            step, i = rest.pop(0)
            step(i)
        take(1)
    one.hand()
    go(small, 1)
    for i in ORDER:
        zero.near(i)
    go(small, 1)
    for i in ORDER:
        zero.across(i)
    go(small, 1)
    one.finish()
    for i in ORDER:
        zero.total(i)
    go(small, 1)
    zero.hand()
    act_out[0].wait()
    back_out[0].wait()

    @pl.when(first)
    def _():
        grads_ref[1] = back_in[...].astype(F32)

    @pl.when(place.section == 1)
    def _():
        grads_ref[0] = back_in[...].astype(F32)

    zero.finish()


SPACING = 3


def run_exit(s, gout, w, heads, idx, proj, scan, gain, conv, wide, d1, hgrad1, act0, act1, gin1):
    copies = 2 * REDUCE_COPIES + 10 + 2
    return pl.pallas_call(
        exit_kernel,
        out_shape=(
            jax.ShapeDtypeStruct((2, T, D), BF16),
            jax.ShapeDtypeStruct((2, T, D), F32),
            jax.ShapeDtypeStruct((2,) + SHARD, F32),
            jax.ShapeDtypeStruct((8, LANE), F32),
        ),
        in_specs=vm(10) + [pl.BlockSpec(memory_space=pl.ANY)] + vm(4),
        out_specs=tuple(vm(4)),
        scratch_shapes=[
            pltpu.VMEM(WHOLE, BF16),
            pltpu.VMEM((T, D), F32),
            pltpu.VMEM((T, D), BF16),
            pltpu.VMEM((8, LANE), F32),
            pltpu.VMEM((8, LANE), F32),
            pltpu.VMEM((4, 4, 8, LANE), F32),
            pltpu.VMEM((T, D), BF16),
            pltpu.VMEM((10, 4, 4, 96, LANE), BF16),
            pltpu.SemaphoreType.DMA((copies,)),
            pltpu.SemaphoreType.DMA((copies,)),
            pltpu.SemaphoreType.DMA((10,)),
        ]
        + backward_scratch()
        + reduce_scratch()
        + reduce_scratch(),
        compiler_params=pltpu.CompilerParams(
            collective_id=1, has_side_effects=True, vmem_limit_bytes=63 * 1024 * 1024
        ),
        name="first_backward_and_reduce",
    )(s, gout, w, heads, idx, proj, scan, gain, conv, wide, d1, hgrad1, act0, act1, gin1)


def run_forward(s, w, heads, idx):
    return pl.pallas_call(
        forward,
        out_shape=(
            jax.ShapeDtypeStruct((T, D), BF16),
            jax.ShapeDtypeStruct((T, WIDE), F32),
            jax.ShapeDtypeStruct((T, DI), F32),
            jax.ShapeDtypeStruct((8, D), F32),
            jax.ShapeDtypeStruct((8, CHANNELS), F32),
            jax.ShapeDtypeStruct((8, DI), F32),
        ),
        in_specs=vm(4),
        out_specs=tuple(vm(6)),
        scratch_shapes=[pltpu.VMEM((T, CHANNELS), BF16), pltpu.VMEM((T, DI), BF16)],
        compiler_params=pltpu.CompilerParams(vmem_limit_bytes=56 * 1024 * 1024),
        name="second_forward",
    )(s, w, heads, idx)


def backward_scratch():
    return [
        pltpu.VMEM((T, CHANNELS), BF16),
        pltpu.VMEM((T, DI), BF16),
        pltpu.VMEM((T, DI), F32),
        pltpu.VMEM((T, WIDE), BF16),
        pltpu.VMEM((T, CHANNELS), F32),
        pltpu.VMEM((2, LANE, GROUP), F32),
        pltpu.VMEM((T, LANE), F32),
        pltpu.VMEM((SMALL, LANE), F32),
        pltpu.VMEM((256, LANE), F32),
        pltpu.VMEM((T, D), BF16),
        pltpu.VMEM((T, D), F32),
    ]


def run_backward(s, gout, w, heads, idx, proj, scan, gain, conv, wide):
    return pl.pallas_call(
        backward,
        out_shape=(
            jax.ShapeDtypeStruct((T, D), F32),
            jax.ShapeDtypeStruct((T, D), BF16),
            jax.ShapeDtypeStruct(WHOLE, BF16),
            jax.ShapeDtypeStruct((8, LANE), F32),
        ),
        in_specs=vm(10),
        out_specs=tuple(vm(4)),
        scratch_shapes=backward_scratch(),
        compiler_params=pltpu.CompilerParams(vmem_limit_bytes=56 * 1024 * 1024),
        name="second_backward",
    )(s, gout, w, heads, idx, proj, scan, gain, conv, wide)


def pack_shards(in_weight, out_weight, norm_gain, conv_weight, conv_bias, gated_gain):
    wide = jnp.pad(in_weight, ((0, 4), (0, WIDE - in_weight.shape[1])))
    wide = wide.reshape(16, 7, 2, 2, LANE).transpose(2, 1, 3, 0, 4)
    taps = jnp.pad(conv_weight, ((0, 0), (0, 4))).reshape(1, LANE)
    rest = (conv_bias, jnp.zeros((4,), BF16), norm_gain, jnp.zeros((20,), BF16), gated_gain, jnp.zeros((40,), BF16))
    small = jnp.concatenate([taps, jnp.concatenate(rest).reshape(1, LANE)], axis=0)
    wide = wide.at[1, 6, 1, 0:2].set(small).reshape(2, 7, 32, LANE)
    tall = jnp.pad(out_weight, ((0, 8), (0, 0))).reshape(32, 3, 2, LANE).transpose(2, 1, 0, 3)
    return jnp.concatenate([wide, tall], axis=1)


def body(
    block_input,
    out_grad,
    live_mask,
    norm_gain,
    in_weight,
    conv_weight,
    conv_bias,
    dt_bias,
    a_log,
    d_skip,
    gated_gain,
    out_weight,
):
    section = lax.axis_index("section")
    first = section == 0
    idx = owner_index()
    shard = pack_shards(
        in_weight[0], out_weight[0], norm_gain[0], conv_weight[0], conv_bias[0], gated_gain[0]
    )
    own_heads = jnp.pad(jnp.concatenate([dt_bias, a_log, d_skip], axis=0), ((0, 5), (0, LANE - HEADS)))
    stream0 = jnp.where(first, block_input[0, 0], block_input[1, 0])
    live = jnp.where(first, live_mask[0, 0], live_mask[1, 0]).astype(BF16)
    cotangent = jnp.where(first, out_grad[0, 0], out_grad[1, 0]) * live
    weight0, weight1, heads, act0, *saved0 = run_entry(stream0, shard, own_heads, idx)
    act1, *saved1 = run_forward(act0, weight1, heads[1], idx)
    grad1, low1, weight_grad1, head_grad1 = run_backward(
        act0, cotangent, weight1, heads[1], idx, *saved1
    )
    activations, input_grads, total, per_head = run_exit(
        stream0, low1, weight0, heads[0], idx, *saved0, weight_grad1, head_grad1, act0, act1, grad1
    )
    per_head = jnp.where(first, per_head[0:3, :HEADS], per_head[4:7, :HEADS])
    wide = total[:, :7].reshape(2, 7, 2, 16, LANE)[:, :, :, :12].transpose(3, 1, 0, 2, 4).reshape(12, WIDE)
    small = total[1, 6, 16:18]
    tall = total[:, 7:, :24].transpose(2, 1, 0, 3).reshape(24, D)
    return (
        activations[None, :, None],
        input_grads[None, :, None],
        small[1:2, 32:44],
        wide[None, :, : in_weight.shape[2]],
        small[0].reshape(1, 4, 32)[:, :, :28],
        small[1:2, 0:28],
        per_head[0:1],
        per_head[1:2],
        per_head[2:3],
        small[1:2, 64:88],
        tall[None],
    )


def solution(mesh):
    placed = (
        P(None, "dp", None, None),
        P(None, "dp", None, None),
        P(None, "dp"),
        P("section", "dp"),
        P("section", "dp", None),
        P("section", None, "dp"),
        P("section", "dp"),
        P("section", None),
        P("section", None),
        P("section", None),
        P("section", "dp"),
        P("section", "dp", None),
    )
    return jax.shard_map(
        body,
        mesh=mesh,
        in_specs=placed,
        out_specs=(
            P("section", None, "dp", None, None),
            P("section", None, "dp", None, None),
            P("section", "dp"),
            P("section", "dp", None),
            P("section", None, "dp"),
            P("section", "dp"),
            P("section", None),
            P("section", None),
            P("section", None),
            P("section", "dp"),
            P("section", "dp", None),
        ),
        check_vma=False,
    )
```

```python
import functools

import jax
import jax.numpy as jnp
import numpy as np
from jax import lax
from jax.experimental import pallas as pl
from jax.experimental.pallas import tpu as pltpu
from jax.sharding import PartitionSpec as P

F32 = jnp.float32
BF16 = jnp.bfloat16
MESH = pl.DeviceIdType.MESH
EPS = 1e-05
T = 256
GROUP = 128
LANE = 128
D = 768
DI = 1536
HEADS = 24
CHANNELS = 1792
WIDE = 3584
ROW_GAIN = 0
ROW_TAPS = 6
ROW_BIAS = 62
ROW_GATED = 76
SMALL = 88


def mm(a, b, dims, precision=None):
    return lax.dot_general(a, b, (dims, ((), ())), precision=precision, preferred_element_type=F32)


NN = ((1,), (0,))
NT = ((1,), (1,))
TN = ((0,), (0,))
EXACT = lax.Precision.HIGHEST


def chunk(j):
    return slice(LANE * j, LANE * (j + 1))


def in_pair(w_ref, j):
    left = w_ref[j // 2, j % 2, :, :, 0:48, :].reshape(D, LANE)
    right = w_ref[j // 2, j % 2, :, :, 48:96, :].reshape(D, LANE)
    return jnp.concatenate([left, right], axis=1)


def out_pair(w_ref, c):
    left = w_ref[7 + c // 2, 0].reshape(DI, LANE)
    right = w_ref[7 + c // 2, 1].reshape(DI, LANE)
    return jnp.concatenate([left, right], axis=1)


def lane_half():
    return lax.broadcasted_iota(jnp.int32, (1, LANE), 1) < 64


def lower_mask():
    rows = lax.broadcasted_iota(jnp.int32, (GROUP, GROUP), 0)
    cols = lax.broadcasted_iota(jnp.int32, (GROUP, GROUP), 1)
    return rows >= cols


def down(x, k):
    if k == 0:
        return x
    rows = lax.broadcasted_iota(jnp.int32, x.shape, 0)
    return jnp.where(rows >= k, pltpu.roll(x, k, 0), 0.0)


def up(x, k):
    if k == 0:
        return x
    rows = lax.broadcasted_iota(jnp.int32, x.shape, 0)
    return jnp.where(rows < T - k, pltpu.roll(x, T - k, 0), 0.0)


def sigmoid(x):
    return 1.0 / (1.0 + jnp.exp(-x))


def conv_of(proj_ref, conv_ref, j):
    x = proj_ref[:, DI + LANE * j : DI + LANE * (j + 1)]
    out = conv_ref[4:5, chunk(j)] + conv_ref[3:4, chunk(j)] * x
    for k in range(1, 4):
        out = out + conv_ref[3 - k : 4 - k, chunk(j)] * down(x, k)
    return x, out


def spread(cols, p):
    return jnp.where(lane_half(), cols[:, 2 * p : 2 * p + 1], cols[:, 2 * p + 1 : 2 * p + 2])


def steps_of(proj_ref, head_ref):
    raw = proj_ref[:, DI + CHANNELS : DI + CHANNELS + LANE] + head_ref[0:1, :]
    steps = jnp.maximum(raw, 0.0) + jnp.log1p(jnp.exp(-jnp.abs(raw)))
    rates = -steps * jnp.exp(head_ref[1:2, :])
    tri = lower_mask().astype(F32)
    cumul = [mm(tri, rates[GROUP * b : GROUP * (b + 1)], NN, EXACT) for b in range(2)]
    return raw, steps, rates, cumul


def forward_steps(s_ref, w_ref, head_ref, idx_ref, act_ref, proj_ref, scan_ref, gain_ref, conv_ref, wide_ref,
            mixed_ref, nout_ref):
    unpack_all(w_ref, idx_ref, head_ref, gain_ref, conv_ref, wide_ref)
    stream = s_ref[...].astype(F32)
    scale = lax.rsqrt(jnp.mean(stream * stream, axis=-1, keepdims=True) + EPS)
    normed = (stream * scale * gain_ref[0:1, :]).astype(BF16)
    for j in range(14):
        got = mm(normed, in_pair(w_ref, j), NN)
        proj_ref[:, 2 * LANE * j : 2 * LANE * (j + 1)] = got
        yield "in"
    for j in range(14):
        _, out = conv_of(proj_ref, conv_ref, j)
        mixed_ref[:, chunk(j)] = (out * sigmoid(out)).astype(BF16)
        yield "conv"
    _, steps, _, cumul = steps_of(proj_ref, head_ref)
    lower = lower_mask()
    half = lane_half()
    key = [mixed_ref[GROUP * b : GROUP * (b + 1), chunk(12)] for b in range(2)]
    query = [mixed_ref[GROUP * b : GROUP * (b + 1), chunk(13)] for b in range(2)]
    scores = [mm(query[b], key[b], NT) for b in range(2)]
    cross = mm(query[1], key[0], NT).astype(BF16)
    cumul_t = [c.T for c in cumul]
    total = jnp.zeros((T, 1), F32)
    for p in range(12):
        tail_u = None
        squares = []
        for b in range(2):
            rows = slice(GROUP * b, GROUP * (b + 1))
            x = mixed_ref[rows, chunk(p)].astype(F32)
            u = x * spread(steps[rows], p)
            weights = []
            for h in (2 * p, 2 * p + 1):
                gap = cumul[b][:, h : h + 1] - cumul_t[b][h : h + 1, :]
                weights.append((scores[b] * jnp.exp(jnp.where(lower, gap, -1e30))).astype(BF16))
            u_two = jnp.concatenate([jnp.where(half, u, 0.0), jnp.where(half, 0.0, u)], axis=0)
            y = mm(jnp.concatenate(weights, axis=1), u_two.astype(BF16), NN)
            cum = spread(cumul[b], p)
            if b == 0:
                tail_u = (jnp.exp(cum[GROUP - 1 : GROUP, :] - cum) * u).astype(BF16)
            else:
                y = y + jnp.exp(cum) * mm(cross, tail_u, NN)
            y = y + x * wide_ref[1:2, chunk(p)]
            scan_ref[rows, chunk(p)] = y
            z = proj_ref[rows, chunk(p)]
            gated = y * (z * sigmoid(z))
            squares.append(jnp.sum(gated * gated, axis=-1, keepdims=True))
        total = total + jnp.concatenate(squares, axis=0)
        yield "scan"
    scale_out = lax.rsqrt(total * (1.0 / DI) + EPS)
    for p in range(12):
        z = proj_ref[:, chunk(p)]
        gated = scan_ref[:, chunk(p)] * (z * sigmoid(z))
        nout_ref[:, chunk(p)] = (gated * scale_out * wide_ref[0:1, chunk(p)]).astype(BF16)
    yield "norm"
    for c in range(0, 6, 2):
        cols = slice(LANE * c, LANE * (c + 2))
        branch = mm(nout_ref[...], out_pair(w_ref, c), NN)
        act_ref[:, cols] = (s_ref[:, cols].astype(F32) + branch).astype(BF16)
        yield "branch"


def forward(s_ref, w_ref, heads_ref, *refs):
    for _ in forward_steps(s_ref, w_ref, heads_ref.at[1], *refs):
        pass


def fold(value, expand):
    high = value.astype(BF16)
    low = (value - high.astype(F32)).astype(BF16)
    return mm(high, expand, NN) + mm(low, expand, NN)


def backward_steps(s_ref, gout_ref, w_ref, head_ref, idx_ref, proj_ref, scan_ref, gain_ref, conv_ref, wide_ref,
             gin_ref, low_ref, d_ref, hgrad_ref,
             mixed_ref, nout_ref, gno_ref, gproj_ref, dmix_ref, dcum_ref, dstep_ref, small_ref, pack_ref, norm_ref, gnorm_ref):
    hgrad_ref[...] = jnp.zeros_like(hgrad_ref)
    skip_sum = jnp.zeros((1, LANE), F32)
    lower = lower_mask()
    half = lane_half()
    grad_branch = gout_ref[...]
    total = jnp.zeros((T, 1), F32)
    for p in range(12):
        z = proj_ref[:, chunk(p)]
        gated = scan_ref[:, chunk(p)] * (z * sigmoid(z))
        total = total + jnp.sum(gated * gated, axis=-1, keepdims=True)
        yield "square", None
    scale_out = lax.rsqrt(total * (1.0 / DI) + EPS)
    for c in range(0, 6, 2):
        part = mm(grad_branch[:, LANE * c : LANE * (c + 2)], out_pair(w_ref, c), NT)
        if c == 0:
            gno_ref[...] = part
        else:
            gno_ref[...] += part
    inner = jnp.zeros((T, 1), F32)
    for p in range(12):
        z = proj_ref[:, chunk(p)]
        gated = scan_ref[:, chunk(p)] * (z * sigmoid(z))
        unit = gated * scale_out
        gain = wide_ref[0:1, chunk(p)]
        nout_ref[:, chunk(p)] = (unit * gain).astype(BF16)
        gno = gno_ref[:, chunk(p)]
        small_ref[ROW_GATED + p : ROW_GATED + p + 1, :] = jnp.sum(gno * unit, axis=0, keepdims=True)
        inner = inner + jnp.sum(gno * gain * unit, axis=-1, keepdims=True)
        yield "inner", None
    inner = inner * (1.0 / DI)
    for c in range(0, 6, 2):
        grad = mm(nout_ref[...], grad_branch[:, LANE * c : LANE * (c + 2)], TN).astype(BF16)
        for e in range(2):
            d_ref[7 + c // 2, e] = grad[:, LANE * e : LANE * (e + 1)].reshape(4, 4, 96, LANE)
        yield "out", 7 + c // 2
    for p in range(12):
        z = proj_ref[:, chunk(p)]
        scan = scan_ref[:, chunk(p)]
        sig = sigmoid(z)
        silu = z * sig
        unit = scan * silu * scale_out
        ggated = scale_out * (gno_ref[:, chunk(p)] * wide_ref[0:1, chunk(p)] - unit * inner)
        gproj_ref[:, chunk(p)] = (ggated * scan * (sig + silu * (1.0 - sig))).astype(BF16)
        gno_ref[:, chunk(p)] = ggated * silu
        yield "gate", None
    stream = s_ref[...].astype(F32)
    scale = lax.rsqrt(jnp.mean(stream * stream, axis=-1, keepdims=True) + EPS)
    norm_ref[...] = (stream * scale * gain_ref[0:1, :]).astype(BF16)

    def in_grad(j):
        gp = gproj_ref[:, 2 * LANE * j : 2 * LANE * (j + 1)]
        grad = mm(norm_ref[...], gp, TN).astype(BF16)
        for e in range(1 if j == 13 else 2):
            part = grad[:, LANE * e : LANE * (e + 1)].reshape(4, 4, 48, LANE)
            d_ref[j // 2, j % 2, :, :, 48 * e : 48 * (e + 1), :] = part
        back = mm(gp, in_pair(w_ref, j), NT)
        if j == 0:
            gnorm_ref[...] = back
        else:
            gnorm_ref[...] += back

    for j in range(6):
        in_grad(j)
        yield "early", j // 2 if j % 2 else None
    for j in range(14):
        _, out = conv_of(proj_ref, conv_ref, j)
        mixed_ref[:, chunk(j)] = (out * sigmoid(out)).astype(BF16)
        yield "conv", None
    raw, steps, rates, cumul = steps_of(proj_ref, head_ref)
    key = [mixed_ref[GROUP * b : GROUP * (b + 1), chunk(12)] for b in range(2)]
    query = [mixed_ref[GROUP * b : GROUP * (b + 1), chunk(13)] for b in range(2)]
    scores = [mm(query[b], key[b], NT) for b in range(2)]
    cross = mm(query[1], key[0], NT).astype(BF16)
    cumul_t = [c.T for c in cumul]
    dscores = [jnp.zeros((GROUP, GROUP), F32) for _ in range(2)]
    dcross = jnp.zeros((GROUP, GROUP), F32)
    dcum_ref[...] = jnp.zeros_like(dcum_ref)
    dstep_ref[...] = jnp.zeros_like(dstep_ref)
    lanes = lax.broadcasted_iota(jnp.int32, (1, LANE), 1)
    head_row = lax.broadcasted_iota(jnp.int32, (LANE, LANE), 0)
    head_col = lax.broadcasted_iota(jnp.int32, (LANE, LANE), 1)
    row_sum = [jnp.zeros((GROUP, LANE), F32) for _ in range(2)]
    for p in range(12):
        expand = (head_col == 2 * p + jnp.where(head_row < 64, 0, 1)).astype(BF16)
        tail_u = eg = None
        us, xs, dus, step_es, grads = [], [], [], [], []
        tail = None
        for b in range(2):
            rows = slice(GROUP * b, GROUP * (b + 1))
            x = mixed_ref[rows, chunk(p)].astype(F32)
            step_e = spread(steps[rows], p)
            u = x * step_e
            g = gno_ref[rows, chunk(p)]
            g_two = jnp.concatenate([jnp.where(half, g, 0.0), jnp.where(half, 0.0, g)], axis=0)
            g_two = g_two.astype(BF16)
            value = mm(g_two, u.astype(BF16), NT)
            weights = []
            for e in range(2):
                h = 2 * p + e
                gap = cumul[b][:, h : h + 1] - cumul_t[b][h : h + 1, :]
                decay = jnp.exp(jnp.where(lower, gap, -1e30))
                weight = scores[b] * decay
                weights.append(weight.astype(BF16))
                v = value[GROUP * e : GROUP * (e + 1)]
                dscores[b] = dscores[b] + v * decay
                both = v * weight
                row_sum[b] = jnp.where(lanes == h, jnp.sum(both, axis=-1, keepdims=True), row_sum[b])
                dcum_ref[b, h : h + 1, :] = -jnp.sum(both, axis=0, keepdims=True)
            du = mm(jnp.concatenate(weights, axis=0), g_two, TN)
            us.append(u)
            xs.append(x)
            dus.append(du)
            step_es.append(step_e)
            grads.append(g)
            cum = spread(cumul[b], p)
            if b == 0:
                tail = jnp.exp(cum[GROUP - 1 : GROUP, :] - cum)
                tail_u = tail * u
            else:
                eg = jnp.exp(cum) * g
        tail_low = tail_u.astype(BF16)
        eg_low = eg.astype(BF16)
        dtail = mm(cross, eg_low, TN)
        dcross = dcross + mm(eg_low, tail_low, NT)
        dus[0] = dus[0] + tail * dtail
        column = fold(tail_u * dtail, expand)
        row_sum[0] = row_sum[0] - column
        row_sum[0] = row_sum[0] + jnp.where(
            lax.broadcasted_iota(jnp.int32, (GROUP, 1), 0) == GROUP - 1,
            jnp.sum(column, axis=0, keepdims=True), 0.0)
        row_sum[1] = row_sum[1] + fold(eg * mm(cross, tail_low, NN), expand)
        skip = jnp.zeros((1, LANE), F32)
        for b in range(2):
            rows = slice(GROUP * b, GROUP * (b + 1))
            dstep_ref[rows, :] += fold(dus[b] * xs[b], expand)
            dmix_ref[rows, chunk(p)] = step_es[b] * dus[b] + grads[b] * wide_ref[1:2, chunk(p)]
            skip = skip + jnp.sum(grads[b] * xs[b], axis=0, keepdims=True)
        yield "scan", None
        skip_sum = skip_sum + fold(jnp.broadcast_to(skip, (8, LANE)), expand)[0:1]
    dcross_low = dcross.astype(BF16)
    ds_low = [d.astype(BF16) for d in dscores]
    dmix_ref[0:GROUP, chunk(12)] = mm(ds_low[0], query[0], TN) + mm(dcross_low, query[1], TN)
    dmix_ref[GROUP:T, chunk(12)] = mm(ds_low[1], query[1], TN)
    dmix_ref[0:GROUP, chunk(13)] = mm(ds_low[0], key[0], NN)
    dmix_ref[GROUP:T, chunk(13)] = mm(ds_low[1], key[1], NN) + mm(dcross_low, key[0], NN)
    tri = lower.astype(F32)
    decay_rate = jnp.exp(head_ref[1:2, :])
    step_sum = jnp.zeros((1, LANE), F32)
    decay_sum = jnp.zeros((1, LANE), F32)
    for b in range(2):
        rows = slice(GROUP * b, GROUP * (b + 1))
        drate = mm(tri, row_sum[b] + dcum_ref[b].T, TN, EXACT)
        draw = (dstep_ref[rows, :] - decay_rate * drate) * sigmoid(raw[rows])
        draw = jnp.where(lanes < HEADS, draw, 0.0)
        decay_sum = decay_sum + jnp.sum(drate * rates[rows], axis=0, keepdims=True)
        step_sum = step_sum + jnp.sum(draw, axis=0, keepdims=True)
        gproj_ref[rows, DI + CHANNELS : DI + CHANNELS + LANE] = draw.astype(BF16)
    hgrad_ref[0:1, :] = step_sum
    hgrad_ref[1:2, :] = decay_sum
    hgrad_ref[2:3, :] = skip_sum
    gproj_ref[:, WIDE - LANE :] = jnp.zeros((T, LANE), BF16)
    for j in range(14):
        x, out = conv_of(proj_ref, conv_ref, j)
        sig = sigmoid(out)
        dconv = dmix_ref[:, chunk(j)] * (sig + out * sig * (1.0 - sig))
        small_ref[ROW_BIAS + j : ROW_BIAS + j + 1, :] = jnp.sum(dconv, axis=0, keepdims=True)
        dx = conv_ref[3:4, chunk(j)] * dconv
        for k in range(4):
            row = ROW_TAPS + 14 * (3 - k) + j
            small_ref[row : row + 1, :] = jnp.sum(dconv * down(x, k), axis=0, keepdims=True)
            if k:
                dx = dx + conv_ref[3 - k : 4 - k, chunk(j)] * up(dconv, k)
        gproj_ref[:, DI + LANE * j : DI + LANE * (j + 1)] = dx.astype(BF16)
        yield "taps", None
    for j in (6, 7, 8, 9, 10, 11, 13, 12):
        in_grad(j)
        yield "late", j // 2 if j % 2 and j < 12 else None
    gnormed = gnorm_ref[...]
    unit = stream * scale
    gain_grad = jnp.sum(gnormed * unit, axis=0, keepdims=True)
    for c in range(6):
        small_ref[ROW_GAIN + c : ROW_GAIN + c + 1, :] = gain_grad[:, chunk(c)]
    pack_all(small_ref, idx_ref, pack_ref)
    d_ref[6, 1, :, :, 48:64, :] = pack_ref[...].astype(BF16).reshape(4, 4, 16, LANE)
    d_ref[6, 1, :, :, 64:96, :] = jnp.zeros((4, 4, 32, LANE), BF16)
    yield "pack", 6
    gunit = gnormed * gain_ref[0:1, :]
    center = jnp.mean(gunit * unit, axis=-1, keepdims=True)
    gin = gout_ref[...].astype(F32) + scale * (gunit - unit * center)
    gin_ref[...] = gin
    low_ref[...] = gin.astype(BF16)
    yield "done", None


def backward(s_ref, grad_ref, live_ref, w_ref, heads_ref, *refs):
    *refs, gout_ref, local = refs
    section = lax.axis_index("section")
    fetch = pltpu.make_async_copy(grad_ref.at[section, 0], gout_ref, local.at[0])
    fetch.start()
    live = jnp.where(section == 0, live_ref[0:1, :], live_ref[1:2, :]).astype(F32)
    fetch.wait()
    gout_ref[...] = (gout_ref[...].astype(F32) * live).astype(BF16)
    for _ in backward_steps(s_ref, gout_ref, w_ref, heads_ref.at[1], *refs):
        pass


KINDS = (
    (2, 12, ROW_GAIN, 6, 32, 1),
    (0, 28, ROW_TAPS, 14, 0, 0),
    (0, 28, ROW_TAPS + 14, 14, 32, 0),
    (0, 28, ROW_TAPS + 28, 14, 64, 0),
    (0, 28, ROW_TAPS + 42, 14, 96, 0),
    (0, 28, ROW_BIAS, 14, 0, 1),
    (4, 24, ROW_GATED, 12, 64, 1),
)


def owner_index():
    table = np.zeros((8, CHANNELS), np.int32)
    for row, width, length in ((0, 28, CHANNELS), (2, 12, D), (4, 24, DI)):
        position = np.arange(length)
        owner = position // width
        table[row, :length] = 16 * (owner // 4) + 2 * (owner % 4)
        table[row + 1, :length] = position % width
    return jnp.asarray(table)


def window(width, c):
    first, last = LANE * c // width, (LANE * c + LANE - 1) // width
    return 16 * (first // 4), 16 * (last // 4) + 16


def unpack(pack, idx_ref, kind, c):
    row, width, _, _, lane, line = kind
    low, high = window(width, c)
    lanes = lax.broadcasted_iota(jnp.int32, (LANE, LANE), 0)
    pick = (lanes == idx_ref[row + 1 : row + 2, chunk(c)] + lane).astype(BF16)
    rows = lax.broadcasted_iota(jnp.int32, (high - low, LANE), 0) + low
    got = mm(pack[low:high], pick, NN)
    return jnp.sum(jnp.where(rows == idx_ref[row : row + 1, chunk(c)] + line, got, 0.0), axis=0, keepdims=True)


def unpack_all(w_ref, idx_ref, head_ref, gain_ref, conv_ref, wide_ref):
    pack = w_ref[6, 1, :, :, 48:64, :].reshape(256, LANE)
    for c in range(6):
        gain_ref[0:1, chunk(c)] = unpack(pack, idx_ref, KINDS[0], c)
    for k in range(5):
        for c in range(14):
            conv_ref[k : k + 1, chunk(c)] = unpack(pack, idx_ref, KINDS[1 + k], c)
    for c in range(12):
        wide_ref[0:1, chunk(c)] = unpack(pack, idx_ref, KINDS[6], c)
        wide_ref[1:2, chunk(c)] = spread(head_ref[2:3, :], c)


def pack_all(small_ref, idx_ref, pack_ref):
    pack_ref[...] = jnp.zeros_like(pack_ref)
    for kind in KINDS:
        row, width, start, count, lane, line = kind
        for c in range(count):
            low, high = window(width, c)
            lanes = lax.broadcasted_iota(jnp.int32, (LANE, LANE), 0)
            pick = (lanes == idx_ref[row + 1 : row + 2, chunk(c)] + lane).astype(BF16)
            rows = lax.broadcasted_iota(jnp.int32, (high - low, LANE), 0) + low
            value = small_ref[start + c : start + c + 1, :]
            held = jnp.where(rows == idx_ref[row : row + 1, chunk(c)] + line, value, 0.0).astype(BF16)
            pack_ref[low:high, :] += mm(held, pick, NT)


def vm(count):
    return [pl.BlockSpec(memory_space=pltpu.VMEM)] * count


class Sems:
    def __init__(self, send, recv):
        self.send, self.recv, self.used = send, recv, 0

    def take(self):
        index = self.used
        self.used += 1
        return self.send.at[index], self.recv.at[index]


class Place:
    def __init__(self):
        self.section = lax.axis_index("section")
        self.dp = lax.axis_index("dp")
        self.z = lax.div(self.dp, 16)
        self.x = lax.rem(lax.div(self.dp, 4), 4)
        self.q = lax.rem(self.dp, 4)
        self.core = lax.rem(self.dp, 2)
        self.column = self.dp - self.q

    def at(self, z, x):
        return (self.section, 16 * z + 4 * x + self.q)

    def along(self, axis, distance):
        if axis == "z":
            return self.at(lax.rem(self.z + distance, 4), self.x)
        return self.at(self.z, lax.rem(self.x + distance, 4))

    def sibling(self):
        return (self.section, self.dp + 1 - 2 * self.core)

    def in_column(self, section, q):
        return (section, self.column + q)


def greet(place):
    barrier = pltpu.get_barrier_semaphore()
    peers = [place.in_column(place.section, lax.rem(place.q + r, 4)) for r in range(1, 4)]
    peers += [place.in_column(1 - place.section, lax.rem(place.q + r, 4)) for r in range(4)]
    peers += [place.along(axis, r) for axis in "zx" for r in range(1, 4)]
    for peer in peers:
        pl.semaphore_signal(barrier, inc=1, device_id=peer, device_id_type=MESH)
    pl.semaphore_wait(barrier, len(peers))


def push(src, dst, sems, device):
    send, recv = sems
    return pltpu.make_async_remote_copy(
        src_ref=src, dst_ref=dst, send_sem=send, recv_sem=recv, device_id=device, device_id_type=MESH
    )


PAIRS = range(10)
AXES = ("xz", "zx", "xz", "zx", "xz", "zx", "xz", "zx", "xz", "zx")
SHARD = (10, 32, LANE)
WHOLE = (10, 2, 4, 4, 96, LANE)


class Copies:
    def __init__(self, place, sems):
        self.place, self.sems, self.sent = place, sems, []

    def start(self, src, dst, device):
        copy = push(src, dst, self.sems.take(), device)
        copy.start()
        self.sent.append(copy)
        return copy

    def end(self):
        for copy in self.sent:
            copy.wait_send()


def coord(place, axis, distance):
    return lax.rem((place.z if axis == "z" else place.x) + distance, 4)


def column_copies(place, layer, sems, source, landing):
    copies = {}
    for other in (0, 1):
        for r in range(4):
            if other == 0 and r == 0:
                continue
            target = lax.rem(place.q + r, 4)
            section = layer if other == 0 else 1 - layer
            copies[other, r] = push(
                source(target), landing, sems.take(), place.in_column(section, target)
            )
    return copies


def gather_steps(layer, place, sems, local, shard_ref, w_ref, slabs, whole, own):
    run = Copies(place, sems)
    core = place.core
    copies = column_copies(place, layer, sems, lambda q: shard_ref.at[lax.rem(q, 2)], slabs.at[place.q])
    mine = pltpu.make_async_copy(shard_ref.at[core], slabs.at[place.q], local.at[0])

    @pl.when(place.section == layer)
    def _():
        for copy in copies.values():
            copy.start()
        mine.start()

    yield "column"

    @pl.when(place.section == layer)
    def _():
        mine.wait()
        for r in range(1, 4):
            copies[0, r].wait_recv()

    @pl.when(place.section != layer)
    def _():
        for r in range(4):
            copies[1, r].wait_recv()

    whole[...] = jnp.zeros_like(whole)
    for q in range(4):
        part = slabs[q].astype(F32)
        whole[0:7, 12 * q : 12 * q + 12, :] = part[0:7, 0:12]
        whole[0:6, 48 + 12 * q : 60 + 12 * q, :] = part[0:6, 16:28]

        @pl.when(core == 0)
        def _():
            whole[6, 48 + 12 * q : 60 + 12 * q, :] = part[6, 16:28]

        @pl.when(core == 1)
        def _():
            whole[6, 48 + 2 * q : 50 + 2 * q, :] = part[6, 16:18]

        whole[7:10, 24 * q : 24 * q + 24, :] = part[7:10, 0:24]
    own[...] = whole[...].astype(BF16)
    keep = pltpu.make_async_copy(own, w_ref.at[:, core, place.z, place.x], local.at[1])
    keep.start()
    first, second, third = {}, {}, {}
    for i in PAIRS:
        there = w_ref.at[i, core, place.z, place.x]
        axis = AXES[i][0]
        first[i] = [run.start(own.at[i], there, place.along(axis, r)) for r in (1, 3, 2)]

    def line(i, distance, rows=None):
        axis = AXES[i][1]
        at = coord(place, axis, distance)
        z, x = (at, pl.ds(0, 4)) if axis == "z" else (pl.ds(0, 4), at)
        if rows is None:
            return w_ref.at[i, core, z, x]
        return w_ref.at[i, core, z, x, pl.ds(rows, 48)]

    for i in PAIRS:
        yield "first"
        if i == 0:
            keep.wait()
        for copy in first[i]:
            copy.wait_recv()
        src = line(i, 0)
        second[i] = [run.start(src, src, place.along(AXES[i][1], r)) for r in (1, 3)]
    for i in PAIRS:
        yield "second"
        second[i][0].wait_recv()
        got = line(i, 3, 0)
        one = run.start(got, got, place.along(AXES[i][1], 1))
        second[i][1].wait_recv()
        got = line(i, 1, 48)
        two = run.start(got, got, place.along(AXES[i][1], 3))
        third[i] = (one, two)
    over = {}
    for i in PAIRS:
        yield "third"
        for copy in third[i]:
            copy.wait_recv()
        half = w_ref.at[i, core]
        over[i] = run.start(half, half, place.sibling())
    for i in PAIRS:
        yield "over"
        over[i].wait_recv()
    yield "whole"
    run.end()

    @pl.when(place.section == layer)
    def _():
        for copy in copies.values():
            copy.wait_send()


GATHER_COPIES = 7 + 8 * 10


def gather_scratch():
    return [
        pltpu.VMEM((4,) + SHARD, BF16),
        pltpu.VMEM((10, 96, LANE), F32),
        pltpu.VMEM((10, 96, LANE), BF16),
        pltpu.SemaphoreType.DMA((2,)),
    ]


def go(steps, count):
    for _ in range(count):
        next(steps, None)


def build_shard(in_ref, out_ref, taps_ref, bias_ref, gain_ref, gated_ref, shard_ref):
    shard_ref[...] = jnp.zeros_like(shard_ref)
    for u in range(27):
        pair, side = u // 2, u % 2
        width = min(LANE, in_ref.shape[2] - LANE * u)
        part = in_ref[0, :, LANE * u : LANE * u + width]
        shard_ref[pair % 2, pair // 2, 16 * side : 16 * side + 12, 0:width] = part
    for c in range(6):
        shard_ref[c % 2, 7 + c // 2, 0:24, :] = out_ref[0, :, chunk(c)]

    def shift(value, start):
        rows = lax.broadcasted_iota(jnp.int32, (value.shape[1], LANE), 0)
        lanes = lax.broadcasted_iota(jnp.int32, (value.shape[1], LANE), 1)
        return mm(value.astype(F32), (lanes == rows + start).astype(F32), NN)

    taps = shift(taps_ref[0, 0:1, :], 0)
    for k in range(1, 4):
        taps = taps + shift(taps_ref[0, k : k + 1, :], 32 * k)
    rest = shift(bias_ref[...], 0) + shift(gain_ref[...], 32) + shift(gated_ref[...], 64)
    small = jnp.concatenate([taps, rest, jnp.zeros((14, LANE), F32)], axis=0)
    shard_ref[1, 6, 16:32, :] = small.astype(BF16)


def entry_kernel(block_ref, in_ref, out_ref, taps_ref, bias_ref, gain_in_ref, gated_ref, step_ref, decay_ref,
                 skip_ref, idx_ref, w0_ref, w1_ref, heads_ref, act_ref, proj_ref, scan_ref,
                 gain_ref, conv_ref, wide_ref, s_ref, shard_ref, head_ref, w_here, mixed, nout,
                 send, recv, local, *scratch):
    place = Place()
    stream = pltpu.make_async_copy(block_ref.at[place.section, 0], s_ref, local.at[1])
    stream.start()
    build_shard(in_ref, out_ref, taps_ref, bias_ref, gain_in_ref, gated_ref, shard_ref)
    head_ref[...] = jnp.zeros_like(head_ref)
    head_ref[0:1, 0:HEADS] = step_ref[...]
    head_ref[1:2, 0:HEADS] = decay_ref[...]
    head_ref[2:3, 0:HEADS] = skip_ref[...]
    greet(place)
    sems = Sems(send, recv)
    partner = place.in_column(1 - place.section, place.q)
    swap = push(head_ref, heads_ref.at[place.section], sems.take(), partner)
    swap.start()
    heads_ref[place.section] = head_ref[...]
    zero = gather_steps(0, place, sems, scratch[3], shard_ref, w_here, *scratch[0:3])
    one = gather_steps(1, place, sems, scratch[7], shard_ref, w1_ref, *scratch[4:7])
    go(zero, 1)
    go(one, 1)
    go(zero, 21)
    go(one, 1)
    go(zero, 10)
    go(one, 10)
    go(zero, 7)
    swap.wait()
    stream.wait()
    work = forward_steps(s_ref, w_here, heads_ref.at[0], idx_ref, act_ref, proj_ref, scan_ref,
                         gain_ref, conv_ref, wide_ref, mixed, nout)
    saved = pltpu.make_async_copy(w_here, w0_ref, local.at[0])
    for count, what in enumerate(work):
        if count in (8, 10, 12):
            go(zero, 1)
        if count == 12:
            saved.start()
        if what in ("conv", "scan", "branch"):
            go(one, 1)
    for _ in one:
        pass
    go(zero, 1)
    saved.wait()


def run_entry(*given):
    copies = 1 + 2 * GATHER_COPIES
    return pl.pallas_call(
        entry_kernel,
        out_shape=(
            jax.ShapeDtypeStruct(WHOLE, BF16),
            jax.ShapeDtypeStruct(WHOLE, BF16),
            jax.ShapeDtypeStruct((2, 8, LANE), F32),
            jax.ShapeDtypeStruct((T, D), BF16),
            jax.ShapeDtypeStruct((T, WIDE), F32),
            jax.ShapeDtypeStruct((T, DI), F32),
            jax.ShapeDtypeStruct((8, D), F32),
            jax.ShapeDtypeStruct((8, CHANNELS), F32),
            jax.ShapeDtypeStruct((8, DI), F32),
        ),
        in_specs=[pl.BlockSpec(memory_space=pl.ANY)] + vm(10),
        out_specs=tuple([pl.BlockSpec(memory_space=pl.ANY)] * 2 + vm(7)),
        scratch_shapes=[
            pltpu.VMEM((T, D), BF16),
            pltpu.VMEM((2,) + SHARD, BF16),
            pltpu.VMEM((8, LANE), F32),
            pltpu.VMEM(WHOLE, BF16),
            pltpu.VMEM((T, CHANNELS), BF16),
            pltpu.VMEM((T, DI), BF16),
            pltpu.SemaphoreType.DMA((copies,)),
            pltpu.SemaphoreType.DMA((copies,)),
            pltpu.SemaphoreType.DMA((2,)),
        ]
        + gather_scratch()
        + gather_scratch(),
        compiler_params=pltpu.CompilerParams(
            collective_id=0, has_side_effects=True, vmem_limit_bytes=56 * 1024 * 1024
        ),
        name="gather_and_first_forward",
    )(*given)


ORDER = (7, 8, 9, 0, 1, 2, 3, 4, 5, 6)


class Reduce:
    def __init__(self, layer, place, sems, local, d_ref, mine_ref, g_ref, bufs):
        self.layer, self.place, self.local = layer, place, local
        self.d, self.mine, self.g = d_ref, mine_ref, g_ref
        self.acc, self.early, self.late, self.last, self.whole, self.rows, self.slabs, self.landed = bufs
        self.sems, self.run = sems, Copies(place, sems)
        self.crossing, self.kept, self.first, self.second, self.third = {}, {}, {}, {}, {}

    def line(self, i, distance, rows=None):
        axis = AXES[i][1]
        at = coord(self.place, axis, distance)
        z, x = (at, pl.ds(0, 4)) if axis == "z" else (pl.ds(0, 4), at)
        return (i, z, x) if rows is None else (i, z, x, pl.ds(rows, 48))

    def cross(self, i):
        core = self.place.core
        self.crossing[i] = self.run.start(self.d.at[i, 1 - core], self.acc.at[i], self.place.sibling())
        if self.mine is not None:
            self.kept[i] = pltpu.make_async_copy(self.d.at[i, core], self.mine.at[i], self.local.at[i])
            self.kept[i].start()

    def add(self, i):
        if self.mine is not None:
            self.kept[i].wait()
            own = self.mine[i]
        else:
            own = self.d[i, self.place.core]
        self.crossing[i].wait_recv()
        self.acc[i] = self.acc[i] + own
        axis = AXES[i][1]
        self.first[i] = (
            self.run.start(self.acc.at[self.line(i, 2, 0)], self.early.at[i, 0], self.place.along(axis, 1)),
            self.run.start(self.acc.at[self.line(i, 2, 48)], self.early.at[i, 1], self.place.along(axis, 3)),
        )

    def near(self, i):
        axis = AXES[i][1]
        copies = []
        for side, (distance, rows) in enumerate(((1, 0), (3, 48))):
            self.first[i][side].wait_recv()
            at = self.line(i, distance, rows)
            self.acc[at] = self.acc[at] + self.early[i, side]
            copies.append(
                self.run.start(self.acc.at[self.line(i, distance)], self.late.at[i, side],
                               self.place.along(axis, distance))
            )
        self.second[i] = copies

    def across(self, i):
        for copy in self.second[i]:
            copy.wait_recv()
        at = self.line(i, 0)
        total = self.acc[at].astype(F32) + self.late[i, 0].astype(F32) + self.late[i, 1].astype(F32)
        self.acc[at] = total.astype(BF16)
        axis = AXES[i][0]
        place = self.place
        copies = []
        for r in (1, 3, 2):
            to = coord(place, axis, r)
            z, x = (to, place.x) if axis == "z" else (place.z, to)
            copies.append(self.run.start(self.acc.at[i, z, x], self.last.at[i, r - 1], place.along(axis, r)))
        self.third[i] = copies

    def total(self, i):
        for copy in self.third[i]:
            copy.wait_recv()
        own = self.acc[i, self.place.z, self.place.x].astype(F32)
        for r in range(3):
            own = own + self.last[i, r].astype(F32)
        self.whole[i] = own

    def hand(self):
        place, layer, whole, slabs, rows = self.place, self.layer, self.whole, self.slabs, self.rows
        rows[...] = jnp.zeros_like(rows)
        for q in range(4):
            rows[0:7, 0:12, :] = whole[0:7, 12 * q : 12 * q + 12, :]
            rows[0:6, 12:24, :] = whole[0:6, 48 + 12 * q : 60 + 12 * q, :]

            @pl.when(place.core == 0)
            def _():
                rows[6, 12:24, :] = whole[6, 48 + 12 * q : 60 + 12 * q, :]

            @pl.when(place.core == 1)
            def _():
                rows[6, 12:14, :] = whole[6, 48 + 2 * q : 50 + 2 * q, :]

            rows[7:10, 0:24, :] = whole[7:10, 24 * q : 24 * q + 24, :]
            slabs[q] = rows[...].reshape(240, LANE).astype(BF16)
        slot = 4 * place.section + place.q
        copies = {}
        for other in (0, 1):
            for r in range(4):
                if other == 0 and r == 0:
                    continue
                target = lax.rem(place.q + r, 4)
                copies[other, r] = push(
                    slabs.at[target], self.landed.at[slot], self.sems.take(), place.in_column(layer, target)
                )

        @pl.when(place.section == layer)
        def _():
            for r in range(1, 4):
                copies[0, r].start()
            self.landed[slot] = slabs[place.q]

        @pl.when(place.section != layer)
        def _():
            for r in range(4):
                copies[1, r].start()

        self.copies = copies

    def finish(self):
        place, copies, landed = self.place, self.copies, self.landed

        @pl.when(place.section == self.layer)
        def _():
            for copy in copies.values():
                copy.wait_recv()
            for core in range(2):
                parts = [landed[2 * y + core].astype(F32) for y in range(4)]
                self.g[core] = (parts[0] + parts[1] + parts[2] + parts[3]).reshape(10, 24, LANE)
            for r in range(1, 4):
                copies[0, r].wait_send()

        @pl.when(place.section != self.layer)
        def _():
            for r in range(4):
                copies[1, r].wait_send()

        self.run.end()


REDUCE_COPIES = 8 * 10 + 7


def reduce_scratch():
    return [
        pltpu.VMEM((10, 4, 4, 96, LANE), BF16),
        pltpu.VMEM((10, 2, 4, 48, LANE), BF16),
        pltpu.VMEM((10, 2, 4, 96, LANE), BF16),
        pltpu.VMEM((10, 3, 96, LANE), BF16),
        pltpu.VMEM((10, 96, LANE), F32),
        pltpu.VMEM((10, 24, LANE), F32),
        pltpu.VMEM((4, 240, LANE), BF16),
        pltpu.VMEM((8, 240, LANE), BF16),
    ]


def head_steps(place, sems, hval, head_out_ref, hbuf):
    y = 2 * place.section + lax.div(place.q, 2)
    for index, axis in enumerate(("core", "y", "x", "z")):
        copies = []
        if axis == "core":
            mine, peers = place.core, [place.sibling()]
        elif axis == "y":
            mine, peers = y, []
            for r in range(1, 4):
                to = lax.rem(y + r, 4)
                peers.append((lax.div(to, 2), place.column + 2 * lax.rem(to, 2) + place.core))
        else:
            mine = place.z if axis == "z" else place.x
            peers = [place.along(axis, r) for r in range(1, 4)]
        for peer in peers:
            copy = push(hval, hbuf.at[index, mine], sems.take(), peer)
            copy.start()
            copies.append(copy)
        hbuf[index, mine] = hval[...]
        yield
        for copy in copies:
            copy.wait_recv()
        for copy in copies:
            copy.wait_send()
        total = hbuf[index, 0] + hbuf[index, 1]
        if axis != "core":
            total = total + hbuf[index, 2] + hbuf[index, 3]
        hval[...] = total
    head_out_ref[...] = hval[...]


def exit_kernel(block_ref, gout_ref, w_ref, heads_ref, idx_ref, proj_ref, scan_ref, gain_ref, conv_ref, wide_ref,
                d1_ref, hgrad1_ref, act0_ref, act1_ref, gin1_ref,
                acts_ref, grads_ref, g_ref, head_out_ref,
                s_ref, d_ref, gin_ref, low_ref, hgrad_ref, hval, hbuf, back_in, mine, send, recv, local, *scratch):
    work_refs, scratch = scratch[:11], scratch[11:]
    place = Place()
    stream = pltpu.make_async_copy(block_ref.at[place.section, 0], s_ref, local.at[10])
    stream.start()
    head_ref = heads_ref.at[0]
    greet(place)
    sems = Sems(send, recv)
    one = Reduce(1, place, sems, local, d1_ref, mine, g_ref, scratch[0:8])
    zero = Reduce(0, place, sems, local, d_ref, None, g_ref, scratch[8:16])
    first = place.section == 0
    partner = place.in_column(1 - place.section, place.q)
    for i in ORDER:
        one.cross(i)
    act_out = [push(ref, acts_ref.at[place.section], pair, partner)
               for pair in (sems.take(),) for ref in (act1_ref, act0_ref)]
    back_out = [push(ref, back_in, pair, partner) for pair in (sems.take(),) for ref in (gout_ref, low_ref)]

    @pl.when(first)
    def _():
        act_out[0].start()
        back_out[0].start()
        acts_ref[0] = act0_ref[...]

    @pl.when(place.section == 1)
    def _():
        act_out[1].start()
        acts_ref[1] = act1_ref[...]
        grads_ref[1] = gin1_ref[...]

    stream.wait()
    work = backward_steps(s_ref, gout_ref, w_ref, head_ref, idx_ref, proj_ref, scan_ref, gain_ref, conv_ref,
                          wide_ref, gin_ref, low_ref, d_ref, hgrad_ref, *work_refs)
    plan = {
        "inner": (12, [(one.add, i) for i in ORDER[:5]]),
        "gate": (12, [(one.add, i) for i in ORDER[5:]]),
        "conv": (14, [(one.near, i) for i in ORDER]),
        "scan": (12, [(zero.add, i) for i in ORDER[:6]]),
        "taps": (14, [(one.across, i) for i in ORDER]),
        "late": (8, [(zero.near, i) for i in ORDER[:6]]),
    }
    seen = {}
    for phase, ready in work:
        if ready is not None:
            zero.cross(ready)
        if phase in plan:
            length, actions = plan[phase]
            at = seen.get(phase, 0)
            seen[phase] = at + 1
            for step, i in actions[at * len(actions) // length : (at + 1) * len(actions) // length]:
                step(i)
    hval[...] = jnp.zeros_like(hval)
    hval[0:4, :] = hgrad_ref[0:4, :]
    hval[4:8, :] = hgrad1_ref[0:4, :]
    small = head_steps(place, sems, hval, head_out_ref, hbuf)
    go(small, 1)

    @pl.when(place.section == 1)
    def _():
        back_out[1].start()

    @pl.when(first)
    def _():
        grads_ref[0] = gin_ref[...]

    for i in ORDER[6:]:
        zero.add(i)
    for i in ORDER:
        one.total(i)
    one.hand()
    go(small, 1)
    for i in ORDER[6:]:
        zero.near(i)
    go(small, 1)
    for i in ORDER:
        zero.across(i)
    go(small, 1)
    one.finish()
    for i in ORDER:
        zero.total(i)
    go(small, 1)
    zero.hand()
    act_out[0].wait()
    back_out[0].wait()

    @pl.when(first)
    def _():
        grads_ref[1] = back_in[...].astype(F32)

    @pl.when(place.section == 1)
    def _():
        grads_ref[0] = back_in[...].astype(F32)

    zero.finish()


def run_exit(block, gout, w, heads, idx, proj, scan, gain, conv, wide, d1, hgrad1, act0, act1, gin1):
    copies = 2 * REDUCE_COPIES + 10 + 2
    return pl.pallas_call(
        exit_kernel,
        out_shape=(
            jax.ShapeDtypeStruct((2, T, D), BF16),
            jax.ShapeDtypeStruct((2, T, D), F32),
            jax.ShapeDtypeStruct((2, 10, 24, LANE), F32),
            jax.ShapeDtypeStruct((8, LANE), F32),
        ),
        in_specs=[pl.BlockSpec(memory_space=pl.ANY)] + vm(9) + [pl.BlockSpec(memory_space=pl.ANY)] + vm(4),
        out_specs=tuple(vm(4)),
        scratch_shapes=[
            pltpu.VMEM((T, D), BF16),
            pltpu.VMEM(WHOLE, BF16),
            pltpu.VMEM((T, D), F32),
            pltpu.VMEM((T, D), BF16),
            pltpu.VMEM((8, LANE), F32),
            pltpu.VMEM((8, LANE), F32),
            pltpu.VMEM((4, 4, 8, LANE), F32),
            pltpu.VMEM((T, D), BF16),
            pltpu.VMEM((10, 4, 4, 96, LANE), BF16),
            pltpu.SemaphoreType.DMA((copies,)),
            pltpu.SemaphoreType.DMA((copies,)),
            pltpu.SemaphoreType.DMA((11,)),
        ]
        + backward_scratch()
        + reduce_scratch()
        + reduce_scratch(),
        compiler_params=pltpu.CompilerParams(
            collective_id=1, has_side_effects=True, vmem_limit_bytes=63 * 1024 * 1024
        ),
        name="first_backward_and_reduce",
    )(block, gout, w, heads, idx, proj, scan, gain, conv, wide, d1, hgrad1, act0, act1, gin1)


def run_forward(s, w, heads, idx):
    return pl.pallas_call(
        forward,
        out_shape=(
            jax.ShapeDtypeStruct((T, D), BF16),
            jax.ShapeDtypeStruct((T, WIDE), F32),
            jax.ShapeDtypeStruct((T, DI), F32),
            jax.ShapeDtypeStruct((8, D), F32),
            jax.ShapeDtypeStruct((8, CHANNELS), F32),
            jax.ShapeDtypeStruct((8, DI), F32),
        ),
        in_specs=vm(4),
        out_specs=tuple(vm(6)),
        scratch_shapes=[pltpu.VMEM((T, CHANNELS), BF16), pltpu.VMEM((T, DI), BF16)],
        compiler_params=pltpu.CompilerParams(vmem_limit_bytes=56 * 1024 * 1024),
        name="second_forward",
    )(s, w, heads, idx)


def backward_scratch():
    return [
        pltpu.VMEM((T, CHANNELS), BF16),
        pltpu.VMEM((T, DI), BF16),
        pltpu.VMEM((T, DI), F32),
        pltpu.VMEM((T, WIDE), BF16),
        pltpu.VMEM((T, CHANNELS), F32),
        pltpu.VMEM((2, LANE, GROUP), F32),
        pltpu.VMEM((T, LANE), F32),
        pltpu.VMEM((SMALL, LANE), F32),
        pltpu.VMEM((256, LANE), F32),
        pltpu.VMEM((T, D), BF16),
        pltpu.VMEM((T, D), F32),
    ]


def run_backward(s, grad, live, w, heads, idx, proj, scan, gain, conv, wide):
    return pl.pallas_call(
        backward,
        out_shape=(
            jax.ShapeDtypeStruct((T, D), F32),
            jax.ShapeDtypeStruct((T, D), BF16),
            jax.ShapeDtypeStruct(WHOLE, BF16),
            jax.ShapeDtypeStruct((8, LANE), F32),
        ),
        in_specs=vm(1) + [pl.BlockSpec(memory_space=pl.ANY)] + vm(9),
        out_specs=tuple(vm(4)),
        scratch_shapes=backward_scratch() + [pltpu.VMEM((T, D), BF16), pltpu.SemaphoreType.DMA((1,))],
        compiler_params=pltpu.CompilerParams(vmem_limit_bytes=56 * 1024 * 1024),
        name="second_backward",
    )(s, grad, live, w, heads, idx, proj, scan, gain, conv, wide)


def finish_kernel(acts_ref, grads_ref, g_ref, heads_ref, act_out, grad_out, gain_out, in_out, taps_out, bias_out,
                  step_out, decay_out, skip_out, gated_out, out_out):
    act_out[0, :, 0] = acts_ref[...]
    grad_out[0, :, 0] = grads_ref[...]
    for u in range(27):
        pair, side = u // 2, u % 2
        width = min(LANE, in_out.shape[2] - LANE * u)
        part = g_ref[pair % 2, pair // 2, 12 * side : 12 * side + 12, 0:width]
        in_out[0, :, LANE * u : LANE * u + width] = part
    for c in range(6):
        out_out[0, :, chunk(c)] = g_ref[c % 2, 7 + c // 2, 0:24, :]
    small = g_ref[1, 6, 8:16, :]
    bias_out[...] = small[5:6, 0:28]
    for k in range(4):
        turned = small if k == 0 else pltpu.roll(small, LANE - 32 * k, 1)
        taps_out[0, k : k + 1, :] = turned[4:5, 0:28]
        if k == 1:
            gain_out[...] = turned[5:6, 0:12]
        if k == 2:
            gated_out[...] = turned[5:6, 0:24]
    heads = jnp.where(lax.axis_index("section") == 0, heads_ref[0:4, :], heads_ref[4:8, :])
    step_out[...] = heads[0:1, 0:HEADS]
    decay_out[...] = heads[1:2, 0:HEADS]
    skip_out[...] = heads[2:3, 0:HEADS]


def run_finish(acts, grads, g, heads):
    shapes = (
        ((1, 2, 1, T, D), BF16),
        ((1, 2, 1, T, D), F32),
        ((1, 12), F32),
        ((1, 12, 3352), F32),
        ((1, 4, 28), F32),
        ((1, 28), F32),
        ((1, HEADS), F32),
        ((1, HEADS), F32),
        ((1, HEADS), F32),
        ((1, 24), F32),
        ((1, 24, D), F32),
    )
    return pl.pallas_call(
        finish_kernel,
        out_shape=tuple(jax.ShapeDtypeStruct(shape, kind) for shape, kind in shapes),
        in_specs=vm(4),
        out_specs=tuple(vm(11)),
        compiler_params=pltpu.CompilerParams(vmem_limit_bytes=32 * 1024 * 1024),
        name="outputs",
    )(acts, grads, g, heads)


def body(
    block_input,
    out_grad,
    live_mask,
    norm_gain,
    in_weight,
    conv_weight,
    conv_bias,
    dt_bias,
    a_log,
    d_skip,
    gated_gain,
    out_weight,
):
    idx = owner_index()
    weight0, weight1, heads, act0, *saved0 = run_entry(
        block_input, in_weight, out_weight, conv_weight, conv_bias, norm_gain, gated_gain, dt_bias, a_log, d_skip,
        idx,
    )
    act1, *saved1 = run_forward(act0, weight1, heads, idx)
    grad1, low1, weight_grad1, head_grad1 = run_backward(
        act0, out_grad, live_mask, weight1, heads, idx, *saved1
    )
    totals = run_exit(
        block_input, low1, weight0, heads, idx, *saved0, weight_grad1, head_grad1, act0, act1, grad1
    )
    return run_finish(*totals)


def solution(mesh):
    placed = (
        P(None, "dp", None, None),
        P(None, "dp", None, None),
        P(None, "dp"),
        P("section", "dp"),
        P("section", "dp", None),
        P("section", None, "dp"),
        P("section", "dp"),
        P("section", None),
        P("section", None),
        P("section", None),
        P("section", "dp"),
        P("section", "dp", None),
    )
    return jax.shard_map(
        body,
        mesh=mesh,
        in_specs=placed,
        out_specs=(
            P("section", None, "dp", None, None),
            P("section", None, "dp", None, None),
            P("section", "dp"),
            P("section", "dp", None),
            P("section", None, "dp"),
            P("section", "dp"),
            P("section", None),
            P("section", None),
            P("section", None),
            P("section", "dp"),
            P("section", "dp", None),
        ),
        check_vma=False,
    )
```

```python
import functools

import jax
import jax.numpy as jnp
import numpy as np
from jax import lax
from jax.experimental import pallas as pl
from jax.experimental.pallas import tpu as pltpu
from jax.sharding import PartitionSpec as P

F32 = jnp.float32
BF16 = jnp.bfloat16
MESH = pl.DeviceIdType.MESH
EPS = 1e-05
T = 256
GROUP = 128
LANE = 128
D = 768
DI = 1536
HEADS = 24
CHANNELS = 1792
WIDE = 3584
ROW_GAIN = 0
ROW_TAPS = 6
ROW_BIAS = 62
ROW_GATED = 76
SMALL = 88


def mm(a, b, dims, precision=None):
    return lax.dot_general(a, b, (dims, ((), ())), precision=precision, preferred_element_type=F32)


NN = ((1,), (0,))
NT = ((1,), (1,))
TN = ((0,), (0,))
EXACT = lax.Precision.HIGHEST


def chunk(j):
    return slice(LANE * j, LANE * (j + 1))


def in_pair(w_ref, j):
    left = w_ref[j // 2, j % 2, :, :, 0:48, :].reshape(D, LANE)
    right = w_ref[j // 2, j % 2, :, :, 48:96, :].reshape(D, LANE)
    return jnp.concatenate([left, right], axis=1)


def out_pair(w_ref, c):
    left = w_ref[7 + c // 2, 0].reshape(DI, LANE)
    right = w_ref[7 + c // 2, 1].reshape(DI, LANE)
    return jnp.concatenate([left, right], axis=1)


def lane_half():
    return lax.broadcasted_iota(jnp.int32, (1, LANE), 1) < 64


def lower_mask():
    rows = lax.broadcasted_iota(jnp.int32, (GROUP, GROUP), 0)
    cols = lax.broadcasted_iota(jnp.int32, (GROUP, GROUP), 1)
    return rows >= cols


def down(x, k):
    if k == 0:
        return x
    rows = lax.broadcasted_iota(jnp.int32, x.shape, 0)
    return jnp.where(rows >= k, pltpu.roll(x, k, 0), 0.0)


def up(x, k):
    if k == 0:
        return x
    rows = lax.broadcasted_iota(jnp.int32, x.shape, 0)
    return jnp.where(rows < T - k, pltpu.roll(x, T - k, 0), 0.0)


def sigmoid(x):
    return 1.0 / (1.0 + jnp.exp(-x))


def conv_of(proj_ref, conv_ref, j):
    x = proj_ref[:, DI + LANE * j : DI + LANE * (j + 1)]
    out = conv_ref[4:5, chunk(j)] + conv_ref[3:4, chunk(j)] * x
    for k in range(1, 4):
        out = out + conv_ref[3 - k : 4 - k, chunk(j)] * down(x, k)
    return x, out


def spread(cols, p):
    return jnp.where(lane_half(), cols[:, 2 * p : 2 * p + 1], cols[:, 2 * p + 1 : 2 * p + 2])


def steps_of(proj_ref, head_ref):
    raw = proj_ref[:, DI + CHANNELS : DI + CHANNELS + LANE] + head_ref[0:1, :]
    steps = jnp.maximum(raw, 0.0) + jnp.log1p(jnp.exp(-jnp.abs(raw)))
    rates = -steps * jnp.exp(head_ref[1:2, :])
    tri = lower_mask().astype(F32)
    cumul = [mm(tri, rates[GROUP * b : GROUP * (b + 1)], NN, EXACT) for b in range(2)]
    return raw, steps, rates, cumul


def forward_steps(s_ref, w_ref, head_ref, idx_ref, act_ref, proj_ref, scan_ref, gain_ref, conv_ref, wide_ref,
            mixed_ref, nout_ref):
    unpack_all(w_ref, idx_ref, head_ref, gain_ref, conv_ref, wide_ref)
    stream = s_ref[...].astype(F32)
    scale = lax.rsqrt(jnp.mean(stream * stream, axis=-1, keepdims=True) + EPS)
    normed = (stream * scale * gain_ref[0:1, :]).astype(BF16)
    for j in range(14):
        got = mm(normed, in_pair(w_ref, j), NN)
        proj_ref[:, 2 * LANE * j : 2 * LANE * (j + 1)] = got
        yield "in"
    for j in range(14):
        _, out = conv_of(proj_ref, conv_ref, j)
        mixed_ref[:, chunk(j)] = (out * sigmoid(out)).astype(BF16)
        yield "conv"
    _, steps, _, cumul = steps_of(proj_ref, head_ref)
    lower = lower_mask()
    half = lane_half()
    key = [mixed_ref[GROUP * b : GROUP * (b + 1), chunk(12)] for b in range(2)]
    query = [mixed_ref[GROUP * b : GROUP * (b + 1), chunk(13)] for b in range(2)]
    scores = [mm(query[b], key[b], NT) for b in range(2)]
    cross = mm(query[1], key[0], NT).astype(BF16)
    cumul_t = [c.T for c in cumul]
    total = jnp.zeros((T, 1), F32)
    for p in range(12):
        tail_u = None
        squares = []
        for b in range(2):
            rows = slice(GROUP * b, GROUP * (b + 1))
            x = mixed_ref[rows, chunk(p)].astype(F32)
            u = x * spread(steps[rows], p)
            weights = []
            for h in (2 * p, 2 * p + 1):
                gap = cumul[b][:, h : h + 1] - cumul_t[b][h : h + 1, :]
                weights.append((scores[b] * jnp.exp(jnp.where(lower, gap, -1e30))).astype(BF16))
            u_two = jnp.concatenate([jnp.where(half, u, 0.0), jnp.where(half, 0.0, u)], axis=0)
            y = mm(jnp.concatenate(weights, axis=1), u_two.astype(BF16), NN)
            cum = spread(cumul[b], p)
            if b == 0:
                tail_u = (jnp.exp(cum[GROUP - 1 : GROUP, :] - cum) * u).astype(BF16)
            else:
                y = y + jnp.exp(cum) * mm(cross, tail_u, NN)
            y = y + x * wide_ref[1:2, chunk(p)]
            scan_ref[rows, chunk(p)] = y
            z = proj_ref[rows, chunk(p)]
            gated = y * (z * sigmoid(z))
            squares.append(jnp.sum(gated * gated, axis=-1, keepdims=True))
        total = total + jnp.concatenate(squares, axis=0)
        yield "scan"
    scale_out = lax.rsqrt(total * (1.0 / DI) + EPS)
    for p in range(12):
        z = proj_ref[:, chunk(p)]
        gated = scan_ref[:, chunk(p)] * (z * sigmoid(z))
        nout_ref[:, chunk(p)] = (gated * scale_out * wide_ref[0:1, chunk(p)]).astype(BF16)
    yield "norm"
    for c in range(0, 6, 2):
        cols = slice(LANE * c, LANE * (c + 2))
        branch = mm(nout_ref[...], out_pair(w_ref, c), NN)
        act_ref[:, cols] = (s_ref[:, cols].astype(F32) + branch).astype(BF16)
        yield "branch"


def fold(value, expand):
    high = value.astype(BF16)
    low = (value - high.astype(F32)).astype(BF16)
    return mm(high, expand, NN) + mm(low, expand, NN)


def backward_steps(s_ref, gout_ref, w_ref, head_ref, idx_ref, proj_ref, scan_ref, gain_ref, conv_ref, wide_ref,
             gin_ref, low_ref, d_ref, hgrad_ref,
             mixed_ref, nout_ref, gno_ref, gproj_ref, dmix_ref, dcum_ref, dstep_ref, small_ref, pack_ref, norm_ref, gnorm_ref):
    hgrad_ref[...] = jnp.zeros_like(hgrad_ref)
    skip_sum = jnp.zeros((1, LANE), F32)
    lower = lower_mask()
    half = lane_half()
    grad_branch = gout_ref[...]
    total = jnp.zeros((T, 1), F32)
    for p in range(12):
        z = proj_ref[:, chunk(p)]
        gated = scan_ref[:, chunk(p)] * (z * sigmoid(z))
        total = total + jnp.sum(gated * gated, axis=-1, keepdims=True)
        yield "square", None
    scale_out = lax.rsqrt(total * (1.0 / DI) + EPS)
    for c in range(0, 6, 2):
        part = mm(grad_branch[:, LANE * c : LANE * (c + 2)], out_pair(w_ref, c), NT)
        if c == 0:
            gno_ref[...] = part
        else:
            gno_ref[...] += part
    inner = jnp.zeros((T, 1), F32)
    for p in range(12):
        z = proj_ref[:, chunk(p)]
        gated = scan_ref[:, chunk(p)] * (z * sigmoid(z))
        unit = gated * scale_out
        gain = wide_ref[0:1, chunk(p)]
        nout_ref[:, chunk(p)] = (unit * gain).astype(BF16)
        gno = gno_ref[:, chunk(p)]
        small_ref[ROW_GATED + p : ROW_GATED + p + 1, :] = jnp.sum(gno * unit, axis=0, keepdims=True)
        inner = inner + jnp.sum(gno * gain * unit, axis=-1, keepdims=True)
        yield "inner", None
    inner = inner * (1.0 / DI)
    for c in range(0, 6, 2):
        grad = mm(nout_ref[...], grad_branch[:, LANE * c : LANE * (c + 2)], TN).astype(BF16)
        for e in range(2):
            d_ref[7 + c // 2, e] = grad[:, LANE * e : LANE * (e + 1)].reshape(4, 4, 96, LANE)
        yield "out", 7 + c // 2
    for p in range(12):
        z = proj_ref[:, chunk(p)]
        scan = scan_ref[:, chunk(p)]
        sig = sigmoid(z)
        silu = z * sig
        unit = scan * silu * scale_out
        ggated = scale_out * (gno_ref[:, chunk(p)] * wide_ref[0:1, chunk(p)] - unit * inner)
        gproj_ref[:, chunk(p)] = (ggated * scan * (sig + silu * (1.0 - sig))).astype(BF16)
        gno_ref[:, chunk(p)] = ggated * silu
        yield "gate", None
    stream = s_ref[...].astype(F32)
    scale = lax.rsqrt(jnp.mean(stream * stream, axis=-1, keepdims=True) + EPS)
    norm_ref[...] = (stream * scale * gain_ref[0:1, :]).astype(BF16)

    def in_grad(j):
        gp = gproj_ref[:, 2 * LANE * j : 2 * LANE * (j + 1)]
        grad = mm(norm_ref[...], gp, TN).astype(BF16)
        for e in range(1 if j == 13 else 2):
            part = grad[:, LANE * e : LANE * (e + 1)].reshape(4, 4, 48, LANE)
            d_ref[j // 2, j % 2, :, :, 48 * e : 48 * (e + 1), :] = part
        back = mm(gp, in_pair(w_ref, j), NT)
        if j == 0:
            gnorm_ref[...] = back
        else:
            gnorm_ref[...] += back

    for j in range(6):
        in_grad(j)
        yield "early", j // 2 if j % 2 else None
    def taps(j):
        x, out = conv_of(proj_ref, conv_ref, j)
        sig = sigmoid(out)
        dconv = dmix_ref[:, chunk(j)] * (sig + out * sig * (1.0 - sig))
        small_ref[ROW_BIAS + j : ROW_BIAS + j + 1, :] = jnp.sum(dconv, axis=0, keepdims=True)
        dx = conv_ref[3:4, chunk(j)] * dconv
        for k in range(4):
            row = ROW_TAPS + 14 * (3 - k) + j
            small_ref[row : row + 1, :] = jnp.sum(dconv * down(x, k), axis=0, keepdims=True)
            if k:
                dx = dx + conv_ref[3 - k : 4 - k, chunk(j)] * up(dconv, k)
        gproj_ref[:, DI + LANE * j : DI + LANE * (j + 1)] = dx.astype(BF16)
    for j in range(14):
        _, out = conv_of(proj_ref, conv_ref, j)
        mixed_ref[:, chunk(j)] = (out * sigmoid(out)).astype(BF16)
        yield "conv", None
    raw, steps, rates, cumul = steps_of(proj_ref, head_ref)
    key = [mixed_ref[GROUP * b : GROUP * (b + 1), chunk(12)] for b in range(2)]
    query = [mixed_ref[GROUP * b : GROUP * (b + 1), chunk(13)] for b in range(2)]
    scores = [mm(query[b], key[b], NT) for b in range(2)]
    cross = mm(query[1], key[0], NT).astype(BF16)
    cumul_t = [c.T for c in cumul]
    dscores = [jnp.zeros((GROUP, GROUP), F32) for _ in range(2)]
    dcross = jnp.zeros((GROUP, GROUP), F32)
    dcum_ref[...] = jnp.zeros_like(dcum_ref)
    dstep_ref[...] = jnp.zeros_like(dstep_ref)
    lanes = lax.broadcasted_iota(jnp.int32, (1, LANE), 1)
    head_row = lax.broadcasted_iota(jnp.int32, (LANE, LANE), 0)
    head_col = lax.broadcasted_iota(jnp.int32, (LANE, LANE), 1)
    row_sum = [jnp.zeros((GROUP, LANE), F32) for _ in range(2)]
    for p in range(12):
        expand = (head_col == 2 * p + jnp.where(head_row < 64, 0, 1)).astype(BF16)
        tail_u = eg = None
        us, xs, dus, step_es, grads = [], [], [], [], []
        tail = None
        for b in range(2):
            rows = slice(GROUP * b, GROUP * (b + 1))
            x = mixed_ref[rows, chunk(p)].astype(F32)
            step_e = spread(steps[rows], p)
            u = x * step_e
            g = gno_ref[rows, chunk(p)]
            g_two = jnp.concatenate([jnp.where(half, g, 0.0), jnp.where(half, 0.0, g)], axis=0)
            g_two = g_two.astype(BF16)
            value = mm(g_two, u.astype(BF16), NT)
            weights = []
            for e in range(2):
                h = 2 * p + e
                gap = cumul[b][:, h : h + 1] - cumul_t[b][h : h + 1, :]
                decay = jnp.exp(jnp.where(lower, gap, -1e30))
                weight = scores[b] * decay
                weights.append(weight.astype(BF16))
                v = value[GROUP * e : GROUP * (e + 1)]
                dscores[b] = dscores[b] + v * decay
                both = v * weight
                row_sum[b] = jnp.where(lanes == h, jnp.sum(both, axis=-1, keepdims=True), row_sum[b])
                dcum_ref[b, h : h + 1, :] = -jnp.sum(both, axis=0, keepdims=True)
            du = mm(jnp.concatenate(weights, axis=0), g_two, TN)
            us.append(u)
            xs.append(x)
            dus.append(du)
            step_es.append(step_e)
            grads.append(g)
            cum = spread(cumul[b], p)
            if b == 0:
                tail = jnp.exp(cum[GROUP - 1 : GROUP, :] - cum)
                tail_u = tail * u
            else:
                eg = jnp.exp(cum) * g
        tail_low = tail_u.astype(BF16)
        eg_low = eg.astype(BF16)
        dtail = mm(cross, eg_low, TN)
        dcross = dcross + mm(eg_low, tail_low, NT)
        dus[0] = dus[0] + tail * dtail
        column = fold(tail_u * dtail, expand)
        row_sum[0] = row_sum[0] - column
        row_sum[0] = row_sum[0] + jnp.where(
            lax.broadcasted_iota(jnp.int32, (GROUP, 1), 0) == GROUP - 1,
            jnp.sum(column, axis=0, keepdims=True), 0.0)
        row_sum[1] = row_sum[1] + fold(eg * mm(cross, tail_low, NN), expand)
        skip = jnp.zeros((1, LANE), F32)
        for b in range(2):
            rows = slice(GROUP * b, GROUP * (b + 1))
            dstep_ref[rows, :] += fold(dus[b] * xs[b], expand)
            dmix_ref[rows, chunk(p)] = step_es[b] * dus[b] + grads[b] * wide_ref[1:2, chunk(p)]
            skip = skip + jnp.sum(grads[b] * xs[b], axis=0, keepdims=True)
        skip_sum = skip_sum + fold(jnp.broadcast_to(skip, (8, LANE)), expand)[0:1]
        taps(p)
        if p % 2:
            in_grad(6 + p // 2)
        yield "scan", 3 + p // 4 if p % 4 == 3 else None
    dcross_low = dcross.astype(BF16)
    ds_low = [d.astype(BF16) for d in dscores]
    dmix_ref[0:GROUP, chunk(12)] = mm(ds_low[0], query[0], TN) + mm(dcross_low, query[1], TN)
    dmix_ref[GROUP:T, chunk(12)] = mm(ds_low[1], query[1], TN)
    dmix_ref[0:GROUP, chunk(13)] = mm(ds_low[0], key[0], NN)
    dmix_ref[GROUP:T, chunk(13)] = mm(ds_low[1], key[1], NN) + mm(dcross_low, key[0], NN)
    tri = lower.astype(F32)
    decay_rate = jnp.exp(head_ref[1:2, :])
    step_sum = jnp.zeros((1, LANE), F32)
    decay_sum = jnp.zeros((1, LANE), F32)
    for b in range(2):
        rows = slice(GROUP * b, GROUP * (b + 1))
        drate = mm(tri, row_sum[b] + dcum_ref[b].T, TN, EXACT)
        draw = (dstep_ref[rows, :] - decay_rate * drate) * sigmoid(raw[rows])
        draw = jnp.where(lanes < HEADS, draw, 0.0)
        decay_sum = decay_sum + jnp.sum(drate * rates[rows], axis=0, keepdims=True)
        step_sum = step_sum + jnp.sum(draw, axis=0, keepdims=True)
        gproj_ref[rows, DI + CHANNELS : DI + CHANNELS + LANE] = draw.astype(BF16)
    hgrad_ref[0:1, :] = step_sum
    hgrad_ref[1:2, :] = decay_sum
    hgrad_ref[2:3, :] = skip_sum
    gproj_ref[:, WIDE - LANE :] = jnp.zeros((T, LANE), BF16)
    taps(12)
    taps(13)
    for j in (13, 12):
        in_grad(j)
        yield "late", None
    gnormed = gnorm_ref[...]
    unit = stream * scale
    gain_grad = jnp.sum(gnormed * unit, axis=0, keepdims=True)
    for c in range(6):
        small_ref[ROW_GAIN + c : ROW_GAIN + c + 1, :] = gain_grad[:, chunk(c)]
    pack_all(small_ref, idx_ref, pack_ref)
    d_ref[6, 1, :, :, 48:64, :] = pack_ref[...].astype(BF16).reshape(4, 4, 16, LANE)
    d_ref[6, 1, :, :, 64:96, :] = jnp.zeros((4, 4, 32, LANE), BF16)
    yield "pack", 6
    gunit = gnormed * gain_ref[0:1, :]
    center = jnp.mean(gunit * unit, axis=-1, keepdims=True)
    gin = gout_ref[...].astype(F32) + scale * (gunit - unit * center)
    gin_ref[...] = gin
    low_ref[...] = gin.astype(BF16)
    yield "done", None


KINDS = (
    (2, 12, ROW_GAIN, 6, 32, 1),
    (0, 28, ROW_TAPS, 14, 0, 0),
    (0, 28, ROW_TAPS + 14, 14, 32, 0),
    (0, 28, ROW_TAPS + 28, 14, 64, 0),
    (0, 28, ROW_TAPS + 42, 14, 96, 0),
    (0, 28, ROW_BIAS, 14, 0, 1),
    (4, 24, ROW_GATED, 12, 64, 1),
)


def owner_index():
    table = np.zeros((8, CHANNELS), np.int32)
    for row, width, length in ((0, 28, CHANNELS), (2, 12, D), (4, 24, DI)):
        position = np.arange(length)
        owner = position // width
        table[row, :length] = 16 * (owner // 4) + 2 * (owner % 4)
        table[row + 1, :length] = position % width
    return jnp.asarray(table)


def window(width, c):
    first, last = LANE * c // width, (LANE * c + LANE - 1) // width
    return 16 * (first // 4), 16 * (last // 4) + 16


def unpack(pack, idx_ref, kind, c):
    row, width, _, _, lane, line = kind
    low, high = window(width, c)
    lanes = lax.broadcasted_iota(jnp.int32, (LANE, LANE), 0)
    pick = (lanes == idx_ref[row + 1 : row + 2, chunk(c)] + lane).astype(BF16)
    rows = lax.broadcasted_iota(jnp.int32, (high - low, LANE), 0) + low
    got = mm(pack[low:high], pick, NN)
    return jnp.sum(jnp.where(rows == idx_ref[row : row + 1, chunk(c)] + line, got, 0.0), axis=0, keepdims=True)


def unpack_all(w_ref, idx_ref, head_ref, gain_ref, conv_ref, wide_ref):
    pack = w_ref[6, 1, :, :, 48:64, :].reshape(256, LANE)
    for c in range(6):
        gain_ref[0:1, chunk(c)] = unpack(pack, idx_ref, KINDS[0], c)
    for k in range(5):
        for c in range(14):
            conv_ref[k : k + 1, chunk(c)] = unpack(pack, idx_ref, KINDS[1 + k], c)
    for c in range(12):
        wide_ref[0:1, chunk(c)] = unpack(pack, idx_ref, KINDS[6], c)
        wide_ref[1:2, chunk(c)] = spread(head_ref[2:3, :], c)


def pack_all(small_ref, idx_ref, pack_ref):
    pack_ref[...] = jnp.zeros_like(pack_ref)
    for kind in KINDS:
        row, width, start, count, lane, line = kind
        for c in range(count):
            low, high = window(width, c)
            lanes = lax.broadcasted_iota(jnp.int32, (LANE, LANE), 0)
            pick = (lanes == idx_ref[row + 1 : row + 2, chunk(c)] + lane).astype(BF16)
            rows = lax.broadcasted_iota(jnp.int32, (high - low, LANE), 0) + low
            value = small_ref[start + c : start + c + 1, :]
            held = jnp.where(rows == idx_ref[row : row + 1, chunk(c)] + line, value, 0.0).astype(BF16)
            pack_ref[low:high, :] += mm(held, pick, NT)


def vm(count):
    return [pl.BlockSpec(memory_space=pltpu.VMEM)] * count


class Sems:
    def __init__(self, send, recv):
        self.send, self.recv, self.used = send, recv, 0

    def take(self):
        index = self.used
        self.used += 1
        return self.send.at[index], self.recv.at[index]


class Place:
    def __init__(self):
        self.section = lax.axis_index("section")
        self.dp = lax.axis_index("dp")
        self.z = lax.div(self.dp, 16)
        self.x = lax.rem(lax.div(self.dp, 4), 4)
        self.q = lax.rem(self.dp, 4)
        self.core = lax.rem(self.dp, 2)
        self.column = self.dp - self.q

    def at(self, z, x):
        return (self.section, 16 * z + 4 * x + self.q)

    def along(self, axis, distance):
        if axis == "z":
            return self.at(lax.rem(self.z + distance, 4), self.x)
        return self.at(self.z, lax.rem(self.x + distance, 4))

    def sibling(self):
        return (self.section, self.dp + 1 - 2 * self.core)

    def in_column(self, section, q):
        return (section, self.column + q)


def greet(place):
    barrier = pltpu.get_barrier_semaphore()
    peers = [place.in_column(place.section, lax.rem(place.q + r, 4)) for r in range(1, 4)]
    peers += [place.in_column(1 - place.section, lax.rem(place.q + r, 4)) for r in range(4)]
    peers += [place.along(axis, r) for axis in "zx" for r in range(1, 4)]
    for peer in peers:
        pl.semaphore_signal(barrier, inc=1, device_id=peer, device_id_type=MESH)
    pl.semaphore_wait(barrier, len(peers))


def push(src, dst, sems, device):
    send, recv = sems
    return pltpu.make_async_remote_copy(
        src_ref=src, dst_ref=dst, send_sem=send, recv_sem=recv, device_id=device, device_id_type=MESH
    )


PAIRS = range(10)
AXES = ("xz", "zx", "xz", "zx", "xz", "zx", "xz", "zx", "xz", "zx")
SHARD = (10, 32, LANE)
WHOLE = (10, 2, 4, 4, 96, LANE)


class Copies:
    def __init__(self, place, sems):
        self.place, self.sems, self.sent = place, sems, []

    def start(self, src, dst, device):
        copy = push(src, dst, self.sems.take(), device)
        copy.start()
        self.sent.append(copy)
        return copy

    def end(self):
        for copy in self.sent:
            copy.wait_send()


def coord(place, axis, distance):
    return lax.rem((place.z if axis == "z" else place.x) + distance, 4)


def column_copies(place, layer, sems, source, landing):
    copies = {}
    for other in (0, 1):
        for r in range(4):
            if other == 0 and r == 0:
                continue
            target = lax.rem(place.q + r, 4)
            section = layer if other == 0 else 1 - layer
            copies[other, r] = push(
                source(target), landing, sems.take(), place.in_column(section, target)
            )
    return copies


def gather_steps(layer, place, sems, local, shard_ref, w_ref, slabs, whole, own):
    run = Copies(place, sems)
    core = place.core
    copies = column_copies(place, layer, sems, lambda q: shard_ref.at[lax.rem(q, 2)], slabs.at[place.q])
    mine = pltpu.make_async_copy(shard_ref.at[core], slabs.at[place.q], local.at[0])

    @pl.when(place.section == layer)
    def _():
        for copy in copies.values():
            copy.start()
        mine.start()

    yield "column"

    @pl.when(place.section == layer)
    def _():
        mine.wait()
        for r in range(1, 4):
            copies[0, r].wait_recv()

    @pl.when(place.section != layer)
    def _():
        for r in range(4):
            copies[1, r].wait_recv()

    whole[...] = jnp.zeros_like(whole)
    for q in range(4):
        part = slabs[q].astype(F32)
        whole[0:7, 12 * q : 12 * q + 12, :] = part[0:7, 0:12]
        whole[0:6, 48 + 12 * q : 60 + 12 * q, :] = part[0:6, 16:28]

        @pl.when(core == 0)
        def _():
            whole[6, 48 + 12 * q : 60 + 12 * q, :] = part[6, 16:28]

        @pl.when(core == 1)
        def _():
            whole[6, 48 + 2 * q : 50 + 2 * q, :] = part[6, 16:18]

        whole[7:10, 24 * q : 24 * q + 24, :] = part[7:10, 0:24]
    own[...] = whole[...].astype(BF16)
    keep = pltpu.make_async_copy(own, w_ref.at[:, core, place.z, place.x], local.at[1])
    keep.start()
    first, second, third = {}, {}, {}
    for i in PAIRS:
        there = w_ref.at[i, core, place.z, place.x]
        axis = AXES[i][0]
        first[i] = [run.start(own.at[i], there, place.along(axis, r)) for r in (1, 3, 2)]

    def line(i, distance, rows=None):
        axis = AXES[i][1]
        at = coord(place, axis, distance)
        z, x = (at, pl.ds(0, 4)) if axis == "z" else (pl.ds(0, 4), at)
        if rows is None:
            return w_ref.at[i, core, z, x]
        return w_ref.at[i, core, z, x, pl.ds(rows, 48)]

    for i in PAIRS:
        yield "first"
        if i == 0:
            keep.wait()
        for copy in first[i]:
            copy.wait_recv()
        src = line(i, 0)
        second[i] = [run.start(src, src, place.along(AXES[i][1], r)) for r in (1, 3)]
    for i in PAIRS:
        yield "second"
        second[i][0].wait_recv()
        got = line(i, 3, 0)
        one = run.start(got, got, place.along(AXES[i][1], 1))
        second[i][1].wait_recv()
        got = line(i, 1, 48)
        two = run.start(got, got, place.along(AXES[i][1], 3))
        third[i] = (one, two)
    over = {}
    for i in PAIRS:
        yield "third"
        for copy in third[i]:
            copy.wait_recv()
        half = w_ref.at[i, core]
        over[i] = run.start(half, half, place.sibling())
    for i in PAIRS:
        yield "over"
        over[i].wait_recv()
    yield "whole"
    run.end()

    @pl.when(place.section == layer)
    def _():
        for copy in copies.values():
            copy.wait_send()


GATHER_COPIES = 7 + 8 * 10


def gather_scratch():
    return [
        pltpu.VMEM((4,) + SHARD, BF16),
        pltpu.VMEM((10, 96, LANE), F32),
        pltpu.VMEM((10, 96, LANE), BF16),
        pltpu.SemaphoreType.DMA((2,)),
    ]


def go(steps, count):
    for _ in range(count):
        next(steps, None)


def build_shard(in_ref, out_ref, taps_ref, bias_ref, gain_ref, gated_ref, shard_ref):
    shard_ref[...] = jnp.zeros_like(shard_ref)
    for u in range(27):
        pair, side = u // 2, u % 2
        width = min(LANE, in_ref.shape[2] - LANE * u)
        part = in_ref[0, :, LANE * u : LANE * u + width]
        shard_ref[pair % 2, pair // 2, 16 * side : 16 * side + 12, 0:width] = part
    for c in range(6):
        shard_ref[c % 2, 7 + c // 2, 0:24, :] = out_ref[0, :, chunk(c)]

    def shift(value, start):
        rows = lax.broadcasted_iota(jnp.int32, (value.shape[1], LANE), 0)
        lanes = lax.broadcasted_iota(jnp.int32, (value.shape[1], LANE), 1)
        return mm(value.astype(F32), (lanes == rows + start).astype(F32), NN)

    taps = shift(taps_ref[0, 0:1, :], 0)
    for k in range(1, 4):
        taps = taps + shift(taps_ref[0, k : k + 1, :], 32 * k)
    rest = shift(bias_ref[...], 0) + shift(gain_ref[...], 32) + shift(gated_ref[...], 64)
    small = jnp.concatenate([taps, rest, jnp.zeros((14, LANE), F32)], axis=0)
    shard_ref[1, 6, 16:32, :] = small.astype(BF16)


ORDER = (7, 8, 9, 0, 1, 2, 3, 4, 5, 6)
SOON, LATER = ORDER[:6], ORDER[6:]


def run_plan(work, plan, ready_step):
    seen = {}
    for phase, ready in work:
        if ready is not None:
            ready_step(ready)
        at = seen.get(phase, 0)
        seen[phase] = at + 1
        if phase in plan:
            length, actions = plan[phase]
            for step, i in actions[at * len(actions) // length : (at + 1) * len(actions) // length]:
                step(i)
        run_steps(plan.get((phase, seen.get(phase, 0)), ()))


def steps_for(step, pairs):
    return [(step, i) for i in pairs]


def run_steps(steps):
    for step, i in steps:
        step(i)


class Reduce:
    def __init__(self, layer, place, sems, d_ref, g_ref, bufs):
        self.layer, self.place, self.d, self.g = layer, place, d_ref, g_ref
        self.acc, self.early, self.late, self.last, self.whole, *self.ends = bufs
        self.sems, self.run = sems, Copies(place, sems)
        self.crossing, self.first, self.second, self.third, self.copies = {}, {}, {}, {}, []

    def line(self, i, distance, rows=None):
        axis = AXES[i][1]
        at = coord(self.place, axis, distance)
        z, x = (at, pl.ds(0, 4)) if axis == "z" else (pl.ds(0, 4), at)
        return (i, z, x) if rows is None else (i, z, x, pl.ds(rows, 48))

    def cross(self, i):
        core = self.place.core
        self.crossing[i] = self.run.start(self.d.at[i, 1 - core], self.acc.at[i], self.place.sibling())

    def add(self, i):
        own = self.d[i, self.place.core]
        self.crossing[i].wait_recv()
        self.acc[i] = self.acc[i] + own

    def add_send(self, i):
        self.add(i)
        self.send(i)

    def send(self, i):
        axis = AXES[i][1]
        self.first[i] = (
            self.run.start(self.acc.at[self.line(i, 2, 0)], self.early.at[i, 0], self.place.along(axis, 1)),
            self.run.start(self.acc.at[self.line(i, 2, 48)], self.early.at[i, 1], self.place.along(axis, 3)),
        )

    def near_add(self, i):
        for side, (distance, rows) in enumerate(((1, 0), (3, 48))):
            self.first[i][side].wait_recv()
            at = self.line(i, distance, rows)
            self.acc[at] = self.acc[at] + self.early[i, side]

    def near_send(self, i):
        axis = AXES[i][1]
        self.second[i] = [
            self.run.start(self.acc.at[self.line(i, distance)], self.late.at[i, side],
                           self.place.along(axis, distance))
            for side, distance in enumerate((1, 3))
        ]

    def near(self, i):
        self.near_add(i)
        self.near_send(i)

    def across(self, i):
        for copy in self.second[i]:
            copy.wait_recv()
        at = self.line(i, 0)
        total = self.acc[at].astype(F32) + self.late[i, 0].astype(F32) + self.late[i, 1].astype(F32)
        self.acc[at] = total.astype(BF16)
        axis = AXES[i][0]
        place = self.place
        copies = []
        for r in (1, 3, 2):
            to = coord(place, axis, r)
            z, x = (to, place.x) if axis == "z" else (place.z, to)
            copies.append(self.run.start(self.acc.at[i, z, x], self.last.at[i, r - 1], place.along(axis, r)))
        self.third[i] = copies

    def total(self, i):
        for copy in self.third[i]:
            copy.wait_recv()
        own = self.acc[i, self.place.z, self.place.x].astype(F32)
        for r in range(3):
            own = own + self.last[i, r].astype(F32)
        self.whole[i] = own

    def hand(self, part):
        place, layer, whole = self.place, self.layer, self.whole
        rows, slabs, landed = self.ends
        low, count = ((0, 192), (192, 48))[part]
        if part == 0:
            rows[...] = jnp.zeros_like(rows)
        for q in range(4):
            if part == 0:
                rows[0:5, 0:12, :] = whole[0:5, 12 * q : 12 * q + 12, :]
                rows[0:5, 12:24, :] = whole[0:5, 48 + 12 * q : 60 + 12 * q, :]
                rows[7:10, 0:24, :] = whole[7:10, 24 * q : 24 * q + 24, :]
                value = jnp.concatenate([rows[0:5].reshape(120, LANE), rows[7:10].reshape(72, LANE)], axis=0)
            else:
                rows[5:7, 0:12, :] = whole[5:7, 12 * q : 12 * q + 12, :]
                rows[5, 12:24, :] = whole[5, 48 + 12 * q : 60 + 12 * q, :]

                @pl.when(place.core == 0)
                def _():
                    rows[6, 12:24, :] = whole[6, 48 + 12 * q : 60 + 12 * q, :]

                @pl.when(place.core == 1)
                def _():
                    rows[6, 12:14, :] = whole[6, 48 + 2 * q : 50 + 2 * q, :]

                value = rows[5:7].reshape(48, LANE)
            slabs[q, low : low + count, :] = value.astype(BF16)
        slot = 4 * place.section + place.q
        copies = {}
        for other in (0, 1):
            for r in range(4):
                if other == 0 and r == 0:
                    continue
                target = lax.rem(place.q + r, 4)
                copies[other, r] = push(
                    slabs.at[target, pl.ds(low, count)], landed.at[slot, pl.ds(low, count)],
                    self.sems.take(), place.in_column(layer, target)
                )

        @pl.when(place.section == layer)
        def _():
            for r in range(1, 4):
                copies[0, r].start()
            landed[slot, low : low + count, :] = slabs[place.q, low : low + count, :]

        @pl.when(place.section != layer)
        def _():
            for r in range(4):
                copies[1, r].start()

        self.copies.append(copies)

    def finish(self):
        place, landed = self.place, self.ends[2]

        @pl.when(place.section == self.layer)
        def _():
            for copies in self.copies:
                for copy in copies.values():
                    copy.wait_recv()
            for core in range(2):
                parts = [landed[2 * y + core].astype(F32) for y in range(4)]
                total = parts[0] + parts[1] + parts[2] + parts[3]
                self.g[core, 0:5] = total[0:120].reshape(5, 24, LANE)
                self.g[core, 7:10] = total[120:192].reshape(3, 24, LANE)
                self.g[core, 5:7] = total[192:240].reshape(2, 24, LANE)
            for copies in self.copies:
                for r in range(1, 4):
                    copies[0, r].wait_send()

        @pl.when(place.section != self.layer)
        def _():
            for copies in self.copies:
                for r in range(4):
                    copies[1, r].wait_send()

        self.run.end()


REDUCE_COPIES = 8 * 10 + 14


def reduce_scratch():
    return [
        pltpu.VMEM((10, 4, 4, 96, LANE), BF16),
        pltpu.VMEM((10, 2, 4, 48, LANE), BF16),
        pltpu.VMEM((10, 2, 4, 96, LANE), BF16),
        pltpu.VMEM((10, 3, 96, LANE), BF16),
        pltpu.VMEM((10, 96, LANE), F32),
    ]


def owner_scratch():
    return [
        pltpu.VMEM((10, 24, LANE), F32),
        pltpu.VMEM((4, 240, LANE), BF16),
        pltpu.VMEM((8, 240, LANE), BF16),
    ]


def head_steps(place, sems, hval, head_out_ref, hbuf):
    y = 2 * place.section + lax.div(place.q, 2)
    for index, axis in enumerate(("core", "y", "x", "z")):
        copies = []
        if axis == "core":
            mine, peers = place.core, [place.sibling()]
        elif axis == "y":
            mine, peers = y, []
            for r in range(1, 4):
                to = lax.rem(y + r, 4)
                peers.append((lax.div(to, 2), place.column + 2 * lax.rem(to, 2) + place.core))
        else:
            mine = place.z if axis == "z" else place.x
            peers = [place.along(axis, r) for r in range(1, 4)]
        for peer in peers:
            copy = push(hval, hbuf.at[index, mine], sems.take(), peer)
            copy.start()
            copies.append(copy)
        hbuf[index, mine] = hval[...]
        yield
        for copy in copies:
            copy.wait_recv()
        for copy in copies:
            copy.wait_send()
        total = hbuf[index, 0] + hbuf[index, 1]
        if axis != "core":
            total = total + hbuf[index, 2] + hbuf[index, 3]
        hval[...] = total
    head_out_ref[...] = hval[...]


def entry_kernel(block_ref, in_ref, out_ref, taps_ref, bias_ref, gain_in_ref, gated_ref, step_ref, decay_ref,
                 skip_ref, idx_ref, grad_ref, live_ref,
                 w0_ref, proj0_ref, scan0_ref, acc_ref, heads_ref, act_ref, gain_ref, conv_ref, wide_ref,
                 act1_ref, gin_ref, low_ref, hgrad_ref,
                 s_ref, gout_ref, shard_ref, head_ref, w_here, w_next, proj_a, scan_a, proj_b, scan_b,
                 gain_b, conv_b, wide_b, send, recv, local, *scratch):
    work_refs, scratch = scratch[:11], scratch[11:]
    mixed, nout = work_refs[0:2]
    place = Place()
    stream = pltpu.make_async_copy(block_ref.at[place.section, 0], s_ref, local.at[0])
    stream.start()
    fetch = pltpu.make_async_copy(grad_ref.at[place.section, 0], gout_ref, local.at[1])
    fetch.start()
    build_shard(in_ref, out_ref, taps_ref, bias_ref, gain_in_ref, gated_ref, shard_ref)
    head_ref[...] = jnp.zeros_like(head_ref)
    head_ref[0:1, 0:HEADS] = step_ref[...]
    head_ref[1:2, 0:HEADS] = decay_ref[...]
    head_ref[2:3, 0:HEADS] = skip_ref[...]
    greet(place)
    sems = Sems(send, recv)
    partner = place.in_column(1 - place.section, place.q)
    swap = push(head_ref, heads_ref.at[place.section], sems.take(), partner)
    swap.start()
    heads_ref[place.section] = head_ref[...]
    zero = gather_steps(0, place, sems, scratch[3], shard_ref, w_here, *scratch[0:3])
    one = gather_steps(1, place, sems, scratch[7], shard_ref, w_next, *scratch[4:7])
    go(zero, 1)
    go(one, 1)
    go(zero, 21)
    go(one, 1)
    go(zero, 10)
    go(one, 10)
    go(zero, 7)
    swap.wait()
    stream.wait()
    work = forward_steps(s_ref, w_here, heads_ref.at[0], idx_ref, act_ref, proj_a, scan_a,
                         gain_ref, conv_ref, wide_ref, mixed, nout)
    saved = [pltpu.make_async_copy(w_here, w0_ref, local.at[2]),
             pltpu.make_async_copy(proj_a, proj0_ref, local.at[3]),
             pltpu.make_async_copy(scan_a, scan0_ref, local.at[4])]
    for count, what in enumerate(work):
        if count in (8, 10, 12):
            go(zero, 1)
        if count == 12:
            saved[0].start()
        if what in ("conv", "scan", "branch"):
            go(one, 1)
    saved[1].start()
    saved[2].start()
    for _ in one:
        pass
    go(zero, 1)
    for _ in forward_steps(act_ref, w_next, heads_ref.at[1], idx_ref, act1_ref, proj_b, scan_b,
                           gain_b, conv_b, wide_b, mixed, nout):
        pass
    live = jnp.where(place.section == 0, live_ref[0:1, :], live_ref[1:2, :]).astype(F32)
    fetch.wait()
    gout_ref[...] = (gout_ref[...].astype(F32) * live).astype(BF16)
    saved[0].wait()
    back = Reduce(1, place, sems, w_here, None, scratch[8:13])
    work = backward_steps(act_ref, gout_ref, w_next, heads_ref.at[1], idx_ref, proj_b, scan_b, gain_b, conv_b,
                          wide_b, gin_ref, low_ref, w_here, hgrad_ref, *work_refs)
    run_plan(
        work,
        {
            "conv": (14, steps_for(back.add_send, SOON)),
            ("scan", 8): steps_for(back.add, (3,)),
            ("scan", 12): steps_for(back.add, (4,)),
        },
        back.cross,
    )
    run_steps(steps_for(back.add, (5, 6)) + steps_for(back.near_add, SOON))
    kept = pltpu.make_async_copy(back.acc, acc_ref, local.at[5])
    kept.start()
    back.run.end()
    saved[1].wait()
    saved[2].wait()
    kept.wait()


def run_entry(*given):
    copies = 1 + 2 * GATHER_COPIES + REDUCE_COPIES
    any_space = pl.BlockSpec(memory_space=pl.ANY)
    return pl.pallas_call(
        entry_kernel,
        out_shape=(
            jax.ShapeDtypeStruct(WHOLE, BF16),
            jax.ShapeDtypeStruct((T, WIDE), F32),
            jax.ShapeDtypeStruct((T, DI), F32),
            jax.ShapeDtypeStruct((10, 4, 4, 96, LANE), BF16),
            jax.ShapeDtypeStruct((2, 8, LANE), F32),
            jax.ShapeDtypeStruct((T, D), BF16),
            jax.ShapeDtypeStruct((8, D), F32),
            jax.ShapeDtypeStruct((8, CHANNELS), F32),
            jax.ShapeDtypeStruct((8, DI), F32),
            jax.ShapeDtypeStruct((T, D), BF16),
            jax.ShapeDtypeStruct((T, D), F32),
            jax.ShapeDtypeStruct((T, D), BF16),
            jax.ShapeDtypeStruct((8, LANE), F32),
        ),
        in_specs=[any_space] + vm(10) + [any_space] + vm(1),
        out_specs=tuple([any_space] * 4 + vm(9)),
        scratch_shapes=[
            pltpu.VMEM((T, D), BF16),
            pltpu.VMEM((T, D), BF16),
            pltpu.VMEM((2,) + SHARD, BF16),
            pltpu.VMEM((8, LANE), F32),
            pltpu.VMEM(WHOLE, BF16),
            pltpu.VMEM(WHOLE, BF16),
            pltpu.VMEM((T, WIDE), F32),
            pltpu.VMEM((T, DI), F32),
            pltpu.VMEM((T, WIDE), F32),
            pltpu.VMEM((T, DI), F32),
            pltpu.VMEM((8, D), F32),
            pltpu.VMEM((8, CHANNELS), F32),
            pltpu.VMEM((8, DI), F32),
            pltpu.SemaphoreType.DMA((copies,)),
            pltpu.SemaphoreType.DMA((copies,)),
            pltpu.SemaphoreType.DMA((6,)),
        ]
        + backward_scratch()
        + gather_scratch()
        + gather_scratch()
        + reduce_scratch(),
        compiler_params=pltpu.CompilerParams(
            collective_id=0, has_side_effects=True, vmem_limit_bytes=60 * 1024 * 1024
        ),
        name="gather_forward_and_second_backward",
    )(*given)


def exit_kernel(block_ref, low1_ref, w0_ref, heads_ref, idx_ref, proj0_ref, scan0_ref, gain_ref, conv_ref, wide_ref,
                acc1_ref, hgrad1_ref, act0_ref, act1_ref, gin1_ref,
                acts_ref, grads_ref, g_ref, head_out_ref,
                s_ref, w_ref, proj_ref, scan_ref, d_ref, gin_ref, low_ref, hgrad_ref, hval, hbuf, back_in,
                send, recv, local, *scratch):
    work_refs, scratch = scratch[:11], scratch[11:]
    place = Place()
    head_ref = heads_ref.at[0]
    one = Reduce(1, place, Sems(send, recv), None, g_ref, scratch[0:8])
    sems = one.sems
    zero = Reduce(0, place, sems, d_ref, g_ref, scratch[8:16])
    loads = [
        pltpu.make_async_copy(acc1_ref, one.acc, local.at[0]),
        pltpu.make_async_copy(scan0_ref, scan_ref, local.at[1]),
        pltpu.make_async_copy(proj0_ref, proj_ref, local.at[2]),
        pltpu.make_async_copy(block_ref.at[place.section, 0], s_ref, local.at[3]),
        pltpu.make_async_copy(w0_ref, w_ref, local.at[4]),
    ]
    for load in loads:
        load.start()
    greet(place)
    first = place.section == 0
    partner = place.in_column(1 - place.section, place.q)
    loads[0].wait()
    run_steps(steps_for(one.near_send, SOON) + steps_for(one.send, LATER))
    act_out = [push(ref, acts_ref.at[place.section], pair, partner)
               for pair in (sems.take(),) for ref in (act1_ref, act0_ref)]
    back_out = [push(ref, back_in, pair, partner) for pair in (sems.take(),) for ref in (low1_ref, low_ref)]

    @pl.when(first)
    def _():
        act_out[0].start()
        back_out[0].start()
        acts_ref[0] = act0_ref[...]

    @pl.when(place.section == 1)
    def _():
        act_out[1].start()
        acts_ref[1] = act1_ref[...]
        grads_ref[1] = gin1_ref[...]

    for load in loads[1:]:
        load.wait()
    work = backward_steps(s_ref, low1_ref, w_ref, head_ref, idx_ref, proj_ref, scan_ref, gain_ref, conv_ref,
                          wide_ref, gin_ref, low_ref, d_ref, hgrad_ref, *work_refs)
    run_plan(
        work,
        {
            "conv": (14, steps_for(zero.add_send, SOON)),
            ("scan", 4): steps_for(one.near, LATER),
            ("scan", 6): steps_for(one.across, SOON[:3]),
            ("scan", 7): steps_for(one.across, SOON[3:]),
            ("scan", 8): steps_for(zero.add_send, (3,)),
            ("scan", 12): steps_for(zero.add_send, (4,)),
            ("late", 1): steps_for(zero.near, SOON[:3]),
            ("late", 2): steps_for(zero.near, SOON[3:]) + steps_for(zero.add_send, (5,)),
        },
        zero.cross,
    )
    hval[...] = jnp.zeros_like(hval)
    hval[0:4, :] = hgrad_ref[0:4, :]
    hval[4:8, :] = hgrad1_ref[0:4, :]
    small = head_steps(place, sems, hval, head_out_ref, hbuf)
    go(small, 1)

    @pl.when(place.section == 1)
    def _():
        back_out[1].start()

    @pl.when(first)
    def _():
        grads_ref[0] = gin_ref[...]

    zero.add_send(6)
    run_steps(steps_for(one.across, LATER) + steps_for(one.total, SOON) + steps_for(zero.near, LATER))
    go(small, 1)
    run_steps(steps_for(one.total, LATER) + steps_for(one.hand, (0, 1)))
    run_steps(steps_for(zero.across, SOON))
    go(small, 1)
    run_steps(steps_for(zero.across, LATER))
    one.finish()
    go(small, 1)
    run_steps(steps_for(zero.total, SOON) + steps_for(zero.total, (3, 4)))
    zero.hand(0)
    run_steps(steps_for(zero.total, (5, 6)))
    zero.hand(1)
    go(small, 1)
    act_out[0].wait()
    back_out[0].wait()

    @pl.when(first)
    def _():
        grads_ref[1] = back_in[...].astype(F32)

    @pl.when(place.section == 1)
    def _():
        grads_ref[0] = back_in[...].astype(F32)

    zero.finish()


def run_exit(*given):
    copies = 2 * REDUCE_COPIES + 10 + 2
    any_space = pl.BlockSpec(memory_space=pl.ANY)
    spaces = [any_space] + vm(1) + [any_space] + vm(2) + [any_space] * 2 + vm(3) + [any_space] + vm(4)
    return pl.pallas_call(
        exit_kernel,
        out_shape=(
            jax.ShapeDtypeStruct((2, T, D), BF16),
            jax.ShapeDtypeStruct((2, T, D), F32),
            jax.ShapeDtypeStruct((2, 10, 24, LANE), F32),
            jax.ShapeDtypeStruct((8, LANE), F32),
        ),
        in_specs=spaces,
        out_specs=tuple(vm(4)),
        scratch_shapes=[
            pltpu.VMEM((T, D), BF16),
            pltpu.VMEM(WHOLE, BF16),
            pltpu.VMEM((T, WIDE), F32),
            pltpu.VMEM((T, DI), F32),
            pltpu.VMEM(WHOLE, BF16),
            pltpu.VMEM((T, D), F32),
            pltpu.VMEM((T, D), BF16),
            pltpu.VMEM((8, LANE), F32),
            pltpu.VMEM((8, LANE), F32),
            pltpu.VMEM((4, 4, 8, LANE), F32),
            pltpu.VMEM((T, D), BF16),
            pltpu.SemaphoreType.DMA((copies,)),
            pltpu.SemaphoreType.DMA((copies,)),
            pltpu.SemaphoreType.DMA((5,)),
        ]
        + backward_scratch()
        + reduce_scratch()
        + owner_scratch()
        + reduce_scratch()
        + owner_scratch(),
        compiler_params=pltpu.CompilerParams(
            collective_id=1, has_side_effects=True, vmem_limit_bytes=63 * 1024 * 1024
        ),
        name="first_backward_and_reduce",
    )(*given)


def backward_scratch():
    return [
        pltpu.VMEM((T, CHANNELS), BF16),
        pltpu.VMEM((T, DI), BF16),
        pltpu.VMEM((T, DI), F32),
        pltpu.VMEM((T, WIDE), BF16),
        pltpu.VMEM((T, CHANNELS), F32),
        pltpu.VMEM((2, LANE, GROUP), F32),
        pltpu.VMEM((T, LANE), F32),
        pltpu.VMEM((SMALL, LANE), F32),
        pltpu.VMEM((256, LANE), F32),
        pltpu.VMEM((T, D), BF16),
        pltpu.VMEM((T, D), F32),
    ]


def finish_kernel(acts_ref, grads_ref, g_ref, heads_ref, act_out, grad_out, gain_out, in_out, taps_out, bias_out,
                  step_out, decay_out, skip_out, gated_out, out_out):
    act_out[0, :, 0] = acts_ref[...]
    grad_out[0, :, 0] = grads_ref[...]
    for u in range(27):
        pair, side = u // 2, u % 2
        width = min(LANE, in_out.shape[2] - LANE * u)
        part = g_ref[pair % 2, pair // 2, 12 * side : 12 * side + 12, 0:width]
        in_out[0, :, LANE * u : LANE * u + width] = part
    for c in range(6):
        out_out[0, :, chunk(c)] = g_ref[c % 2, 7 + c // 2, 0:24, :]
    small = g_ref[1, 6, 8:16, :]
    bias_out[...] = small[5:6, 0:28]
    for k in range(4):
        turned = small if k == 0 else pltpu.roll(small, LANE - 32 * k, 1)
        taps_out[0, k : k + 1, :] = turned[4:5, 0:28]
        if k == 1:
            gain_out[...] = turned[5:6, 0:12]
        if k == 2:
            gated_out[...] = turned[5:6, 0:24]
    heads = jnp.where(lax.axis_index("section") == 0, heads_ref[0:4, :], heads_ref[4:8, :])
    step_out[...] = heads[0:1, 0:HEADS]
    decay_out[...] = heads[1:2, 0:HEADS]
    skip_out[...] = heads[2:3, 0:HEADS]


def run_finish(acts, grads, g, heads):
    shapes = (
        ((1, 2, 1, T, D), BF16),
        ((1, 2, 1, T, D), F32),
        ((1, 12), F32),
        ((1, 12, 3352), F32),
        ((1, 4, 28), F32),
        ((1, 28), F32),
        ((1, HEADS), F32),
        ((1, HEADS), F32),
        ((1, HEADS), F32),
        ((1, 24), F32),
        ((1, 24, D), F32),
    )
    return pl.pallas_call(
        finish_kernel,
        out_shape=tuple(jax.ShapeDtypeStruct(shape, kind) for shape, kind in shapes),
        in_specs=vm(4),
        out_specs=tuple(vm(11)),
        compiler_params=pltpu.CompilerParams(vmem_limit_bytes=32 * 1024 * 1024),
        name="outputs",
    )(acts, grads, g, heads)


def body(
    block_input,
    out_grad,
    live_mask,
    norm_gain,
    in_weight,
    conv_weight,
    conv_bias,
    dt_bias,
    a_log,
    d_skip,
    gated_gain,
    out_weight,
):
    idx = owner_index()
    weight, proj, scan, acc, heads, act0, gain, conv, wide, act1, grad1, low1, head_grad1 = run_entry(
        block_input, in_weight, out_weight, conv_weight, conv_bias, norm_gain, gated_gain, dt_bias, a_log, d_skip,
        idx, out_grad, live_mask,
    )
    totals = run_exit(
        block_input, low1, weight, heads, idx, proj, scan, gain, conv, wide, acc, head_grad1, act0, act1, grad1
    )
    return run_finish(*totals)


def solution(mesh):
    placed = (
        P(None, "dp", None, None),
        P(None, "dp", None, None),
        P(None, "dp"),
        P("section", "dp"),
        P("section", "dp", None),
        P("section", None, "dp"),
        P("section", "dp"),
        P("section", None),
        P("section", None),
        P("section", None),
        P("section", "dp"),
        P("section", "dp", None),
    )
    return jax.shard_map(
        body,
        mesh=mesh,
        in_specs=placed,
        out_specs=(
            P("section", None, "dp", None, None),
            P("section", None, "dp", None, None),
            P("section", "dp"),
            P("section", "dp", None),
            P("section", None, "dp"),
            P("section", "dp"),
            P("section", None),
            P("section", None),
            P("section", None),
            P("section", "dp"),
            P("section", "dp", None),
        ),
        check_vma=False,
    )
```

```python
import functools

import jax
import jax.numpy as jnp
import numpy as np
from jax import lax
from jax.experimental import pallas as pl
from jax.experimental.pallas import tpu as pltpu
from jax.sharding import PartitionSpec as P

F32 = jnp.float32
BF16 = jnp.bfloat16
MESH = pl.DeviceIdType.MESH
EPS = 1e-05
T = 256
GROUP = 128
LANE = 128
D = 768
DI = 1536
HEADS = 24
CHANNELS = 1792
WIDE = 3584
ROW_GAIN = 0
ROW_TAPS = 6
ROW_BIAS = 62
ROW_GATED = 76
SMALL = 88


def mm(a, b, dims, precision=None):
    return lax.dot_general(a, b, (dims, ((), ())), precision=precision, preferred_element_type=F32)


NN = ((1,), (0,))
NT = ((1,), (1,))
TN = ((0,), (0,))
EXACT = lax.Precision.HIGHEST


def chunk(j):
    return slice(LANE * j, LANE * (j + 1))


def in_pair(w_ref, j):
    left = w_ref[j // 2, j % 2, :, :, 0:48, :].reshape(D, LANE)
    right = w_ref[j // 2, j % 2, :, :, 48:96, :].reshape(D, LANE)
    return jnp.concatenate([left, right], axis=1)


def out_pair(w_ref, c):
    left = w_ref[7 + c // 2, 0].reshape(DI, LANE)
    right = w_ref[7 + c // 2, 1].reshape(DI, LANE)
    return jnp.concatenate([left, right], axis=1)


def lane_half():
    return lax.broadcasted_iota(jnp.int32, (1, LANE), 1) < 64


def lower_mask():
    rows = lax.broadcasted_iota(jnp.int32, (GROUP, GROUP), 0)
    cols = lax.broadcasted_iota(jnp.int32, (GROUP, GROUP), 1)
    return rows >= cols


def down(x, k):
    if k == 0:
        return x
    rows = lax.broadcasted_iota(jnp.int32, x.shape, 0)
    return jnp.where(rows >= k, pltpu.roll(x, k, 0), 0.0)


def up(x, k):
    if k == 0:
        return x
    rows = lax.broadcasted_iota(jnp.int32, x.shape, 0)
    return jnp.where(rows < T - k, pltpu.roll(x, T - k, 0), 0.0)


def sigmoid(x):
    return 1.0 / (1.0 + jnp.exp(-x))


def conv_of(proj_ref, conv_ref, j):
    x = proj_ref[:, DI + LANE * j : DI + LANE * (j + 1)]
    out = conv_ref[4:5, chunk(j)] + conv_ref[3:4, chunk(j)] * x
    for k in range(1, 4):
        out = out + conv_ref[3 - k : 4 - k, chunk(j)] * down(x, k)
    return x, out


def spread(cols, p):
    return jnp.where(lane_half(), cols[:, 2 * p : 2 * p + 1], cols[:, 2 * p + 1 : 2 * p + 2])


def steps_of(proj_ref, head_ref):
    raw = proj_ref[:, DI + CHANNELS : DI + CHANNELS + LANE] + head_ref[0:1, :]
    steps = jnp.maximum(raw, 0.0) + jnp.log1p(jnp.exp(-jnp.abs(raw)))
    rates = -steps * jnp.exp(head_ref[1:2, :])
    tri = lower_mask().astype(F32)
    cumul = [mm(tri, rates[GROUP * b : GROUP * (b + 1)], NN, EXACT) for b in range(2)]
    return raw, steps, rates, cumul


def forward_steps(s_ref, w_ref, head_ref, idx_ref, act_ref, proj_ref, scan_ref, gain_ref, conv_ref, wide_ref,
            mixed_ref, nout_ref):
    unpack_all(w_ref, idx_ref, head_ref, gain_ref, conv_ref, wide_ref)
    stream = s_ref[...].astype(F32)
    scale = lax.rsqrt(jnp.mean(stream * stream, axis=-1, keepdims=True) + EPS)
    normed = (stream * scale * gain_ref[0:1, :]).astype(BF16)
    for j in range(14):
        got = mm(normed, in_pair(w_ref, j), NN)
        proj_ref[:, 2 * LANE * j : 2 * LANE * (j + 1)] = got
        yield "in"
    for j in range(14):
        _, out = conv_of(proj_ref, conv_ref, j)
        mixed_ref[:, chunk(j)] = (out * sigmoid(out)).astype(BF16)
        yield "conv"
    _, steps, _, cumul = steps_of(proj_ref, head_ref)
    lower = lower_mask()
    half = lane_half()
    key = [mixed_ref[GROUP * b : GROUP * (b + 1), chunk(12)] for b in range(2)]
    query = [mixed_ref[GROUP * b : GROUP * (b + 1), chunk(13)] for b in range(2)]
    scores = [mm(query[b], key[b], NT) for b in range(2)]
    cross = mm(query[1], key[0], NT).astype(BF16)
    cumul_t = [c.T for c in cumul]
    total = jnp.zeros((T, 1), F32)
    for p in range(12):
        tail_u = None
        squares = []
        for b in range(2):
            rows = slice(GROUP * b, GROUP * (b + 1))
            x = mixed_ref[rows, chunk(p)].astype(F32)
            u = x * spread(steps[rows], p)
            weights = []
            for h in (2 * p, 2 * p + 1):
                gap = cumul[b][:, h : h + 1] - cumul_t[b][h : h + 1, :]
                weights.append((scores[b] * jnp.exp(jnp.where(lower, gap, -1e30))).astype(BF16))
            u_two = jnp.concatenate([jnp.where(half, u, 0.0), jnp.where(half, 0.0, u)], axis=0)
            y = mm(jnp.concatenate(weights, axis=1), u_two.astype(BF16), NN)
            cum = spread(cumul[b], p)
            if b == 0:
                tail_u = (jnp.exp(cum[GROUP - 1 : GROUP, :] - cum) * u).astype(BF16)
            else:
                y = y + jnp.exp(cum) * mm(cross, tail_u, NN)
            y = y + x * wide_ref[1:2, chunk(p)]
            scan_ref[rows, chunk(p)] = y
            z = proj_ref[rows, chunk(p)]
            gated = y * (z * sigmoid(z))
            squares.append(jnp.sum(gated * gated, axis=-1, keepdims=True))
        total = total + jnp.concatenate(squares, axis=0)
        yield "scan"
    scale_out = lax.rsqrt(total * (1.0 / DI) + EPS)
    for p in range(12):
        z = proj_ref[:, chunk(p)]
        gated = scan_ref[:, chunk(p)] * (z * sigmoid(z))
        nout_ref[:, chunk(p)] = (gated * scale_out * wide_ref[0:1, chunk(p)]).astype(BF16)
    yield "norm"
    for c in range(0, 6, 2):
        cols = slice(LANE * c, LANE * (c + 2))
        branch = mm(nout_ref[...], out_pair(w_ref, c), NN)
        act_ref[:, cols] = (s_ref[:, cols].astype(F32) + branch).astype(BF16)
        yield "branch"


def fold(value, expand):
    high = value.astype(BF16)
    low = (value - high.astype(F32)).astype(BF16)
    return mm(high, expand, NN) + mm(low, expand, NN)


def backward_steps(s_ref, gout_ref, w_ref, head_ref, idx_ref, proj_ref, scan_ref, gain_ref, conv_ref, wide_ref,
             gin_ref, low_ref, d_ref, hgrad_ref,
             mixed_ref, nout_ref, gno_ref, gproj_ref, dmix_ref, dcum_ref, dstep_ref, small_ref, pack_ref, norm_ref, gnorm_ref):
    hgrad_ref[...] = jnp.zeros_like(hgrad_ref)
    skip_sum = jnp.zeros((1, LANE), F32)
    lower = lower_mask()
    half = lane_half()
    grad_branch = gout_ref[...]
    total = jnp.zeros((T, 1), F32)
    for p in range(12):
        z = proj_ref[:, chunk(p)]
        gated = scan_ref[:, chunk(p)] * (z * sigmoid(z))
        total = total + jnp.sum(gated * gated, axis=-1, keepdims=True)
        yield "square", None
    scale_out = lax.rsqrt(total * (1.0 / DI) + EPS)
    for c in range(0, 6, 2):
        part = mm(grad_branch[:, LANE * c : LANE * (c + 2)], out_pair(w_ref, c), NT)
        if c == 0:
            gno_ref[...] = part
        else:
            gno_ref[...] += part
    inner = jnp.zeros((T, 1), F32)
    for p in range(12):
        z = proj_ref[:, chunk(p)]
        gated = scan_ref[:, chunk(p)] * (z * sigmoid(z))
        unit = gated * scale_out
        gain = wide_ref[0:1, chunk(p)]
        nout_ref[:, chunk(p)] = (unit * gain).astype(BF16)
        gno = gno_ref[:, chunk(p)]
        small_ref[ROW_GATED + p : ROW_GATED + p + 1, :] = jnp.sum(gno * unit, axis=0, keepdims=True)
        inner = inner + jnp.sum(gno * gain * unit, axis=-1, keepdims=True)
        yield "inner", None
    inner = inner * (1.0 / DI)
    for c in range(0, 6, 2):
        grad = mm(nout_ref[...], grad_branch[:, LANE * c : LANE * (c + 2)], TN).astype(BF16)
        for e in range(2):
            d_ref[7 + c // 2, e] = grad[:, LANE * e : LANE * (e + 1)].reshape(4, 4, 96, LANE)
        yield "out", 7 + c // 2
    for p in range(12):
        z = proj_ref[:, chunk(p)]
        scan = scan_ref[:, chunk(p)]
        sig = sigmoid(z)
        silu = z * sig
        unit = scan * silu * scale_out
        ggated = scale_out * (gno_ref[:, chunk(p)] * wide_ref[0:1, chunk(p)] - unit * inner)
        gproj_ref[:, chunk(p)] = (ggated * scan * (sig + silu * (1.0 - sig))).astype(BF16)
        gno_ref[:, chunk(p)] = ggated * silu
        yield "gate", None
    stream = s_ref[...].astype(F32)
    scale = lax.rsqrt(jnp.mean(stream * stream, axis=-1, keepdims=True) + EPS)
    norm_ref[...] = (stream * scale * gain_ref[0:1, :]).astype(BF16)

    def in_grad(j):
        gp = gproj_ref[:, 2 * LANE * j : 2 * LANE * (j + 1)]
        grad = mm(norm_ref[...], gp, TN).astype(BF16)
        for e in range(1 if j == 13 else 2):
            part = grad[:, LANE * e : LANE * (e + 1)].reshape(4, 4, 48, LANE)
            d_ref[j // 2, j % 2, :, :, 48 * e : 48 * (e + 1), :] = part
        back = mm(gp, in_pair(w_ref, j), NT)
        if j == 0:
            gnorm_ref[...] = back
        else:
            gnorm_ref[...] += back

    for j in range(6):
        in_grad(j)
        yield "early", j // 2 if j % 2 else None
    def taps(j):
        x, out = conv_of(proj_ref, conv_ref, j)
        sig = sigmoid(out)
        dconv = dmix_ref[:, chunk(j)] * (sig + out * sig * (1.0 - sig))
        small_ref[ROW_BIAS + j : ROW_BIAS + j + 1, :] = jnp.sum(dconv, axis=0, keepdims=True)
        dx = conv_ref[3:4, chunk(j)] * dconv
        for k in range(4):
            row = ROW_TAPS + 14 * (3 - k) + j
            small_ref[row : row + 1, :] = jnp.sum(dconv * down(x, k), axis=0, keepdims=True)
            if k:
                dx = dx + conv_ref[3 - k : 4 - k, chunk(j)] * up(dconv, k)
        gproj_ref[:, DI + LANE * j : DI + LANE * (j + 1)] = dx.astype(BF16)
    for j in range(14):
        _, out = conv_of(proj_ref, conv_ref, j)
        mixed_ref[:, chunk(j)] = (out * sigmoid(out)).astype(BF16)
        yield "conv", None
    raw, steps, rates, cumul = steps_of(proj_ref, head_ref)
    key = [mixed_ref[GROUP * b : GROUP * (b + 1), chunk(12)] for b in range(2)]
    query = [mixed_ref[GROUP * b : GROUP * (b + 1), chunk(13)] for b in range(2)]
    scores = [mm(query[b], key[b], NT) for b in range(2)]
    cross = mm(query[1], key[0], NT).astype(BF16)
    cumul_t = [c.T for c in cumul]
    dscores = [jnp.zeros((GROUP, GROUP), F32) for _ in range(2)]
    dcross = jnp.zeros((GROUP, GROUP), F32)
    dcum_ref[...] = jnp.zeros_like(dcum_ref)
    dstep_ref[...] = jnp.zeros_like(dstep_ref)
    lanes = lax.broadcasted_iota(jnp.int32, (1, LANE), 1)
    head_row = lax.broadcasted_iota(jnp.int32, (LANE, LANE), 0)
    head_col = lax.broadcasted_iota(jnp.int32, (LANE, LANE), 1)
    row_sum = [jnp.zeros((GROUP, LANE), F32) for _ in range(2)]
    for p in range(12):
        expand = (head_col == 2 * p + jnp.where(head_row < 64, 0, 1)).astype(BF16)
        tail_u = eg = None
        us, xs, dus, step_es, grads = [], [], [], [], []
        tail = None
        for b in range(2):
            rows = slice(GROUP * b, GROUP * (b + 1))
            x = mixed_ref[rows, chunk(p)].astype(F32)
            step_e = spread(steps[rows], p)
            u = x * step_e
            g = gno_ref[rows, chunk(p)]
            g_two = jnp.concatenate([jnp.where(half, g, 0.0), jnp.where(half, 0.0, g)], axis=0)
            g_two = g_two.astype(BF16)
            value = mm(g_two, u.astype(BF16), NT)
            weights = []
            for e in range(2):
                h = 2 * p + e
                gap = cumul[b][:, h : h + 1] - cumul_t[b][h : h + 1, :]
                decay = jnp.exp(jnp.where(lower, gap, -1e30))
                weight = scores[b] * decay
                weights.append(weight.astype(BF16))
                v = value[GROUP * e : GROUP * (e + 1)]
                dscores[b] = dscores[b] + v * decay
                both = v * weight
                row_sum[b] = jnp.where(lanes == h, jnp.sum(both, axis=-1, keepdims=True), row_sum[b])
                dcum_ref[b, h : h + 1, :] = -jnp.sum(both, axis=0, keepdims=True)
            du = mm(jnp.concatenate(weights, axis=0), g_two, TN)
            us.append(u)
            xs.append(x)
            dus.append(du)
            step_es.append(step_e)
            grads.append(g)
            cum = spread(cumul[b], p)
            if b == 0:
                tail = jnp.exp(cum[GROUP - 1 : GROUP, :] - cum)
                tail_u = tail * u
            else:
                eg = jnp.exp(cum) * g
        tail_low = tail_u.astype(BF16)
        eg_low = eg.astype(BF16)
        dtail = mm(cross, eg_low, TN)
        dcross = dcross + mm(eg_low, tail_low, NT)
        dus[0] = dus[0] + tail * dtail
        column = fold(tail_u * dtail, expand)
        row_sum[0] = row_sum[0] - column
        row_sum[0] = row_sum[0] + jnp.where(
            lax.broadcasted_iota(jnp.int32, (GROUP, 1), 0) == GROUP - 1,
            jnp.sum(column, axis=0, keepdims=True), 0.0)
        row_sum[1] = row_sum[1] + fold(eg * mm(cross, tail_low, NN), expand)
        skip = jnp.zeros((1, LANE), F32)
        for b in range(2):
            rows = slice(GROUP * b, GROUP * (b + 1))
            dstep_ref[rows, :] += fold(dus[b] * xs[b], expand)
            dmix_ref[rows, chunk(p)] = step_es[b] * dus[b] + grads[b] * wide_ref[1:2, chunk(p)]
            skip = skip + jnp.sum(grads[b] * xs[b], axis=0, keepdims=True)
        skip_sum = skip_sum + fold(jnp.broadcast_to(skip, (8, LANE)), expand)[0:1]
        taps(p)
        if p % 2:
            in_grad(6 + p // 2)
        yield "scan", 3 + p // 4 if p % 4 == 3 else None
    dcross_low = dcross.astype(BF16)
    ds_low = [d.astype(BF16) for d in dscores]
    dmix_ref[0:GROUP, chunk(12)] = mm(ds_low[0], query[0], TN) + mm(dcross_low, query[1], TN)
    dmix_ref[GROUP:T, chunk(12)] = mm(ds_low[1], query[1], TN)
    dmix_ref[0:GROUP, chunk(13)] = mm(ds_low[0], key[0], NN)
    dmix_ref[GROUP:T, chunk(13)] = mm(ds_low[1], key[1], NN) + mm(dcross_low, key[0], NN)
    tri = lower.astype(F32)
    decay_rate = jnp.exp(head_ref[1:2, :])
    step_sum = jnp.zeros((1, LANE), F32)
    decay_sum = jnp.zeros((1, LANE), F32)
    for b in range(2):
        rows = slice(GROUP * b, GROUP * (b + 1))
        drate = mm(tri, row_sum[b] + dcum_ref[b].T, TN, EXACT)
        draw = (dstep_ref[rows, :] - decay_rate * drate) * sigmoid(raw[rows])
        draw = jnp.where(lanes < HEADS, draw, 0.0)
        decay_sum = decay_sum + jnp.sum(drate * rates[rows], axis=0, keepdims=True)
        step_sum = step_sum + jnp.sum(draw, axis=0, keepdims=True)
        gproj_ref[rows, DI + CHANNELS : DI + CHANNELS + LANE] = draw.astype(BF16)
    hgrad_ref[0:1, :] = step_sum
    hgrad_ref[1:2, :] = decay_sum
    hgrad_ref[2:3, :] = skip_sum
    gproj_ref[:, WIDE - LANE :] = jnp.zeros((T, LANE), BF16)
    taps(12)
    taps(13)
    for j in (13, 12):
        in_grad(j)
        yield "late", None
    gnormed = gnorm_ref[...]
    unit = stream * scale
    gain_grad = jnp.sum(gnormed * unit, axis=0, keepdims=True)
    for c in range(6):
        small_ref[ROW_GAIN + c : ROW_GAIN + c + 1, :] = gain_grad[:, chunk(c)]
    pack_all(small_ref, idx_ref, pack_ref)
    d_ref[6, 1, :, :, 48:64, :] = pack_ref[...].astype(BF16).reshape(4, 4, 16, LANE)
    d_ref[6, 1, :, :, 64:96, :] = jnp.zeros((4, 4, 32, LANE), BF16)
    yield "pack", 6
    gunit = gnormed * gain_ref[0:1, :]
    center = jnp.mean(gunit * unit, axis=-1, keepdims=True)
    gin = gout_ref[...].astype(F32) + scale * (gunit - unit * center)
    gin_ref[...] = gin
    low_ref[...] = gin.astype(BF16)
    yield "done", None


KINDS = (
    (2, 12, ROW_GAIN, 6, 32, 1),
    (0, 28, ROW_TAPS, 14, 0, 0),
    (0, 28, ROW_TAPS + 14, 14, 32, 0),
    (0, 28, ROW_TAPS + 28, 14, 64, 0),
    (0, 28, ROW_TAPS + 42, 14, 96, 0),
    (0, 28, ROW_BIAS, 14, 0, 1),
    (4, 24, ROW_GATED, 12, 64, 1),
)


def owner_index():
    table = np.zeros((8, CHANNELS), np.int32)
    for row, width, length in ((0, 28, CHANNELS), (2, 12, D), (4, 24, DI)):
        position = np.arange(length)
        owner = position // width
        table[row, :length] = 16 * (owner // 4) + 2 * (owner % 4)
        table[row + 1, :length] = position % width
    return jnp.asarray(table)


def window(width, c):
    first, last = LANE * c // width, (LANE * c + LANE - 1) // width
    return 16 * (first // 4), 16 * (last // 4) + 16


def unpack(pack, idx_ref, kind, c):
    row, width, _, _, lane, line = kind
    low, high = window(width, c)
    lanes = lax.broadcasted_iota(jnp.int32, (LANE, LANE), 0)
    pick = (lanes == idx_ref[row + 1 : row + 2, chunk(c)] + lane).astype(BF16)
    rows = lax.broadcasted_iota(jnp.int32, (high - low, LANE), 0) + low
    got = mm(pack[low:high], pick, NN)
    return jnp.sum(jnp.where(rows == idx_ref[row : row + 1, chunk(c)] + line, got, 0.0), axis=0, keepdims=True)


def unpack_all(w_ref, idx_ref, head_ref, gain_ref, conv_ref, wide_ref):
    pack = w_ref[6, 1, :, :, 48:64, :].reshape(256, LANE)
    for c in range(6):
        gain_ref[0:1, chunk(c)] = unpack(pack, idx_ref, KINDS[0], c)
    for k in range(5):
        for c in range(14):
            conv_ref[k : k + 1, chunk(c)] = unpack(pack, idx_ref, KINDS[1 + k], c)
    for c in range(12):
        wide_ref[0:1, chunk(c)] = unpack(pack, idx_ref, KINDS[6], c)
        wide_ref[1:2, chunk(c)] = spread(head_ref[2:3, :], c)


def pack_all(small_ref, idx_ref, pack_ref):
    pack_ref[...] = jnp.zeros_like(pack_ref)
    for kind in KINDS:
        row, width, start, count, lane, line = kind
        for c in range(count):
            low, high = window(width, c)
            lanes = lax.broadcasted_iota(jnp.int32, (LANE, LANE), 0)
            pick = (lanes == idx_ref[row + 1 : row + 2, chunk(c)] + lane).astype(BF16)
            rows = lax.broadcasted_iota(jnp.int32, (high - low, LANE), 0) + low
            value = small_ref[start + c : start + c + 1, :]
            held = jnp.where(rows == idx_ref[row : row + 1, chunk(c)] + line, value, 0.0).astype(BF16)
            pack_ref[low:high, :] += mm(held, pick, NT)


def vm(count):
    return [pl.BlockSpec(memory_space=pltpu.VMEM)] * count


class Sems:
    def __init__(self, send, recv):
        self.send, self.recv, self.used = send, recv, 0

    def take(self):
        index = self.used
        self.used += 1
        return self.send.at[index], self.recv.at[index]


class Place:
    def __init__(self):
        self.section = lax.axis_index("section")
        self.dp = lax.axis_index("dp")
        self.z = lax.div(self.dp, 16)
        self.x = lax.rem(lax.div(self.dp, 4), 4)
        self.q = lax.rem(self.dp, 4)
        self.core = lax.rem(self.dp, 2)
        self.column = self.dp - self.q

    def at(self, z, x):
        return (self.section, 16 * z + 4 * x + self.q)

    def along(self, axis, distance):
        if axis == "z":
            return self.at(lax.rem(self.z + distance, 4), self.x)
        return self.at(self.z, lax.rem(self.x + distance, 4))

    def sibling(self):
        return (self.section, self.dp + 1 - 2 * self.core)

    def in_column(self, section, q):
        return (section, self.column + q)


def greet(place):
    barrier = pltpu.get_barrier_semaphore()
    peers = [place.in_column(place.section, lax.rem(place.q + r, 4)) for r in range(1, 4)]
    peers += [place.in_column(1 - place.section, lax.rem(place.q + r, 4)) for r in range(4)]
    peers += [place.along(axis, r) for axis in "zx" for r in range(1, 4)]
    for peer in peers:
        pl.semaphore_signal(barrier, inc=1, device_id=peer, device_id_type=MESH)
    pl.semaphore_wait(barrier, len(peers))


def push(src, dst, sems, device):
    send, recv = sems
    return pltpu.make_async_remote_copy(
        src_ref=src, dst_ref=dst, send_sem=send, recv_sem=recv, device_id=device, device_id_type=MESH
    )


PAIRS = range(10)
AXES = ("xz", "zx", "xz", "zx", "xz", "zx", "xz", "zx", "xz", "zx")
SHARD = (10, 32, LANE)
WHOLE = (10, 2, 4, 4, 96, LANE)


class Copies:
    def __init__(self, place, sems):
        self.place, self.sems, self.sent = place, sems, []

    def start(self, src, dst, device):
        copy = push(src, dst, self.sems.take(), device)
        copy.start()
        self.sent.append(copy)
        return copy

    def end(self):
        for copy in self.sent:
            copy.wait_send()


def coord(place, axis, distance):
    return lax.rem((place.z if axis == "z" else place.x) + distance, 4)


def column_copies(place, layer, sems, source, landing):
    copies = {}
    for other in (0, 1):
        for r in range(4):
            if other == 0 and r == 0:
                continue
            target = lax.rem(place.q + r, 4)
            section = layer if other == 0 else 1 - layer
            copies[other, r] = push(
                source(target), landing, sems.take(), place.in_column(section, target)
            )
    return copies


def gather_steps(layer, place, sems, local, shard_ref, w_ref, slabs, whole, own):
    run = Copies(place, sems)
    core = place.core
    copies = column_copies(place, layer, sems, lambda q: shard_ref.at[lax.rem(q, 2)], slabs.at[place.q])
    mine = pltpu.make_async_copy(shard_ref.at[core], slabs.at[place.q], local.at[0])

    @pl.when(place.section == layer)
    def _():
        for copy in copies.values():
            copy.start()
        mine.start()

    yield "column"

    @pl.when(place.section == layer)
    def _():
        mine.wait()
        for r in range(1, 4):
            copies[0, r].wait_recv()

    @pl.when(place.section != layer)
    def _():
        for r in range(4):
            copies[1, r].wait_recv()

    whole[...] = jnp.zeros_like(whole)
    for q in range(4):
        part = slabs[q].astype(F32)
        whole[0:7, 12 * q : 12 * q + 12, :] = part[0:7, 0:12]
        whole[0:6, 48 + 12 * q : 60 + 12 * q, :] = part[0:6, 16:28]

        @pl.when(core == 0)
        def _():
            whole[6, 48 + 12 * q : 60 + 12 * q, :] = part[6, 16:28]

        @pl.when(core == 1)
        def _():
            whole[6, 48 + 2 * q : 50 + 2 * q, :] = part[6, 16:18]

        whole[7:10, 24 * q : 24 * q + 24, :] = part[7:10, 0:24]
    own[...] = whole[...].astype(BF16)
    keep = pltpu.make_async_copy(own, w_ref.at[:, core, place.z, place.x], local.at[1])
    keep.start()
    first, second, third = {}, {}, {}
    for i in PAIRS:
        there = w_ref.at[i, core, place.z, place.x]
        axis = AXES[i][0]
        first[i] = [run.start(own.at[i], there, place.along(axis, r)) for r in (1, 3, 2)]

    def line(i, distance, rows=None):
        axis = AXES[i][1]
        at = coord(place, axis, distance)
        z, x = (at, pl.ds(0, 4)) if axis == "z" else (pl.ds(0, 4), at)
        if rows is None:
            return w_ref.at[i, core, z, x]
        return w_ref.at[i, core, z, x, pl.ds(rows, 48)]

    for i in PAIRS:
        yield "first"
        if i == 0:
            keep.wait()
        for copy in first[i]:
            copy.wait_recv()
        src = line(i, 0)
        second[i] = [run.start(src, src, place.along(AXES[i][1], r)) for r in (1, 3)]
    for i in PAIRS:
        yield "second"
        second[i][0].wait_recv()
        got = line(i, 3, 0)
        one = run.start(got, got, place.along(AXES[i][1], 1))
        second[i][1].wait_recv()
        got = line(i, 1, 48)
        two = run.start(got, got, place.along(AXES[i][1], 3))
        third[i] = (one, two)
    over = {}
    for i in PAIRS:
        yield "third"
        for copy in third[i]:
            copy.wait_recv()
        half = w_ref.at[i, core]
        over[i] = run.start(half, half, place.sibling())
    for i in PAIRS:
        yield "over"
        over[i].wait_recv()
    yield "whole"
    run.end()

    @pl.when(place.section == layer)
    def _():
        for copy in copies.values():
            copy.wait_send()


GATHER_COPIES = 7 + 8 * 10


def gather_scratch():
    return [
        pltpu.VMEM((4,) + SHARD, BF16),
        pltpu.VMEM((10, 96, LANE), F32),
        pltpu.VMEM((10, 96, LANE), BF16),
        pltpu.SemaphoreType.DMA((2,)),
    ]


def go(steps, count):
    for _ in range(count):
        next(steps, None)


def build_shard(in_ref, out_ref, taps_ref, bias_ref, gain_ref, gated_ref, shard_ref):
    shard_ref[...] = jnp.zeros_like(shard_ref)
    for u in range(27):
        pair, side = u // 2, u % 2
        width = min(LANE, in_ref.shape[2] - LANE * u)
        part = in_ref[0, :, LANE * u : LANE * u + width]
        shard_ref[pair % 2, pair // 2, 16 * side : 16 * side + 12, 0:width] = part
    for c in range(6):
        shard_ref[c % 2, 7 + c // 2, 0:24, :] = out_ref[0, :, chunk(c)]

    def shift(value, start):
        rows = lax.broadcasted_iota(jnp.int32, (value.shape[1], LANE), 0)
        lanes = lax.broadcasted_iota(jnp.int32, (value.shape[1], LANE), 1)
        return mm(value.astype(F32), (lanes == rows + start).astype(F32), NN)

    taps = shift(taps_ref[0, 0:1, :], 0)
    for k in range(1, 4):
        taps = taps + shift(taps_ref[0, k : k + 1, :], 32 * k)
    rest = shift(bias_ref[...], 0) + shift(gain_ref[...], 32) + shift(gated_ref[...], 64)
    small = jnp.concatenate([taps, rest, jnp.zeros((14, LANE), F32)], axis=0)
    shard_ref[1, 6, 16:32, :] = small.astype(BF16)


ORDER = (7, 8, 9, 0, 1, 2, 3, 4, 5, 6)
SOON, LATER = ORDER[:6], ORDER[6:]


def run_plan(work, plan, ready_step):
    seen = {}
    for phase, ready in work:
        if ready is not None:
            ready_step(ready)
        at = seen.get(phase, 0)
        seen[phase] = at + 1
        if phase in plan:
            length, actions = plan[phase]
            for step, i in actions[at * len(actions) // length : (at + 1) * len(actions) // length]:
                step(i)
        run_steps(plan.get((phase, seen.get(phase, 0)), ()))


def steps_for(step, pairs):
    return [(step, i) for i in pairs]


def run_steps(steps):
    for step, i in steps:
        step(i)


class Reduce:
    def __init__(self, layer, place, sems, d_ref, g_ref, bufs):
        self.layer, self.place, self.d, self.g = layer, place, d_ref, g_ref
        self.acc, self.early, self.late, self.last, self.whole, *self.ends = bufs
        self.sems, self.run = sems, Copies(place, sems)
        self.crossing, self.first, self.second, self.third, self.copies = {}, {}, {}, {}, []

    def line(self, i, distance, rows=None):
        axis = AXES[i][1]
        at = coord(self.place, axis, distance)
        z, x = (at, pl.ds(0, 4)) if axis == "z" else (pl.ds(0, 4), at)
        return (i, z, x) if rows is None else (i, z, x, pl.ds(rows, 48))

    def cross(self, i):
        core = self.place.core
        self.crossing[i] = self.run.start(self.d.at[i, 1 - core], self.acc.at[i], self.place.sibling())

    def add(self, i):
        own = self.d[i, self.place.core]
        self.crossing[i].wait_recv()
        self.acc[i] = self.acc[i] + own

    def add_send(self, i):
        self.add(i)
        self.send(i)

    def send(self, i):
        axis = AXES[i][1]
        self.first[i] = (
            self.run.start(self.acc.at[self.line(i, 2, 0)], self.early.at[i, 0], self.place.along(axis, 1)),
            self.run.start(self.acc.at[self.line(i, 2, 48)], self.early.at[i, 1], self.place.along(axis, 3)),
        )

    def near_add(self, i):
        for side, (distance, rows) in enumerate(((1, 0), (3, 48))):
            self.first[i][side].wait_recv()
            at = self.line(i, distance, rows)
            self.acc[at] = self.acc[at] + self.early[i, side]

    def near_send(self, i):
        axis = AXES[i][1]
        self.second[i] = [
            self.run.start(self.acc.at[self.line(i, distance)], self.late.at[i, side],
                           self.place.along(axis, distance))
            for side, distance in enumerate((1, 3))
        ]

    def near(self, i):
        self.near_add(i)
        self.near_send(i)

    def across(self, i):
        for copy in self.second[i]:
            copy.wait_recv()
        at = self.line(i, 0)
        total = self.acc[at].astype(F32) + self.late[i, 0].astype(F32) + self.late[i, 1].astype(F32)
        self.acc[at] = total.astype(BF16)
        axis = AXES[i][0]
        place = self.place
        copies = []
        for r in (1, 3, 2):
            to = coord(place, axis, r)
            z, x = (to, place.x) if axis == "z" else (place.z, to)
            copies.append(self.run.start(self.acc.at[i, z, x], self.last.at[i, r - 1], place.along(axis, r)))
        self.third[i] = copies

    def total(self, i):
        for copy in self.third[i]:
            copy.wait_recv()
        own = self.acc[i, self.place.z, self.place.x].astype(F32)
        for r in range(3):
            own = own + self.last[i, r].astype(F32)
        self.whole[i] = own

    def hand(self, part):
        place, layer, whole = self.place, self.layer, self.whole
        rows, slabs, landed = self.ends
        low, count = ((0, 192), (192, 48))[part]
        if part == 0:
            rows[...] = jnp.zeros_like(rows)
        for q in range(4):
            if part == 0:
                rows[0:5, 0:12, :] = whole[0:5, 12 * q : 12 * q + 12, :]
                rows[0:5, 12:24, :] = whole[0:5, 48 + 12 * q : 60 + 12 * q, :]
                rows[7:10, 0:24, :] = whole[7:10, 24 * q : 24 * q + 24, :]
                value = jnp.concatenate([rows[0:5].reshape(120, LANE), rows[7:10].reshape(72, LANE)], axis=0)
            else:
                rows[5:7, 0:12, :] = whole[5:7, 12 * q : 12 * q + 12, :]
                rows[5, 12:24, :] = whole[5, 48 + 12 * q : 60 + 12 * q, :]

                @pl.when(place.core == 0)
                def _():
                    rows[6, 12:24, :] = whole[6, 48 + 12 * q : 60 + 12 * q, :]

                @pl.when(place.core == 1)
                def _():
                    rows[6, 12:14, :] = whole[6, 48 + 2 * q : 50 + 2 * q, :]

                value = rows[5:7].reshape(48, LANE)
            slabs[q, low : low + count, :] = value.astype(BF16)
        slot = 4 * place.section + place.q
        copies = {}
        for other in (0, 1):
            for r in range(4):
                if other == 0 and r == 0:
                    continue
                target = lax.rem(place.q + r, 4)
                copies[other, r] = push(
                    slabs.at[target, pl.ds(low, count)], landed.at[slot, pl.ds(low, count)],
                    self.sems.take(), place.in_column(layer, target)
                )

        @pl.when(place.section == layer)
        def _():
            for r in range(1, 4):
                copies[0, r].start()
            landed[slot, low : low + count, :] = slabs[place.q, low : low + count, :]

        @pl.when(place.section != layer)
        def _():
            for r in range(4):
                copies[1, r].start()

        self.copies.append(copies)

    def finish(self):
        place, landed = self.place, self.ends[2]

        @pl.when(place.section == self.layer)
        def _():
            for copies in self.copies:
                for copy in copies.values():
                    copy.wait_recv()
            for core in range(2):
                parts = [landed[2 * y + core].astype(F32) for y in range(4)]
                total = parts[0] + parts[1] + parts[2] + parts[3]
                self.g[core, 0:5] = total[0:120].reshape(5, 24, LANE)
                self.g[core, 7:10] = total[120:192].reshape(3, 24, LANE)
                self.g[core, 5:7] = total[192:240].reshape(2, 24, LANE)
            for copies in self.copies:
                for r in range(1, 4):
                    copies[0, r].wait_send()

        @pl.when(place.section != self.layer)
        def _():
            for copies in self.copies:
                for r in range(4):
                    copies[1, r].wait_send()

        self.run.end()


REDUCE_COPIES = 8 * 10 + 14


def reduce_scratch():
    return [
        pltpu.VMEM((10, 4, 4, 96, LANE), BF16),
        pltpu.VMEM((10, 2, 4, 48, LANE), BF16),
        pltpu.VMEM((10, 2, 4, 96, LANE), BF16),
        pltpu.VMEM((10, 3, 96, LANE), BF16),
        pltpu.VMEM((10, 96, LANE), F32),
    ]


def owner_scratch():
    return [
        pltpu.VMEM((10, 24, LANE), F32),
        pltpu.VMEM((4, 240, LANE), BF16),
        pltpu.VMEM((8, 240, LANE), BF16),
    ]


def head_steps(place, sems, hval, head_out_ref, hbuf):
    y = 2 * place.section + lax.div(place.q, 2)
    for index, axis in enumerate(("core", "y", "x", "z")):
        copies = []
        if axis == "core":
            mine, peers = place.core, [place.sibling()]
        elif axis == "y":
            mine, peers = y, []
            for r in range(1, 4):
                to = lax.rem(y + r, 4)
                peers.append((lax.div(to, 2), place.column + 2 * lax.rem(to, 2) + place.core))
        else:
            mine = place.z if axis == "z" else place.x
            peers = [place.along(axis, r) for r in range(1, 4)]
        for peer in peers:
            copy = push(hval, hbuf.at[index, mine], sems.take(), peer)
            copy.start()
            copies.append(copy)
        hbuf[index, mine] = hval[...]
        yield
        for copy in copies:
            copy.wait_recv()
        for copy in copies:
            copy.wait_send()
        total = hbuf[index, 0] + hbuf[index, 1]
        if axis != "core":
            total = total + hbuf[index, 2] + hbuf[index, 3]
        hval[...] = total
    head_out_ref[...] = hval[...]


def entry_kernel(block_ref, in_ref, out_ref, taps_ref, bias_ref, gain_in_ref, gated_ref, step_ref, decay_ref,
                 skip_ref, idx_ref, grad_ref, live_ref,
                 w0_ref, proj0_ref, scan0_ref, acc_ref, heads_ref, act_ref, gain_ref, conv_ref, wide_ref,
                 act1_ref, gin_ref, low_ref, hgrad_ref,
                 s_ref, gout_ref, shard_ref, head_ref, w_here, w_next, proj_a, scan_a, proj_b, scan_b,
                 gain_b, conv_b, wide_b, send, recv, local, *scratch):
    work_refs, scratch = scratch[:11], scratch[11:]
    mixed, nout = work_refs[0:2]
    place = Place()
    stream = pltpu.make_async_copy(block_ref.at[place.section, 0], s_ref, local.at[0])
    stream.start()
    fetch = pltpu.make_async_copy(grad_ref.at[place.section, 0], gout_ref, local.at[1])
    fetch.start()
    build_shard(in_ref, out_ref, taps_ref, bias_ref, gain_in_ref, gated_ref, shard_ref)
    head_ref[...] = jnp.zeros_like(head_ref)
    head_ref[0:1, 0:HEADS] = step_ref[...]
    head_ref[1:2, 0:HEADS] = decay_ref[...]
    head_ref[2:3, 0:HEADS] = skip_ref[...]
    greet(place)
    sems = Sems(send, recv)
    partner = place.in_column(1 - place.section, place.q)
    swap = push(head_ref, heads_ref.at[place.section], sems.take(), partner)
    swap.start()
    heads_ref[place.section] = head_ref[...]
    zero = gather_steps(0, place, sems, scratch[3], shard_ref, w_here, *scratch[0:3])
    one = gather_steps(1, place, sems, scratch[7], shard_ref, w_next, *scratch[4:7])
    go(zero, 1)
    go(one, 1)
    go(zero, 21)
    go(one, 1)
    go(zero, 10)
    go(one, 10)
    go(zero, 7)
    swap.wait()
    stream.wait()
    work = forward_steps(s_ref, w_here, heads_ref.at[0], idx_ref, act_ref, proj_a, scan_a,
                         gain_ref, conv_ref, wide_ref, mixed, nout)
    saved = [pltpu.make_async_copy(w_here, w0_ref, local.at[2]),
             pltpu.make_async_copy(proj_a, proj0_ref, local.at[3]),
             pltpu.make_async_copy(scan_a, scan0_ref, local.at[4])]
    for count, what in enumerate(work):
        if count in (8, 10, 12):
            go(zero, 1)
        if count == 12:
            saved[0].start()
        if what in ("conv", "scan", "branch"):
            go(one, 1)
    saved[1].start()
    saved[2].start()
    for _ in one:
        pass
    go(zero, 1)
    for _ in forward_steps(act_ref, w_next, heads_ref.at[1], idx_ref, act1_ref, proj_b, scan_b,
                           gain_b, conv_b, wide_b, mixed, nout):
        pass
    live = jnp.where(place.section == 0, live_ref[:, 0:1], live_ref[:, 1:2]).astype(F32)
    fetch.wait()
    gout_ref[...] = (gout_ref[...].astype(F32) * live).astype(BF16)
    saved[0].wait()
    back = Reduce(1, place, sems, w_here, None, scratch[8:13])
    work = backward_steps(act_ref, gout_ref, w_next, heads_ref.at[1], idx_ref, proj_b, scan_b, gain_b, conv_b,
                          wide_b, gin_ref, low_ref, w_here, hgrad_ref, *work_refs)
    run_plan(
        work,
        {
            "conv": (14, steps_for(back.add_send, SOON)),
            ("scan", 8): steps_for(back.add, (3,)),
            ("scan", 12): steps_for(back.add, (4,)),
        },
        back.cross,
    )
    run_steps(steps_for(back.add, (5, 6)) + steps_for(back.near_add, SOON))
    kept = pltpu.make_async_copy(back.acc, acc_ref, local.at[5])
    kept.start()
    back.run.end()
    saved[1].wait()
    saved[2].wait()
    kept.wait()


def run_entry(*given):
    copies = 1 + 2 * GATHER_COPIES + REDUCE_COPIES
    any_space = pl.BlockSpec(memory_space=pl.ANY)
    return pl.pallas_call(
        entry_kernel,
        out_shape=(
            jax.ShapeDtypeStruct(WHOLE, BF16),
            jax.ShapeDtypeStruct((T, WIDE), F32),
            jax.ShapeDtypeStruct((T, DI), F32),
            jax.ShapeDtypeStruct((10, 4, 4, 96, LANE), BF16),
            jax.ShapeDtypeStruct((2, 8, LANE), F32),
            jax.ShapeDtypeStruct((T, D), BF16),
            jax.ShapeDtypeStruct((8, D), F32),
            jax.ShapeDtypeStruct((8, CHANNELS), F32),
            jax.ShapeDtypeStruct((8, DI), F32),
            jax.ShapeDtypeStruct((T, D), BF16),
            jax.ShapeDtypeStruct((T, D), F32),
            jax.ShapeDtypeStruct((T, D), BF16),
            jax.ShapeDtypeStruct((8, LANE), F32),
        ),
        in_specs=[any_space] + vm(10) + [any_space] + vm(1),
        out_specs=tuple([any_space] * 4 + vm(9)),
        scratch_shapes=[
            pltpu.VMEM((T, D), BF16),
            pltpu.VMEM((T, D), BF16),
            pltpu.VMEM((2,) + SHARD, BF16),
            pltpu.VMEM((8, LANE), F32),
            pltpu.VMEM(WHOLE, BF16),
            pltpu.VMEM(WHOLE, BF16),
            pltpu.VMEM((T, WIDE), F32),
            pltpu.VMEM((T, DI), F32),
            pltpu.VMEM((T, WIDE), F32),
            pltpu.VMEM((T, DI), F32),
            pltpu.VMEM((8, D), F32),
            pltpu.VMEM((8, CHANNELS), F32),
            pltpu.VMEM((8, DI), F32),
            pltpu.SemaphoreType.DMA((copies,)),
            pltpu.SemaphoreType.DMA((copies,)),
            pltpu.SemaphoreType.DMA((6,)),
        ]
        + backward_scratch()
        + gather_scratch()
        + gather_scratch()
        + reduce_scratch(),
        compiler_params=pltpu.CompilerParams(
            collective_id=0, has_side_effects=True, vmem_limit_bytes=60 * 1024 * 1024
        ),
        name="gather_forward_and_second_backward",
    )(*given)


def exit_kernel(block_ref, low1_ref, w0_ref, heads_ref, idx_ref, proj0_ref, scan0_ref, gain_ref, conv_ref, wide_ref,
                acc1_ref, hgrad1_ref, act0_ref, act1_ref, gin1_ref,
                acts_ref, grads_ref, g_ref, head_out_ref,
                s_ref, w_ref, proj_ref, scan_ref, d_ref, gin_ref, low_ref, hgrad_ref, hval, hbuf, back_in,
                send, recv, local, *scratch):
    work_refs, scratch = scratch[:11], scratch[11:]
    place = Place()
    head_ref = heads_ref.at[0]
    one = Reduce(1, place, Sems(send, recv), None, g_ref, scratch[0:8])
    sems = one.sems
    zero = Reduce(0, place, sems, d_ref, g_ref, scratch[8:16])
    loads = [
        pltpu.make_async_copy(acc1_ref, one.acc, local.at[0]),
        pltpu.make_async_copy(scan0_ref, scan_ref, local.at[1]),
        pltpu.make_async_copy(proj0_ref, proj_ref, local.at[2]),
        pltpu.make_async_copy(block_ref.at[place.section, 0], s_ref, local.at[3]),
        pltpu.make_async_copy(w0_ref, w_ref, local.at[4]),
    ]
    for load in loads:
        load.start()
    greet(place)
    first = place.section == 0
    partner = place.in_column(1 - place.section, place.q)
    loads[0].wait()
    run_steps(steps_for(one.near_send, SOON) + steps_for(one.send, LATER))
    act_out = [push(ref, acts_ref.at[place.section], pair, partner)
               for pair in (sems.take(),) for ref in (act1_ref, act0_ref)]
    back_out = [push(ref, back_in, pair, partner) for pair in (sems.take(),) for ref in (low1_ref, low_ref)]

    @pl.when(first)
    def _():
        act_out[0].start()
        back_out[0].start()
        acts_ref[0] = act0_ref[...]

    @pl.when(place.section == 1)
    def _():
        act_out[1].start()
        acts_ref[1] = act1_ref[...]
        grads_ref[1] = gin1_ref[...]

    for load in loads[1:]:
        load.wait()
    work = backward_steps(s_ref, low1_ref, w_ref, head_ref, idx_ref, proj_ref, scan_ref, gain_ref, conv_ref,
                          wide_ref, gin_ref, low_ref, d_ref, hgrad_ref, *work_refs)
    run_plan(
        work,
        {
            "conv": (14, steps_for(zero.add_send, SOON)),
            ("scan", 4): steps_for(one.near, LATER),
            ("scan", 6): steps_for(one.across, SOON[:3]),
            ("scan", 7): steps_for(one.across, SOON[3:]),
            ("scan", 8): steps_for(zero.add_send, (3,)),
            ("scan", 12): steps_for(zero.add_send, (4,)),
            ("late", 1): steps_for(zero.near, SOON[:3]),
            ("late", 2): steps_for(zero.near, SOON[3:]) + steps_for(zero.add_send, (5,)),
        },
        zero.cross,
    )
    hval[...] = jnp.zeros_like(hval)
    hval[0:4, :] = hgrad_ref[0:4, :]
    hval[4:8, :] = hgrad1_ref[0:4, :]
    small = head_steps(place, sems, hval, head_out_ref, hbuf)
    go(small, 1)

    @pl.when(place.section == 1)
    def _():
        back_out[1].start()

    @pl.when(first)
    def _():
        grads_ref[0] = gin_ref[...]

    zero.add_send(6)
    run_steps(steps_for(one.across, LATER) + steps_for(one.total, SOON) + steps_for(zero.near, LATER))
    go(small, 1)
    run_steps(steps_for(one.total, LATER) + steps_for(one.hand, (0, 1)))
    run_steps(steps_for(zero.across, SOON))
    go(small, 1)
    run_steps(steps_for(zero.across, LATER))
    one.finish()
    go(small, 1)
    run_steps(steps_for(zero.total, SOON) + steps_for(zero.total, (3, 4)))
    zero.hand(0)
    run_steps(steps_for(zero.total, (5, 6)))
    zero.hand(1)
    go(small, 1)
    act_out[0].wait()
    back_out[0].wait()

    @pl.when(first)
    def _():
        grads_ref[1] = back_in[...].astype(F32)

    @pl.when(place.section == 1)
    def _():
        grads_ref[0] = back_in[...].astype(F32)

    zero.finish()


def run_exit(*given):
    copies = 2 * REDUCE_COPIES + 10 + 2
    any_space = pl.BlockSpec(memory_space=pl.ANY)
    spaces = [any_space] + vm(1) + [any_space] + vm(2) + [any_space] * 2 + vm(3) + [any_space] + vm(4)
    return pl.pallas_call(
        exit_kernel,
        out_shape=(
            jax.ShapeDtypeStruct((2, T, D), BF16),
            jax.ShapeDtypeStruct((2, T, D), F32),
            jax.ShapeDtypeStruct((2, 10, 24, LANE), F32),
            jax.ShapeDtypeStruct((8, LANE), F32),
        ),
        in_specs=spaces,
        out_specs=tuple(vm(4)),
        scratch_shapes=[
            pltpu.VMEM((T, D), BF16),
            pltpu.VMEM(WHOLE, BF16),
            pltpu.VMEM((T, WIDE), F32),
            pltpu.VMEM((T, DI), F32),
            pltpu.VMEM(WHOLE, BF16),
            pltpu.VMEM((T, D), F32),
            pltpu.VMEM((T, D), BF16),
            pltpu.VMEM((8, LANE), F32),
            pltpu.VMEM((8, LANE), F32),
            pltpu.VMEM((4, 4, 8, LANE), F32),
            pltpu.VMEM((T, D), BF16),
            pltpu.SemaphoreType.DMA((copies,)),
            pltpu.SemaphoreType.DMA((copies,)),
            pltpu.SemaphoreType.DMA((5,)),
        ]
        + backward_scratch()
        + reduce_scratch()
        + owner_scratch()
        + reduce_scratch()
        + owner_scratch(),
        compiler_params=pltpu.CompilerParams(
            collective_id=1, has_side_effects=True, vmem_limit_bytes=63 * 1024 * 1024
        ),
        name="first_backward_and_reduce",
    )(*given)


def backward_scratch():
    return [
        pltpu.VMEM((T, CHANNELS), BF16),
        pltpu.VMEM((T, DI), BF16),
        pltpu.VMEM((T, DI), F32),
        pltpu.VMEM((T, WIDE), BF16),
        pltpu.VMEM((T, CHANNELS), F32),
        pltpu.VMEM((2, LANE, GROUP), F32),
        pltpu.VMEM((T, LANE), F32),
        pltpu.VMEM((SMALL, LANE), F32),
        pltpu.VMEM((256, LANE), F32),
        pltpu.VMEM((T, D), BF16),
        pltpu.VMEM((T, D), F32),
    ]


def finish_kernel(acts_ref, grads_ref, g_ref, heads_ref, act_out, grad_out, gain_out, in_out, taps_out, bias_out,
                  step_out, decay_out, skip_out, gated_out, out_out, local):
    loads = [
        pltpu.make_async_copy(acts_ref, act_out.at[0, :, 0], local.at[0]),
        pltpu.make_async_copy(grads_ref, grad_out.at[0, :, 0], local.at[1]),
    ]
    for load in loads:
        load.start()
    for u in range(27):
        pair, side = u // 2, u % 2
        width = min(LANE, in_out.shape[2] - LANE * u)
        part = g_ref[pair % 2, pair // 2, 12 * side : 12 * side + 12, 0:width]
        in_out[0, :, LANE * u : LANE * u + width] = part
    for c in range(6):
        out_out[0, :, chunk(c)] = g_ref[c % 2, 7 + c // 2, 0:24, :]
    small = g_ref[1, 6, 8:16, :]
    bias_out[...] = small[5:6, 0:28]
    for k in range(4):
        turned = small if k == 0 else pltpu.roll(small, LANE - 32 * k, 1)
        taps_out[0, k : k + 1, :] = turned[4:5, 0:28]
        if k == 1:
            gain_out[...] = turned[5:6, 0:12]
        if k == 2:
            gated_out[...] = turned[5:6, 0:24]
    heads = jnp.where(lax.axis_index("section") == 0, heads_ref[0:4, :], heads_ref[4:8, :])
    step_out[...] = heads[0:1, 0:HEADS]
    decay_out[...] = heads[1:2, 0:HEADS]
    skip_out[...] = heads[2:3, 0:HEADS]
    for load in loads:
        load.wait()


def run_finish(acts, grads, g, heads):
    shapes = (
        ((1, 2, 1, T, D), BF16),
        ((1, 2, 1, T, D), F32),
        ((1, 12), F32),
        ((1, 12, 3352), F32),
        ((1, 4, 28), F32),
        ((1, 28), F32),
        ((1, HEADS), F32),
        ((1, HEADS), F32),
        ((1, HEADS), F32),
        ((1, 24), F32),
        ((1, 24, D), F32),
    )
    return pl.pallas_call(
        finish_kernel,
        out_shape=tuple(jax.ShapeDtypeStruct(shape, kind) for shape, kind in shapes),
        in_specs=[pl.BlockSpec(memory_space=pl.ANY)] * 2 + vm(2),
        out_specs=tuple(vm(11)),
        scratch_shapes=[pltpu.SemaphoreType.DMA((2,))],
        compiler_params=pltpu.CompilerParams(vmem_limit_bytes=62 * 1024 * 1024),
        name="outputs",
    )(acts, grads, g, heads)


def body(
    block_input,
    out_grad,
    live_mask,
    norm_gain,
    in_weight,
    conv_weight,
    conv_bias,
    dt_bias,
    a_log,
    d_skip,
    gated_gain,
    out_weight,
):
    idx = owner_index()
    weight, proj, scan, acc, heads, act0, gain, conv, wide, act1, grad1, low1, head_grad1 = run_entry(
        block_input, in_weight, out_weight, conv_weight, conv_bias, norm_gain, gated_gain, dt_bias, a_log, d_skip,
        idx, out_grad, live_mask.T,
    )
    totals = run_exit(
        block_input, low1, weight, heads, idx, proj, scan, gain, conv, wide, acc, head_grad1, act0, act1, grad1
    )
    return run_finish(*totals)


def solution(mesh):
    placed = (
        P(None, "dp", None, None),
        P(None, "dp", None, None),
        P(None, "dp"),
        P("section", "dp"),
        P("section", "dp", None),
        P("section", None, "dp"),
        P("section", "dp"),
        P("section", None),
        P("section", None),
        P("section", None),
        P("section", "dp"),
        P("section", "dp", None),
    )
    return jax.shard_map(
        body,
        mesh=mesh,
        in_specs=placed,
        out_specs=(
            P("section", None, "dp", None, None),
            P("section", None, "dp", None, None),
            P("section", "dp"),
            P("section", "dp", None),
            P("section", None, "dp"),
            P("section", "dp"),
            P("section", None),
            P("section", None),
            P("section", None),
            P("section", "dp"),
            P("section", "dp", None),
        ),
        check_vma=False,
    )
```
